32 devices in a mesh: rep: 16 (over z, y, core), shard: 2 (over x).
Axes of the slice: x: 2, y: 2, z: 4, core: 2. Of those that a mesh axis runs over, the one named last changes fastest.
Arguments:
- tokens: bfloat16 [65536, 768], P(('rep', 'shard')), may hold values from -6 to 6
- cotangent: bfloat16 [65536, 768], P(('rep', 'shard')), may hold values from -6 to 6
- seq_lengths: int32 [64], replicated, may hold values from 256 to 1792, as said below
- seq_device: int32 [64], replicated, may hold values from 0 to 31, as said below
- norm_gain: bfloat16 [768], P('shard'), may hold values from 0.5 to 1.5
- in_weight: bfloat16 [768, 3352], P('shard'), may hold values from -0.21875 to 0.21875
- conv_weight: bfloat16 [4, 1792], P(None, 'shard'), may hold values from -3 to 3
- conv_bias: bfloat16 [1792], P('shard'), may hold values from -3 to 3
- step_bias: bfloat16 [24], P('shard'), may hold values from -6 to -2
- decay_log: bfloat16 [24], P('shard'), may hold values from 0 to 2.765625
- skip_gain: bfloat16 [24], P('shard'), may hold values from 0.5 to 1.5
- gate_gain: bfloat16 [1536], P('shard'), may hold values from 0.5 to 1.5
- out_weight: bfloat16 [1536, 768], P('shard'), may hold values from -0.15625 to 0.15625
Outputs:
- block_out: bfloat16 [65536, 768], P(('rep', 'shard'))
- grad_tokens: bfloat16 [65536, 768], P(('rep', 'shard'))
- grad_norm_gain: float32 [768], P('shard')
- grad_in_weight: float32 [768, 3352], P('shard')
- grad_conv_weight: float32 [4, 1792], P(None, 'shard')
- grad_conv_bias: float32 [1792], P('shard')
- grad_step_bias: float32 [24], P('shard')
- grad_decay_log: float32 [24], P('shard')
- grad_skip_gain: float32 [24], P('shard')
- grad_gate_gain: float32 [1536], P('shard')
- grad_out_weight: float32 [1536, 768], P('shard')
The draws below stay inside these ranges and needn't reach their ends.
Inputs may be any that keep to these rules, and one draw needn't show every extreme that they name: `seq_lengths`: sequences j and j + 32 lie on one device, in that order from its slot 0; their two lengths add up to at most 2048, and in every draw some device is filled. `seq_device`: each device index appears exactly once among the first 32 entries, and entry j + 32 equals entry j.
All inputs are finite; a program needn't handle non-finite values.
Results may differ from the reference program's by a relative error of at most 0.011.
Values may be sent and summed in bfloat16 or wider, within the bound.
No kernel may reach another device: no remote copies, remote signals or barrier semaphores. Data moves between devices by JAX's collectives and lax.ppermute only.
A program may use at most 384 MiB of HBM per device.

```python
import jax
import jax.numpy as jnp
from jax import lax

D = 768
HEADS = 24
CONV_K = 4
SPAN = 256
MINLEN = 256
TOK_DEV = 2048
E = 1536
CONV_CH = 1792
IN_W = 3352
NSEQ = 64
TOKENS = 65536
N_REP = 16
N_SHARD = 2


def draw_seq_lengths(key, part):
    pairs = NSEQ // 2
    key_first, key_second, key_full = jax.random.split(key, 3)
    first_len = jax.random.randint(key_first, (pairs,), MINLEN, TOK_DEV - MINLEN + 1)
    spread = jax.random.randint(key_second, (pairs,), 0, 1 << 20)
    second_len = MINLEN + spread % (TOK_DEV - first_len - MINLEN + 1)
    chosen = jax.random.randint(key_full, (), 0, pairs)
    slot_index = jnp.arange(pairs)
    first_len = jnp.where(slot_index == chosen, TOK_DEV - MINLEN, first_len)
    second_len = jnp.where(slot_index == chosen, MINLEN, second_len)
    return jnp.concatenate([first_len, second_len]).astype(jnp.int32)


def draw_seq_device(key, part):
    order = jax.random.permutation(key, NSEQ // 2)
    return jnp.concatenate([order, order]).astype(jnp.int32)


def steps_of(own_key, extent, shards, low, high):
    gain = 1.0
    for dim, blocks in shards:
        steps = jax.random.uniform(jax.random.fold_in(jax.random.fold_in(own_key, 6), dim), (blocks,), jnp.float32, low / len(shards), high / len(shards))
        gain = gain * jnp.repeat(jnp.exp(steps), extent[dim] // blocks).reshape((-1,) + (1,) * (len(extent) - 1 - dim))
    return gain


def centred(key, extent, width, bound, cuts=(), held_as=jnp.bfloat16):
    array = width * jax.random.normal(key, extent, jnp.float32)
    if cuts:
        array = array * steps_of(key, extent, cuts, -0.22, 0.18)
    return jnp.clip(array, -bound, bound).astype(held_as)


def setup_inputs(seed: int = 0) -> dict:
    splits = jax.random.split(jax.random.key(seed), 14)
    return {
        "tokens": centred(splits[0], (TOKENS, D), 1.0, 6.0, ((0, 32),)),
        "cotangent": centred(splits[1], (TOKENS, D), 1.0, 6.0, ((0, 32),)),
        "seq_lengths": draw_seq_lengths(jax.random.fold_in(splits[13], 71), 0),
        "seq_device": draw_seq_device(jax.random.fold_in(splits[13], 71), 0),
        "norm_gain": jnp.clip(1.0 + 0.1 * jax.random.normal(splits[4], (D,), jnp.float32), 0.5, 1.5).astype(jnp.bfloat16),
        "in_weight": centred(splits[5], (D, IN_W), D ** -0.5, 0.21875, ((0, 2),)),
        "conv_weight": centred(splits[6], (CONV_K, CONV_CH), CONV_K ** -0.5, 3.0, ((1, 2),)),
        "conv_bias": centred(splits[7], (CONV_CH,), 0.5, 3.0, ((0, 2),)),
        "step_bias": jnp.clip(-6.0 + 4.0 * jax.random.uniform(splits[8], (HEADS,), jnp.float32) ** steps_of(splits[8], (HEADS,), ((0, 2),), -0.2, 0.2), -6.0, -2.0).astype(jnp.bfloat16),
        "decay_log": jnp.clip(2.765625 * jax.random.uniform(splits[9], (HEADS,), jnp.float32) ** steps_of(splits[9], (HEADS,), ((0, 2),), -0.2, 0.2), 0.0, 2.765625).astype(jnp.bfloat16),
        "skip_gain": jnp.clip(0.5 + 1.0 * jax.random.uniform(splits[10], (HEADS,), jnp.float32) ** steps_of(splits[10], (HEADS,), ((0, 2),), -0.2, 0.2), 0.5, 1.5).astype(jnp.bfloat16),
        "gate_gain": jnp.clip(1.0 + 0.1 * jax.random.normal(splits[11], (E,), jnp.float32), 0.5, 1.5).astype(jnp.bfloat16),
        "out_weight": centred(splits[12], (E, D), E ** -0.5, 0.15625, ((0, 2),)),
    }


highest = lax.Precision.HIGHEST

@jax.custom_vjp
def low(v):
    return lax.optimization_barrier(v.astype(jnp.bfloat16)).astype(jnp.float32)

@jax.custom_vjp
def low_back(v):
    return v

def low_keep(v):
    return (low(v), None)

def low_pass(kept, grad):
    return (grad,)

def back_keep(v):
    return (v, None)

def back_low(kept, grad):
    return (low(grad),)
low.defvjp(low_keep, low_pass)
low_back.defvjp(back_keep, back_low)

def pre_norm(rows_in, gain_vec):
    return rows_in * lax.rsqrt(lax.optimization_barrier(jnp.mean(rows_in * rows_in, axis=-1, keepdims=True)) + 1e-05) * gain_vec[None, :]

def conv_mix(channels, conv_taps, conv_shift, segment):
    tap_count = conv_taps.shape[0]
    running = conv_shift[None, :] + conv_taps[tap_count - 1][None, :] * channels
    for offset in range(1, tap_count):
        earlier = jnp.concatenate([jnp.zeros((offset, channels.shape[1]), channels.dtype), channels[:-offset]], axis=0)
        earlier_seg = jnp.concatenate([jnp.full((offset,), -1, jnp.int32), segment[:-offset]], axis=0)
        same_doc = (earlier_seg == segment).astype(channels.dtype)
        running = running + conv_taps[tap_count - 1 - offset][None, :] * earlier * same_doc[:, None]
    return jax.nn.silu(running)

def block_scan(inputs, write_vec, read_vec, step_size, log_rate, segment):
    rows_all, head_count, head_size = inputs.shape
    state_dim = write_vec.shape[1]
    blocks = rows_all // SPAN
    position = lax.iota(jnp.int32, SPAN)

    def advance(carry, item):
        hidden_state, last_seg = carry
        block_in, block_write, block_read, block_step, block_rate, block_seg = item
        cum_rate = jnp.cumsum(block_rate, axis=0)
        rate_heads = cum_rate.T
        allowed = (block_seg[:, None] == block_seg[None, :]) & (position[:, None] >= position[None, :])
        rate_gap = rate_heads[:, :, None] - rate_heads[:, None, :]
        decay_mat = jnp.where(allowed[None], jnp.exp(jnp.where(allowed[None], rate_gap, 0.0)), 0.0)
        gram_mat = jnp.dot(block_read, block_write.T, precision=highest)
        mixing = gram_mat[None] * decay_mat * block_step.T[:, None, :]
        inner = jnp.einsum('hij,jhp->ihp', mixing, block_in, precision=highest)
        entry = (block_seg == last_seg).astype(block_in.dtype)
        carried = jnp.einsum('in,hpn->ihp', block_read, hidden_state, precision=highest)
        carried = carried * (entry[:, None] * jnp.exp(cum_rate))[:, :, None]
        end_seg = block_seg[SPAN - 1]
        tail_weight = (block_seg == end_seg).astype(block_in.dtype)[:, None] * jnp.exp(cum_rate[SPAN - 1][None, :] - cum_rate) * block_step
        fresh = jnp.einsum('jh,jhp,jn->hpn', tail_weight, block_in, block_write, precision=highest)
        keep_rate = (end_seg == last_seg).astype(block_in.dtype) * jnp.exp(cum_rate[SPAN - 1])
        new_state = keep_rate[:, None, None] * hidden_state + fresh
        return ((new_state, end_seg), inner + carried)
    items = (inputs.reshape(blocks, SPAN, head_count, head_size), write_vec.reshape(blocks, SPAN, state_dim), read_vec.reshape(blocks, SPAN, state_dim), step_size.reshape(blocks, SPAN, head_count), log_rate.reshape(blocks, SPAN, head_count), segment.reshape(blocks, SPAN))
    start = (jnp.zeros((head_count, head_size, state_dim), inputs.dtype), jnp.int32(-1))
    final_carry, outputs = lax.scan(jax.checkpoint(advance), start, items)
    return outputs.reshape(rows_all, head_count, head_size)

def mixer(projected, conv_taps, conv_shift, step_shift, decay_rate, skip_rate, gate_rate, segment):
    inner_dim = gate_rate.shape[0]
    head_count = step_shift.shape[0]
    state_dim = (projected.shape[1] - 2 * inner_dim - head_count) // 2
    row_count = projected.shape[0]
    gate_part = projected[:, :inner_dim]
    conv_in = projected[:, inner_dim:2 * inner_dim + 2 * state_dim]
    step_raw = projected[:, 2 * inner_dim + 2 * state_dim:]
    mixed = conv_mix(conv_in, conv_taps, conv_shift, segment)
    inputs = mixed[:, :inner_dim].reshape(row_count, head_count, inner_dim // head_count)
    write_vec = mixed[:, inner_dim:inner_dim + state_dim]
    read_vec = mixed[:, inner_dim + state_dim:]
    step_size = jax.nn.softplus(step_raw + step_shift[None, :])
    log_rate = -jnp.exp(decay_rate)[None, :] * step_size
    scanned = block_scan(inputs, write_vec, read_vec, step_size, log_rate, segment) + skip_rate[None, :, None] * inputs
    scanned = scanned.reshape(row_count, inner_dim)
    product = scanned * jax.nn.silu(gate_part)
    return product * lax.rsqrt(lax.optimization_barrier(jnp.mean(product * product, axis=-1, keepdims=True)) + 1e-05) * gate_rate[None, :]

def layout(seq_lengths, seq_device, device_count, slot_count):
    half_count = seq_lengths.shape[0] // 2
    match = seq_device[None, :half_count] == lax.iota(jnp.int32, device_count)[:, None]
    first_len = lax.optimization_barrier(jnp.sum(jnp.where(match, seq_lengths[None, :half_count], 0), axis=1)).astype(jnp.int32)
    second_len = lax.optimization_barrier(jnp.sum(jnp.where(match, seq_lengths[None, half_count:], 0), axis=1)).astype(jnp.int32)
    position = lax.iota(jnp.int32, slot_count)[None, :]
    ending = (first_len + second_len)[:, None]
    segment = (position >= first_len[:, None]).astype(jnp.int32) + (position >= ending).astype(jnp.int32)
    live_mask = (position < ending).astype(jnp.float32)
    return (segment, live_mask)

def reference(tokens, cotangent, seq_lengths, seq_device, norm_gain, in_weight, conv_weight, conv_bias, step_bias, decay_log, skip_gain, gate_gain, out_weight):
    device_count = N_REP * N_SHARD
    segment, live_mask = layout(seq_lengths, seq_device, device_count, TOK_DEV)
    params = (norm_gain.astype(jnp.float32), in_weight.astype(jnp.float32), conv_weight.astype(jnp.float32), conv_bias.astype(jnp.float32), step_bias.astype(jnp.float32), decay_log.astype(jnp.float32), skip_gain.astype(jnp.float32), gate_gain.astype(jnp.float32), out_weight.astype(jnp.float32))
    rows_in = tokens.astype(jnp.float32).reshape(device_count, TOK_DEV, D)

    def forward(weights, rows_all):
        gain_pre, weight_in, conv_taps, conv_shift, step_shift, decay_rate, skip_rate, gate_rate, weight_out = weights

        def slab_fn(slab_item):
            slab_rows, slab_seg, slab_live = slab_item
            normed = low(pre_norm(slab_rows, gain_pre))
            projected = low_back(jnp.dot(normed, weight_in, precision=highest, preferred_element_type=jnp.float32))
            gated = low(mixer(projected, conv_taps, conv_shift, step_shift, decay_rate, skip_rate, gate_rate, slab_seg))
            output = jnp.dot(gated, weight_out, precision=highest, preferred_element_type=jnp.float32)
            return slab_rows + slab_live[:, None] * output
        return lax.map(jax.checkpoint(slab_fn), (rows_all, segment, live_mask.astype(rows_all.dtype)))
    block_out, back_fn = jax.vjp(forward, params, rows_in)
    grads, grad_rows = back_fn(cotangent.astype(jnp.float32).reshape(device_count, TOK_DEV, D))
    return (block_out.reshape(TOKENS, D).astype(jnp.bfloat16), grad_rows.reshape(TOKENS, D).astype(jnp.bfloat16), grads[0], grads[1], grads[2], grads[3], grads[4], grads[5], grads[6], grads[7], grads[8])
```

```python
import functools

import jax
import jax.numpy as jnp
from jax import lax
from jax.experimental import pallas as pl
from jax.experimental.pallas import tpu as pltpu
from jax.sharding import PartitionSpec as P

ROWS = 256
CHUNK = 128
LANES = 128
LOG2E = 1.4426950408889634
F32 = jnp.float32
BF16 = jnp.bfloat16
HIGH = lax.Precision.HIGHEST
VMEM_LIMIT = 60 * 1024 * 1024


def dot(a, b, dims=((1,), (0,)), precision=None):
    return lax.dot_general(a, b, (dims, ((), ())), precision=precision, preferred_element_type=F32)


def fold8(v):
    return jnp.sum(v.reshape(v.shape[0] // 8, 8, v.shape[1]), axis=0)


def segment_of(position, first_end, second_end):
    return (position >= first_end).astype(jnp.int32) + (position >= second_end).astype(jnp.int32)


def softplus(v):
    return jnp.maximum(v, 0.0) + jnp.log1p(jnp.exp(-jnp.abs(v)))


def head_sums(v, heads):
    high = v.astype(BF16)
    low = (v - high.astype(F32)).astype(BF16)
    return dot(high, heads) + dot(low, heads)


def lane_pair(v, p, lane_low):
    shape = lane_low.shape
    a = jnp.broadcast_to(v[:, 2 * p : 2 * p + 1], shape)
    b = jnp.broadcast_to(v[:, 2 * p + 1 : 2 * p + 2], shape)
    return a, b


def split_rows(pair, lane_low):
    zero = jnp.zeros_like(pair)
    return jnp.concatenate(
        [jnp.where(lane_low, pair, zero), jnp.where(lane_low, zero, pair)], axis=0
    )


def chunk_setup(raw, step_bias, neg_rate, start, first_end, second_end):
    row = lax.broadcasted_iota(jnp.int32, (CHUNK, LANES), 0)
    col = lax.broadcasted_iota(jnp.int32, (CHUNK, LANES), 1)
    step = softplus(raw + step_bias)
    rate = neg_rate * step
    lower = (row >= col).astype(F32)
    cum = dot(lower, rate, precision=HIGH) * LOG2E
    seg_row = segment_of(row + start, first_end, second_end)
    seg_col = segment_of(col + start, first_end, second_end)
    last_seg = segment_of(start - 1, first_end, second_end)
    end_seg = segment_of(start + CHUNK - 1, first_end, second_end)
    entry = (seg_row == last_seg).astype(F32)
    tail = (seg_row == end_seg).astype(F32)
    keep = (last_seg == end_seg).astype(F32)
    same = seg_row == seg_col
    return row, col, step, rate, cum, same, entry, tail, keep


def forward_kernel(
    ends,
    tok,
    cot,
    w_in,
    w_out,
    norm_gain,
    conv_w,
    conv_b,
    step_bias,
    neg_rate,
    skip,
    gate_gain,
    heads,
    block_out,
    normed_out,
    gated_out,
    u_out,
    conv_in_out,
    raw_out,
    dy_out,
    dgate_out,
    s1_out,
    state_out,
    gain_grad,
    skip_grad,
    gate_s,
    ext,
    xs,
    bc,
    ys,
    prod_s,
    dg_s,
    wx_s,
    keep_s,
    state,
):
    step_id = pl.program_id(0)
    first_end = ends[0]
    second_end = ends[1]
    inner = gate_s.shape[1]
    channels = ext.shape[1]
    pairs = inner // LANES
    base = step_id * ROWS

    @pl.when(step_id == 0)
    def _():
        ext[0:8, :] = jnp.zeros((8, channels), F32)
        state[...] = jnp.zeros_like(state)
        gain_grad[...] = jnp.zeros_like(gain_grad)
        skip_grad[...] = jnp.zeros_like(skip_grad)

    rows = tok[...].astype(F32)
    scale = lax.rsqrt(jnp.mean(rows * rows, axis=-1, keepdims=True) + 1e-05)
    normed = (rows * scale * norm_gain[...]).astype(BF16)
    normed_out[...] = normed
    gate_s[...] = dot(normed, w_in[:, :inner])
    conv_in = dot(normed, w_in[:, inner : inner + channels])
    ext[8 : 8 + ROWS, :] = conv_in
    conv_in_out[...] = conv_in.astype(BF16)
    raw_out[...] = dot(normed, w_in[:, inner + channels :])

    pos = lax.broadcasted_iota(jnp.int32, (ROWS, LANES), 0) + base
    seg = segment_of(pos, first_end, second_end)
    shift_mask = [
        ((segment_of(pos - k, first_end, second_end) == seg) & (pos >= k)).astype(F32)
        for k in range(1, 4)
    ]

    def conv_tile(ct):
        cols = slice(ct * LANES, (ct + 1) * LANES)
        total = conv_b[:, cols] + conv_w[3:4, cols] * ext[8 : 8 + ROWS, cols]
        for k in range(1, 4):
            total += (conv_w[3 - k : 4 - k, cols] * ext[8 - k : 8 - k + ROWS, cols]) * shift_mask[k - 1]
        u = total.astype(BF16)
        u_out[:, cols] = u
        half = 0.5 * u.astype(F32)
        return half + half * jnp.tanh(half)

    for ct in range(pairs):
        xs[:, ct * LANES : (ct + 1) * LANES] = conv_tile(ct)
    for ct in range(pairs, channels // LANES):
        bc[:, (ct - pairs) * LANES : (ct - pairs + 1) * LANES] = conv_tile(ct)
    ext[0:8, :] = ext[ROWS : ROWS + 8, :]

    def chunk(q, carry):
        r0 = pl.multiple_of(q * CHUNK, CHUNK)
        rsl = pl.ds(r0, CHUNK)
        row, col, step, rate, cum, same, entry, tail, keep = chunk_setup(
            raw_out[rsl, :], step_bias[...], neg_rate[...], base + r0, first_end, second_end
        )
        cum_t = cum.T
        lane_low = col < (LANES // 2)
        b_f = bc[rsl, 0:LANES]
        b_low = b_f.astype(BF16)
        c_low = bc[rsl, LANES : 2 * LANES].astype(BF16)
        gram = dot(c_low, b_low, ((1,), (1,)))
        gram = jnp.where(same & (row >= col), gram, 0.0)
        state_low = state[...].astype(BF16)
        state_out[q] = state_low
        ys[rsl, :] = dot(c_low, state_low)
        for p in range(pairs):
            cols = slice(p * LANES, (p + 1) * LANES)
            ca, cb = lane_pair(cum, p, lane_low)
            sa, sb = lane_pair(step, p, lane_low)
            ma = (jnp.exp2(jnp.minimum(ca - cum_t[2 * p : 2 * p + 1, :], 0.0)) * gram).astype(BF16)
            mb = (jnp.exp2(jnp.minimum(cb - cum_t[2 * p + 1 : 2 * p + 2, :], 0.0)) * gram).astype(BF16)
            both = jnp.where(lane_low, ca, cb)
            xdt = xs[rsl, cols] * jnp.where(lane_low, sa, sb)
            xdt_low = xdt.astype(BF16)
            inner_y = dot(jnp.concatenate([ma, mb], axis=1), split_rows(xdt_low, lane_low))
            ys[rsl, cols] = inner_y + ys[rsl, cols] * (jnp.exp2(both) * entry)
            end = both[CHUNK - 1 : CHUNK, :]
            wx_s[:, cols] = (xdt * (jnp.exp2(end - both) * tail)).astype(BF16)
            keep_s[0:1, cols] = jnp.exp2(end) * keep
        state[...] = state[...] * keep_s[0:1, :] + dot(b_f.T.astype(BF16), wx_s[...])
        return carry

    lax.fori_loop(0, ROWS // CHUNK, chunk, 0)

    live = (pos < second_end).astype(F32)
    dg_s[...] = dot(
        (cot[...].astype(F32) * live[:, 0:1]).astype(BF16), w_out[...], ((1,), (1,))
    )
    sq = jnp.zeros((ROWS, LANES), F32)
    cross = jnp.zeros((ROWS, LANES), F32)
    for ct in range(pairs):
        cols = slice(ct * LANES, (ct + 1) * LANES)
        half = 0.5 * gate_s[:, cols]
        product = (ys[:, cols] + skip[:, cols] * xs[:, cols]) * (half + half * jnp.tanh(half))
        prod_s[:, cols] = product
        sq += product * product
        cross += dg_s[:, cols] * gate_gain[:, cols] * product
    r = lax.rsqrt(jnp.sum(sq, axis=1, keepdims=True) / inner + 1e-05)
    m = jnp.sum(cross, axis=1, keepdims=True) / inner
    r_wide = jnp.broadcast_to(r, (ROWS, LANES))
    m_wide = jnp.broadcast_to(r * r * r * m, (ROWS, LANES))
    for ct in range(pairs):
        cols = slice(ct * LANES, (ct + 1) * LANES)
        g = gate_s[:, cols]
        sig = 0.5 + 0.5 * jnp.tanh(0.5 * g)
        act = g * sig
        x = xs[:, cols]
        y = ys[:, cols]
        product = prod_s[:, cols]
        pr = product * r_wide
        gated_out[:, cols] = (pr * gate_gain[:, cols]).astype(BF16)
        dg = dg_s[:, cols]
        gain_grad[:, cols] += fold8(dg * pr)
        dprod = r_wide * (dg * gate_gain[:, cols]) - product * m_wide
        dsc = dprod * act
        dgate_out[:, cols] = (
            dprod * (y + skip[:, cols] * x) * (sig + act * (1.0 - sig))
        ).astype(BF16)
        dy = dsc.astype(BF16)
        dy_out[:, cols] = dy
        skip_grad[:, cols] += fold8(dsc * x)
        ys[:, cols] = dy.astype(F32) * y
    s1_out[...] = head_sums(ys[...], heads[...])
    out = dot(gated_out[...], w_out[...])
    block_out[...] = (rows + live[:, 0:1] * out).astype(BF16)


def backward_kernel(
    ends,
    u_in,
    conv_in,
    raw_in,
    dy_in,
    s1_in,
    state_in,
    conv_w,
    step_bias,
    neg_rate,
    skip,
    heads,
    dconv_out,
    draw_out,
    conv_w_grad,
    conv_b_grad,
    step_grad,
    decay_grad,
    ext,
    xs,
    bc,
    slope,
    bds,
    q_s,
    dye_s,
    wx_s,
    rows_s,
    dstate,
):
    step_id = pl.program_id(0)
    first_end = ends[0]
    second_end = ends[1]
    inner = xs.shape[1]
    channels = ext.shape[1]
    pairs = inner // LANES
    base = (pl.num_programs(0) - 1 - step_id) * ROWS

    @pl.when(step_id == 0)
    def _():
        ext[ROWS : ROWS + 8, :] = jnp.zeros((8, channels), F32)
        dstate[...] = jnp.zeros_like(dstate)
        rows_s[...] = jnp.zeros_like(rows_s)
        conv_w_grad[...] = jnp.zeros_like(conv_w_grad)
        conv_b_grad[...] = jnp.zeros_like(conv_b_grad)
        step_grad[...] = jnp.zeros_like(step_grad)
        decay_grad[...] = jnp.zeros_like(decay_grad)

    for ct in range(channels // LANES):
        cols = slice(ct * LANES, (ct + 1) * LANES)
        u = u_in[:, cols].astype(F32)
        sig = 0.5 + 0.5 * jnp.tanh(0.5 * u)
        act = u * sig
        slope[:, cols] = sig + act * (1.0 - sig)
        if ct < pairs:
            xs[:, cols] = act
        else:
            bc[:, (ct - pairs) * LANES : (ct - pairs + 1) * LANES] = act

    def chunk(k, carry):
        q = ROWS // CHUNK - 1 - k
        r0 = pl.multiple_of(q * CHUNK, CHUNK)
        rsl = pl.ds(r0, CHUNK)
        raw = raw_in[rsl, :]
        row, col, step, rate, cum, same, entry, tail, keep = chunk_setup(
            raw, step_bias[...], neg_rate[...], base + r0, first_end, second_end
        )
        cum_t = cum.T
        lane_low = col < (LANES // 2)
        b_low = bc[rsl, 0:LANES].astype(BF16)
        c_f = bc[rsl, LANES : 2 * LANES]
        c_low = c_f.astype(BF16)
        allowed = same & (row <= col)
        gram = jnp.where(allowed, dot(b_low, c_low, ((1,), (1,))), 0.0)
        dstate_low = dstate[...].astype(BF16)
        bds[...] = dot(b_low, dstate_low)
        dgram = jnp.zeros((CHUNK, CHUNK), F32)
        for p in range(pairs):
            cols = slice(p * LANES, (p + 1) * LANES)
            ca, cb = lane_pair(cum, p, lane_low)
            sa, sb = lane_pair(step, p, lane_low)
            la = jnp.exp2(jnp.minimum(cum_t[2 * p : 2 * p + 1, :] - ca, 0.0))
            lb = jnp.exp2(jnp.minimum(cum_t[2 * p + 1 : 2 * p + 2, :] - cb, 0.0))
            both = jnp.where(lane_low, ca, cb)
            step_pair = jnp.where(lane_low, sa, sb)
            dy_low = dy_in[rsl, cols]
            dy = dy_low.astype(F32)
            dy2 = split_rows(dy_low, lane_low)
            xdt = xs[rsl, cols] * step_pair
            xdt_low = xdt.astype(BF16)
            mt = jnp.concatenate([(la * gram).astype(BF16), (lb * gram).astype(BF16)], axis=1)
            dmt = dot(xdt_low, dy2, ((1,), (1,)))
            dgram += dmt[:, :CHUNK] * la + dmt[:, CHUNK:] * lb
            end = both[CHUNK - 1 : CHUNK, :]
            weight = jnp.exp2(end - both) * tail
            gxs = weight * bds[:, cols]
            gx = dot(mt, dy2) + gxs
            xdt_r = xdt_low.astype(F32)
            q_s[:, cols] = xdt_r * gx
            ext[rsl, cols] = (step_pair * gx + skip[:, cols] * dy) * slope[rsl, cols]
            wx_s[:, cols] = (xdt * weight).astype(BF16)
            dye_s[:, cols] = (dy * (jnp.exp2(both) * entry)).astype(BF16)
            keep_row = jnp.exp2(end) * keep
            rows_s[8:9, cols] = keep_row
            rows_s[0:8, cols] = fold8(xdt_r * gxs) + keep_row * fold8(
                dstate[:, cols] * state_in[q, :, cols].astype(F32)
            )
        dgram = jnp.where(allowed, dgram, 0.0)
        dc = dot(dgram.T.astype(BF16), b_low) + dot(dye_s[...], state_in[q], ((1,), (1,)))
        db = dot(dgram.astype(BF16), c_low) + dot(wx_s[...], dstate_low, ((1,), (1,)))
        bsl = slice(inner, inner + LANES)
        csl = slice(inner + LANES, inner + 2 * LANES)
        ext[rsl, bsl] = db * slope[rsl, bsl]
        ext[rsl, csl] = dc * slope[rsl, csl]
        dstate[...] = dstate[...] * rows_s[8:9, :] + dot(c_f.T.astype(BF16), dye_s[...])
        sx = head_sums(q_s[...], heads[...])
        end_term = jnp.sum(head_sums(rows_s[0:8, :], heads[...]), axis=0, keepdims=True)
        upper = (row <= col).astype(F32)
        drate = dot(upper, s1_in[rsl, :] - sx, precision=HIGH) + end_term
        dstep = sx / jnp.maximum(step, 1e-37) + neg_rate[...] * drate
        draw = dstep * jax.nn.sigmoid(raw + step_bias[...])
        draw_out[rsl, :] = draw.astype(BF16)
        step_grad[...] += fold8(draw)
        decay_grad[...] += fold8(drate * rate)
        return carry

    lax.fori_loop(0, ROWS // CHUNK, chunk, 0)

    pos = lax.broadcasted_iota(jnp.int32, (ROWS, LANES), 0) + base
    seg = segment_of(pos, first_end, second_end)
    shift_mask = [
        (segment_of(pos + k, first_end, second_end) == seg).astype(F32) for k in range(1, 4)
    ]
    for ct in range(channels // LANES):
        cols = slice(ct * LANES, (ct + 1) * LANES)
        du = ext[0:ROWS, cols]
        source = conv_in[:, cols].astype(F32)
        conv_b_grad[:, cols] += fold8(du)
        conv_w_grad[24:32, cols] += fold8(source * du)
        total = conv_w[3:4, cols] * du
        for k in range(1, 4):
            later = ext[k : k + ROWS, cols] * shift_mask[k - 1]
            total += conv_w[3 - k : 4 - k, cols] * later
            conv_w_grad[8 * (3 - k) : 8 * (4 - k), cols] += fold8(source * later)
        dconv_out[:, cols] = total.astype(BF16)
    ext[ROWS : ROWS + 8, :] = ext[0:8, :]


def whole(shape):
    return pl.BlockSpec(shape, lambda i: (0,) * len(shape))


def run_forward(ends, tok, cot, w_in, w_out, norm_gain, conv_w, conv_b, step_bias, neg_rate, skip, gate_gain, heads):
    count, width = tok.shape
    inner = w_out.shape[0]
    channels = conv_w.shape[1]
    grid = count // ROWS
    per = ROWS // CHUNK

    def rows_of(n):
        return pl.BlockSpec((ROWS, n), lambda i: (i, 0))

    return pl.pallas_call(
        forward_kernel,
        grid=(grid,),
        in_specs=[
            pl.BlockSpec(memory_space=pltpu.SMEM),
            rows_of(width),
            rows_of(width),
            whole(w_in.shape),
            whole(w_out.shape),
            whole(norm_gain.shape),
            whole(conv_w.shape),
            whole(conv_b.shape),
            whole(step_bias.shape),
            whole(neg_rate.shape),
            whole(skip.shape),
            whole(gate_gain.shape),
            whole(heads.shape),
        ],
        out_specs=[
            rows_of(width),
            rows_of(width),
            rows_of(inner),
            rows_of(channels),
            rows_of(channels),
            rows_of(LANES),
            rows_of(inner),
            rows_of(inner),
            rows_of(LANES),
            pl.BlockSpec((per, LANES, inner), lambda i: (i, 0, 0)),
            whole((8, inner)),
            whole((8, inner)),
        ],
        out_shape=[
            jax.ShapeDtypeStruct((count, width), BF16),
            jax.ShapeDtypeStruct((count, width), BF16),
            jax.ShapeDtypeStruct((count, inner), BF16),
            jax.ShapeDtypeStruct((count, channels), BF16),
            jax.ShapeDtypeStruct((count, channels), BF16),
            jax.ShapeDtypeStruct((count, LANES), F32),
            jax.ShapeDtypeStruct((count, inner), BF16),
            jax.ShapeDtypeStruct((count, inner), BF16),
            jax.ShapeDtypeStruct((count, LANES), F32),
            jax.ShapeDtypeStruct((count // CHUNK, LANES, inner), BF16),
            jax.ShapeDtypeStruct((8, inner), F32),
            jax.ShapeDtypeStruct((8, inner), F32),
        ],
        scratch_shapes=[
            pltpu.VMEM((ROWS, inner), F32),
            pltpu.VMEM((ROWS + 8, channels), F32),
            pltpu.VMEM((ROWS, inner), F32),
            pltpu.VMEM((ROWS, 2 * LANES), F32),
            pltpu.VMEM((ROWS, inner), F32),
            pltpu.VMEM((ROWS, inner), F32),
            pltpu.VMEM((ROWS, inner), F32),
            pltpu.VMEM((CHUNK, inner), BF16),
            pltpu.VMEM((8, inner), F32),
            pltpu.VMEM((LANES, inner), F32),
        ],
        compiler_params=pltpu.CompilerParams(
            dimension_semantics=("arbitrary",), vmem_limit_bytes=VMEM_LIMIT
        ),
        cost_estimate=pl.CostEstimate(
            flops=30_000_000_000, bytes_accessed=70_000_000, transcendentals=20_000_000
        ),
        name="mixer_forward",
    )(ends, tok, cot, w_in, w_out, norm_gain, conv_w, conv_b, step_bias, neg_rate, skip, gate_gain, heads)


def run_backward(ends, u, conv_in, raw, dy, s1, states, conv_w, step_bias, neg_rate, skip, heads):
    count, channels = u.shape
    inner = dy.shape[1]
    grid = count // ROWS
    per = ROWS // CHUNK
    last = grid - 1

    def rows_of(n):
        return pl.BlockSpec((ROWS, n), lambda i: (last - i, 0))

    return pl.pallas_call(
        backward_kernel,
        grid=(grid,),
        in_specs=[
            pl.BlockSpec(memory_space=pltpu.SMEM),
            rows_of(channels),
            rows_of(channels),
            rows_of(LANES),
            rows_of(inner),
            rows_of(LANES),
            pl.BlockSpec((per, LANES, inner), lambda i: (last - i, 0, 0)),
            whole(conv_w.shape),
            whole(step_bias.shape),
            whole(neg_rate.shape),
            whole(skip.shape),
            whole(heads.shape),
        ],
        out_specs=[
            rows_of(channels),
            rows_of(LANES),
            whole((32, channels)),
            whole((8, channels)),
            whole((8, LANES)),
            whole((8, LANES)),
        ],
        out_shape=[
            jax.ShapeDtypeStruct((count, channels), BF16),
            jax.ShapeDtypeStruct((count, LANES), BF16),
            jax.ShapeDtypeStruct((32, channels), F32),
            jax.ShapeDtypeStruct((8, channels), F32),
            jax.ShapeDtypeStruct((8, LANES), F32),
            jax.ShapeDtypeStruct((8, LANES), F32),
        ],
        scratch_shapes=[
            pltpu.VMEM((ROWS + 8, channels), F32),
            pltpu.VMEM((ROWS, inner), F32),
            pltpu.VMEM((ROWS, 2 * LANES), F32),
            pltpu.VMEM((ROWS, channels), F32),
            pltpu.VMEM((CHUNK, inner), F32),
            pltpu.VMEM((CHUNK, inner), F32),
            pltpu.VMEM((CHUNK, inner), BF16),
            pltpu.VMEM((CHUNK, inner), BF16),
            pltpu.VMEM((16, inner), F32),
            pltpu.VMEM((LANES, inner), F32),
        ],
        compiler_params=pltpu.CompilerParams(
            dimension_semantics=("arbitrary",), vmem_limit_bytes=VMEM_LIMIT
        ),
        cost_estimate=pl.CostEstimate(
            flops=30_000_000_000, bytes_accessed=50_000_000, transcendentals=20_000_000
        ),
        name="mixer_backward",
    )(ends, u, conv_in, raw, dy, s1, states, conv_w, step_bias, neg_rate, skip, heads)


def pad_lanes(v):
    return jnp.pad(v, ((0, 0), (0, LANES - v.shape[1])))


def local_terms(tokens, cotangent, first_len, second_len, norm_gain, w_in, conv_w, conv_b, step_bias, decay_log, skip_gain, gate_gain, w_out):
    count, width = tokens.shape
    inner = w_out.shape[0]
    channels = conv_w.shape[1]
    head_count = step_bias.shape[0]
    size = inner // head_count
    ends = jnp.stack([first_len, first_len + second_len]).astype(jnp.int32)
    lane_head = lax.broadcasted_iota(jnp.int32, (inner, LANES), 0) // size
    heads = (lane_head == lax.broadcasted_iota(jnp.int32, (inner, LANES), 1)).astype(BF16)
    w_in_pad = jnp.pad(w_in, ((0, 0), (0, LANES - head_count)))
    skip = jnp.repeat(skip_gain.astype(F32), size)[None, :]
    step_row = pad_lanes(step_bias.astype(F32)[None, :])
    neg_rate = pad_lanes(-jnp.exp(decay_log.astype(F32))[None, :])
    conv_wf = conv_w.astype(F32)
    conv_bf = conv_b.astype(F32)[None, :]
    norm_row = norm_gain.astype(F32)[None, :]
    gate_row = gate_gain.astype(F32)[None, :]
    (block_out, normed, gated, u, conv_in, raw, dy, dgate, s1, states, gain8, skip8) = run_forward(
        ends, tokens, cotangent, w_in_pad, w_out, norm_row, conv_wf, conv_bf, step_row, neg_rate, skip, gate_row, heads
    )
    live = (lax.iota(jnp.int32, count) < ends[1]).astype(BF16)
    g_out = dot(gated, cotangent * live[:, None], ((0,), (0,)))
    g_in_gate = dot(normed, dgate, ((0,), (0,)))
    dconv, draw, cw8, cb8, sb8, dl8 = run_backward(
        ends, u, conv_in, raw, dy, s1, states, conv_wf, step_row, neg_rate, skip, heads
    )
    rest = jnp.concatenate([dconv, draw[:, :head_count]], axis=1)
    g_in_rest = dot(normed, rest, ((0,), (0,)))
    grad_normed = (
        dot(dgate, w_in[:, :inner], ((1,), (1,)))
        + dot(rest, w_in[:, inner:], ((1,), (1,)))
    )
    rows = tokens.astype(F32)
    r = lax.rsqrt(jnp.mean(rows * rows, axis=-1, keepdims=True) + 1e-05)
    n = rows * r
    g_norm = jnp.sum(grad_normed * n, axis=0)
    weighted = norm_row * grad_normed
    grad_tokens = (
        r * (weighted - n * jnp.mean(weighted * n, axis=-1, keepdims=True)) + cotangent.astype(F32)
    ).astype(BF16)
    g_conv = jnp.sum(cw8.reshape(4, 8, channels), axis=1)
    g_bias = jnp.sum(cb8, axis=0)
    g_step = jnp.sum(sb8, axis=0)[:head_count]
    g_decay = jnp.sum(dl8, axis=0)[:head_count]
    g_skip = jnp.sum(skip8.reshape(8, head_count, size), axis=(0, 2))
    g_gain = jnp.sum(gain8, axis=0)
    return block_out, grad_tokens, g_out, g_in_gate, g_in_rest, (g_norm, g_conv, g_bias, g_step, g_decay, g_skip, g_gain)


def per_device(
    tokens,
    cotangent,
    seq_lengths,
    seq_device,
    norm_gain,
    in_weight,
    conv_weight,
    conv_bias,
    step_bias,
    decay_log,
    skip_gain,
    gate_gain,
    out_weight,
):
    shards = lax.axis_size("shard")
    device = lax.axis_index("rep") * shards + lax.axis_index("shard")
    half_count = seq_lengths.shape[0] // 2
    owned = seq_device[:half_count] == device
    first_len = jnp.sum(jnp.where(owned, seq_lengths[:half_count], 0))
    second_len = jnp.sum(jnp.where(owned, seq_lengths[half_count:], 0))

    small = (norm_gain, conv_weight.reshape(-1), conv_bias, step_bias, decay_log, skip_gain, gate_gain)
    sizes = [v.shape[0] for v in small]
    packed = lax.all_gather(jnp.concatenate(small), "shard", axis=0, tiled=False)
    parts = []
    at = 0
    for n in sizes:
        parts.append(packed[:, at : at + n])
        at += n
    taps = conv_weight.shape[0]
    full_conv = parts[1].reshape(shards, taps, -1).transpose(1, 0, 2).reshape(taps, -1)
    flat = [p.reshape(-1) for p in parts]
    full_in = lax.all_gather(in_weight, "shard", axis=0, tiled=True)
    full_out = lax.all_gather(out_weight, "shard", axis=0, tiled=True)

    block_out, grad_tokens, g_out, g_in_gate, g_in_rest, smalls = local_terms(
        tokens, cotangent, first_len, second_len, flat[0], full_in, full_conv, flat[2], flat[3], flat[4], flat[5], flat[6], full_out
    )

    def total(v):
        low = lax.psum_scatter(v.astype(BF16), "shard", scatter_dimension=0, tiled=True)
        return lax.psum(low, "rep").astype(F32)

    t_out = total(g_out)
    t_in = jnp.concatenate([total(g_in_gate), total(g_in_rest)], axis=1)
    g_norm, g_conv, g_bias, g_step, g_decay, g_skip, g_gain = smalls
    pieces = (
        g_norm.reshape(shards, -1),
        g_conv.reshape(taps, shards, -1).transpose(1, 0, 2).reshape(shards, -1),
        g_bias.reshape(shards, -1),
        g_step.reshape(shards, -1),
        g_decay.reshape(shards, -1),
        g_skip.reshape(shards, -1),
        g_gain.reshape(shards, -1),
    )
    summed = lax.psum(jnp.concatenate(pieces, axis=1), ("rep", "shard"))
    mine = lax.dynamic_index_in_dim(summed, lax.axis_index("shard"), 0, keepdims=False)
    outs = []
    at = 0
    for n in sizes:
        outs.append(mine[at : at + n])
        at += n
    return (
        block_out,
        grad_tokens,
        outs[0],
        t_in,
        outs[1].reshape(taps, -1),
        outs[2],
        outs[3],
        outs[4],
        outs[5],
        outs[6],
        t_out,
    )


def solution(mesh):
    in_specs = (
        P(("rep", "shard"), None),
        P(("rep", "shard"), None),
        P(),
        P(),
        P("shard"),
        P("shard", None),
        P(None, "shard"),
        P("shard"),
        P("shard"),
        P("shard"),
        P("shard"),
        P("shard"),
        P("shard", None),
    )
    out_specs = (
        P(("rep", "shard"), None),
        P(("rep", "shard"), None),
        P("shard"),
        P("shard", None),
        P(None, "shard"),
        P("shard"),
        P("shard"),
        P("shard"),
        P("shard"),
        P("shard"),
        P("shard", None),
    )
    return jax.shard_map(
        per_device, mesh=mesh, in_specs=in_specs, out_specs=out_specs, check_vma=False
    )
```

```python
import functools

import jax
import jax.numpy as jnp
from jax import lax
from jax.experimental import pallas as pl
from jax.experimental.pallas import tpu as pltpu
from jax.sharding import PartitionSpec as P

ROWS = 256
CHUNK = 128
TAIL = 512
LANES = 128
LOG2E = 1.4426950408889634
F32 = jnp.float32
BF16 = jnp.bfloat16
HIGH = lax.Precision.HIGHEST
VMEM_LIMIT = 60 * 1024 * 1024


def dot(a, b, dims=((1,), (0,)), precision=None):
    return lax.dot_general(a, b, (dims, ((), ())), precision=precision, preferred_element_type=F32)


def fold8(v):
    return jnp.sum(v.reshape(v.shape[0] // 8, 8, v.shape[1]), axis=0)


def segment_of(position, first_end, second_end):
    return (position >= first_end).astype(jnp.int32) + (position >= second_end).astype(jnp.int32)


def softplus(v):
    return jnp.maximum(v, 0.0) + jnp.log1p(jnp.exp(-jnp.abs(v)))


def head_sums(v, heads):
    high = v.astype(BF16)
    low = (v - high.astype(F32)).astype(BF16)
    return dot(high, heads) + dot(low, heads)


def lane_pair(v, p, lane_low):
    shape = lane_low.shape
    a = jnp.broadcast_to(v[:, 2 * p : 2 * p + 1], shape)
    b = jnp.broadcast_to(v[:, 2 * p + 1 : 2 * p + 2], shape)
    return a, b


def split_rows(pair, lane_low):
    zero = jnp.zeros_like(pair)
    return jnp.concatenate(
        [jnp.where(lane_low, pair, zero), jnp.where(lane_low, zero, pair)], axis=0
    )


def chunk_setup(raw, step_bias, neg_rate, start, first_end, second_end):
    row = lax.broadcasted_iota(jnp.int32, (CHUNK, LANES), 0)
    col = lax.broadcasted_iota(jnp.int32, (CHUNK, LANES), 1)
    step = softplus(raw + step_bias)
    rate = neg_rate * step
    lower = (row >= col).astype(F32)
    cum = dot(lower, rate, precision=HIGH) * LOG2E
    seg_row = segment_of(row + start, first_end, second_end)
    seg_col = segment_of(col + start, first_end, second_end)
    last_seg = segment_of(start - 1, first_end, second_end)
    end_seg = segment_of(start + CHUNK - 1, first_end, second_end)
    entry = (seg_row == last_seg).astype(F32)
    tail = (seg_row == end_seg).astype(F32)
    keep = (last_seg == end_seg).astype(F32)
    same = seg_row == seg_col
    return row, col, step, rate, cum, same, entry, tail, keep


def place_rows(dst, width, local, far, near, core, shard):
    half = far.shape[0]
    own_at = pl.multiple_of(shard * (2 * half), half)
    other_at = (1 - shard) * (2 * half)
    dst[pl.ds(own_at, 2 * half), :width] = local
    dst[pl.ds(pl.multiple_of(other_at + core * half, half), half), :width] = far[...]
    dst[pl.ds(pl.multiple_of(other_at + (1 - core) * half, half), half), :width] = near[...]


def scan_kernel(
    ends,
    tok,
    w_local,
    w_far,
    w_near,
    norm_gain,
    conv_w,
    conv_b,
    step_bias,
    neg_rate,
    normed_out,
    u_out,
    conv_in_out,
    raw_out,
    y_out,
    state_out,
    w_conv,
    ext,
    xs,
    bc,
    wx_s,
    keep_s,
    state,
):
    step_id = pl.program_id(0)
    first_end = ends[0]
    second_end = ends[1]
    inner = xs.shape[1]
    channels = ext.shape[1]
    pairs = inner // LANES
    base = step_id * ROWS

    @pl.when(step_id == 0)
    def _():
        w_conv[:, channels:] = jnp.zeros((w_conv.shape[0], LANES), BF16)
        used = w_far.shape[1]
        place_rows(w_conv, used, w_local[:, inner:], w_far, w_near, ends[2], ends[3])
        ext[0:8, :] = jnp.zeros((8, channels), F32)
        state[...] = jnp.zeros_like(state)

    rows = tok[...].astype(F32)
    scale = lax.rsqrt(jnp.mean(rows * rows, axis=-1, keepdims=True) + 1e-05)
    normed = (rows * scale * norm_gain[...]).astype(BF16)
    normed_out[...] = normed
    conv_in = dot(normed, w_conv[:, :channels])
    ext[8 : 8 + ROWS, :] = conv_in
    conv_in_out[...] = conv_in.astype(BF16)
    raw_out[...] = dot(normed, w_conv[:, channels:])

    pos = lax.broadcasted_iota(jnp.int32, (ROWS, LANES), 0) + base
    seg = segment_of(pos, first_end, second_end)
    shift_mask = [
        ((segment_of(pos - k, first_end, second_end) == seg) & (pos >= k)).astype(F32)
        for k in range(1, 4)
    ]

    def conv_tile(ct):
        cols = slice(ct * LANES, (ct + 1) * LANES)
        total = conv_b[:, cols] + conv_w[3:4, cols] * ext[8 : 8 + ROWS, cols]
        for k in range(1, 4):
            total += (conv_w[3 - k : 4 - k, cols] * ext[8 - k : 8 - k + ROWS, cols]) * shift_mask[k - 1]
        u = total.astype(BF16)
        u_out[:, cols] = u
        half = 0.5 * u.astype(F32)
        return half + half * jnp.tanh(half)

    for ct in range(pairs):
        xs[:, ct * LANES : (ct + 1) * LANES] = conv_tile(ct)
    for ct in range(pairs, channels // LANES):
        bc[:, (ct - pairs) * LANES : (ct - pairs + 1) * LANES] = conv_tile(ct)
    ext[0:8, :] = ext[ROWS : ROWS + 8, :]

    def chunk(q, carry):
        r0 = pl.multiple_of(q * CHUNK, CHUNK)
        rsl = pl.ds(r0, CHUNK)
        row, col, step, rate, cum, same, entry, tail, keep = chunk_setup(
            raw_out[rsl, :], step_bias[...], neg_rate[...], base + r0, first_end, second_end
        )
        cum_t = cum.T
        lane_low = col < (LANES // 2)
        b_f = bc[rsl, 0:LANES]
        b_low = b_f.astype(BF16)
        c_low = bc[rsl, LANES : 2 * LANES].astype(BF16)
        gram = dot(c_low, b_low, ((1,), (1,)))
        gram = jnp.where(same & (row >= col), gram, 0.0)
        state_low = state[...].astype(BF16)
        state_out[q] = state_low
        y_out[rsl, :] = dot(c_low, state_low)
        for p in range(pairs):
            cols = slice(p * LANES, (p + 1) * LANES)
            ca, cb = lane_pair(cum, p, lane_low)
            sa, sb = lane_pair(step, p, lane_low)
            ma = (jnp.exp2(jnp.minimum(ca - cum_t[2 * p : 2 * p + 1, :], 0.0)) * gram).astype(BF16)
            mb = (jnp.exp2(jnp.minimum(cb - cum_t[2 * p + 1 : 2 * p + 2, :], 0.0)) * gram).astype(BF16)
            both = jnp.where(lane_low, ca, cb)
            xdt = xs[rsl, cols] * jnp.where(lane_low, sa, sb)
            xdt_low = xdt.astype(BF16)
            inner_y = dot(jnp.concatenate([ma, mb], axis=1), split_rows(xdt_low, lane_low))
            y_out[rsl, cols] = inner_y + y_out[rsl, cols] * (jnp.exp2(both) * entry)
            end = both[CHUNK - 1 : CHUNK, :]
            wx_s[:, cols] = (xdt * (jnp.exp2(end - both) * tail)).astype(BF16)
            keep_s[0:1, cols] = jnp.exp2(end) * keep
        state[...] = state[...] * keep_s[0:1, :] + dot(b_f.T.astype(BF16), wx_s[...])
        return carry

    lax.fori_loop(0, ROWS // CHUNK, chunk, 0)


def gate_kernel(
    ends,
    cot,
    normed,
    u_in,
    y_in,
    w_local,
    gate_far,
    gate_near,
    out_local,
    out_far,
    out_near,
    skip,
    gate_gain,
    heads,
    w_gate,
    w_out,
    gated_out,
    masked_out,
    dy_out,
    dgate_out,
    s1_out,
    gain_grad,
    skip_grad,
    gate_s,
    xs,
    prod_s,
    dg_s,
):
    step_id = pl.program_id(0)
    second_end = ends[1]
    inner = gate_s.shape[1]
    pairs = inner // LANES
    base = step_id * ROWS

    @pl.when(step_id == 0)
    def _():
        place_rows(w_gate, inner, w_local[...], gate_far, gate_near, ends[2], ends[3])
        place_rows(w_out, w_out.shape[1], out_local[...], out_far, out_near, ends[2], ends[3])
        gain_grad[...] = jnp.zeros_like(gain_grad)
        skip_grad[...] = jnp.zeros_like(skip_grad)

    gate_s[...] = dot(normed[...], w_gate[...])
    pos = lax.broadcasted_iota(jnp.int32, (ROWS, LANES), 0) + base
    live = (pos < second_end).astype(F32)
    masked = (cot[...].astype(F32) * live[:, 0:1]).astype(BF16)
    masked_out[...] = masked
    dg_s[...] = dot(masked, w_out[...], ((1,), (1,)))
    sq = jnp.zeros((ROWS, LANES), F32)
    cross = jnp.zeros((ROWS, LANES), F32)
    for ct in range(pairs):
        cols = slice(ct * LANES, (ct + 1) * LANES)
        half = 0.5 * gate_s[:, cols]
        half_u = 0.5 * u_in[:, cols].astype(F32)
        x = half_u + half_u * jnp.tanh(half_u)
        xs[:, cols] = x
        product = (y_in[:, cols] + skip[:, cols] * x) * (half + half * jnp.tanh(half))
        prod_s[:, cols] = product
        sq += product * product
        cross += dg_s[:, cols] * gate_gain[:, cols] * product
    r = lax.rsqrt(jnp.sum(sq, axis=1, keepdims=True) / inner + 1e-05)
    m = jnp.sum(cross, axis=1, keepdims=True) / inner
    r_wide = jnp.broadcast_to(r, (ROWS, LANES))
    m_wide = jnp.broadcast_to(r * r * r * m, (ROWS, LANES))
    for ct in range(pairs):
        cols = slice(ct * LANES, (ct + 1) * LANES)
        g = gate_s[:, cols]
        sig = 0.5 + 0.5 * jnp.tanh(0.5 * g)
        act = g * sig
        x = xs[:, cols]
        y = y_in[:, cols]
        product = prod_s[:, cols]
        pr = product * r_wide
        gated_out[:, cols] = (pr * gate_gain[:, cols]).astype(BF16)
        dg = dg_s[:, cols]
        gain_grad[:, cols] += fold8(dg * pr)
        dprod = r_wide * (dg * gate_gain[:, cols]) - product * m_wide
        dsc = dprod * act
        dgate_out[:, cols] = (
            dprod * (y + skip[:, cols] * x) * (sig + act * (1.0 - sig))
        ).astype(BF16)
        dy = dsc.astype(BF16)
        dy_out[:, cols] = dy
        skip_grad[:, cols] += fold8(dsc * x)
        prod_s[:, cols] = dy.astype(F32) * y
    s1_out[...] = head_sums(prod_s[...], heads[...])


def backward_kernel(
    first_pair,
    pairs,
    with_bc,
    last,
    resumed,
    ends,
    u_in,
    conv_in,
    ubc_in,
    cbc_in,
    raw_in,
    dy_in,
    s1_in,
    state_in,
    part_in,
    conv_w,
    step_bias,
    neg_rate,
    skip,
    heads,
    *refs,
):
    carried = refs[:8] if resumed else None
    refs = refs[8:] if resumed else refs
    (
        dconv_out,
        part_out,
        conv_w_grad,
        conv_b_grad,
        step_grad,
        decay_grad,
        dstate,
        halo,
        ext,
        xs,
        bc,
        slope,
        bds,
        q_s,
        dye_s,
        wx_s,
        rows_s,
    ) = refs
    step_id = pl.program_id(0)
    first_end = ends[0]
    second_end = ends[1]
    inner = pairs * LANES
    channels = ext.shape[1]
    base = (last - step_id) * ROWS

    @pl.when(step_id == 0)
    def _():
        sums = (conv_w_grad, conv_b_grad, step_grad, decay_grad, dstate, halo)
        for at, ref in enumerate(sums):
            ref[...] = carried[2 + at][...] if resumed else jnp.zeros_like(ref)
        ext[ROWS : ROWS + 8, :] = halo[...]
        rows_s[...] = jnp.zeros_like(rows_s)

    for ct in range(pairs + 2):
        if ct < pairs:
            u = u_in[:, ct * LANES : (ct + 1) * LANES].astype(F32)
        else:
            u = ubc_in[:, (ct - pairs) * LANES : (ct - pairs + 1) * LANES].astype(F32)
        sig = 0.5 + 0.5 * jnp.tanh(0.5 * u)
        act = u * sig
        if ct < pairs or with_bc:
            slope[:, ct * LANES : (ct + 1) * LANES] = sig + act * (1.0 - sig)
        if ct < pairs:
            xs[:, ct * LANES : (ct + 1) * LANES] = act
        else:
            bc[:, (ct - pairs) * LANES : (ct - pairs + 1) * LANES] = act

    def chunk(k, carry):
        q = ROWS // CHUNK - 1 - k
        r0 = pl.multiple_of(q * CHUNK, CHUNK)
        rsl = pl.ds(r0, CHUNK)
        raw = raw_in[rsl, :]
        row, col, step, rate, cum, same, entry, tail, keep = chunk_setup(
            raw, step_bias[...], neg_rate[...], base + r0, first_end, second_end
        )
        cum_t = cum.T
        lane_low = col < (LANES // 2)
        b_low = bc[rsl, 0:LANES].astype(BF16)
        c_f = bc[rsl, LANES : 2 * LANES]
        c_low = c_f.astype(BF16)
        allowed = same & (row <= col)
        gram = jnp.where(allowed, dot(b_low, c_low, ((1,), (1,))), 0.0)
        dstate_low = dstate[...].astype(BF16)
        bds[...] = dot(b_low, dstate_low)
        dgram = jnp.zeros((CHUNK, CHUNK), F32)
        for p in range(pairs):
            cols = slice(p * LANES, (p + 1) * LANES)
            head = 2 * (p + first_pair)
            ca, cb = lane_pair(cum, p + first_pair, lane_low)
            sa, sb = lane_pair(step, p + first_pair, lane_low)
            la = jnp.exp2(jnp.minimum(cum_t[head : head + 1, :] - ca, 0.0))
            lb = jnp.exp2(jnp.minimum(cum_t[head + 1 : head + 2, :] - cb, 0.0))
            both = jnp.where(lane_low, ca, cb)
            step_pair = jnp.where(lane_low, sa, sb)
            dy_low = dy_in[rsl, cols]
            dy = dy_low.astype(F32)
            dy2 = split_rows(dy_low, lane_low)
            xdt = xs[rsl, cols] * step_pair
            xdt_low = xdt.astype(BF16)
            mt = jnp.concatenate([(la * gram).astype(BF16), (lb * gram).astype(BF16)], axis=1)
            dmt = dot(xdt_low, dy2, ((1,), (1,)))
            dgram += dmt[:, :CHUNK] * la + dmt[:, CHUNK:] * lb
            end = both[CHUNK - 1 : CHUNK, :]
            weight = jnp.exp2(end - both) * tail
            gxs = weight * bds[:, cols]
            gx = dot(mt, dy2) + gxs
            xdt_r = xdt_low.astype(F32)
            q_s[:, cols] = xdt_r * gx
            ext[rsl, cols] = (step_pair * gx + skip[:, cols] * dy) * slope[rsl, cols]
            wx_s[:, cols] = (xdt * weight).astype(BF16)
            dye_s[:, cols] = (dy * (jnp.exp2(both) * entry)).astype(BF16)
            keep_row = jnp.exp2(end) * keep
            rows_s[8:9, cols] = keep_row
            rows_s[0:8, cols] = fold8(xdt_r * gxs) + keep_row * fold8(
                dstate[:, cols] * state_in[q, :, cols].astype(F32)
            )
        dgram = jnp.where(allowed, dgram, 0.0)
        dc = dot(dgram.T.astype(BF16), b_low) + dot(dye_s[...], state_in[q], ((1,), (1,)))
        db = dot(dgram.astype(BF16), c_low) + dot(wx_s[...], dstate_low, ((1,), (1,)))
        if with_bc:
            bsl = slice(inner, inner + LANES)
            csl = slice(inner + LANES, inner + 2 * LANES)
            ext[rsl, bsl] = (db + part_in[rsl, 0:LANES]) * slope[rsl, bsl]
            ext[rsl, csl] = (dc + part_in[rsl, LANES : 2 * LANES]) * slope[rsl, csl]
        else:
            part_out[rsl, 0:LANES] = db
            part_out[rsl, LANES : 2 * LANES] = dc
        dstate[...] = dstate[...] * rows_s[8:9, :] + dot(c_f.T.astype(BF16), dye_s[...])
        sx = head_sums(q_s[...], heads[...])
        end_term = jnp.sum(head_sums(rows_s[0:8, :], heads[...]), axis=0, keepdims=True)
        upper = (row <= col).astype(F32)
        drate = dot(upper, s1_in[rsl, :] - sx, precision=HIGH) + end_term
        own = (col >= 2 * first_pair) & (col < 2 * (first_pair + pairs))
        drate = jnp.where(own, drate, 0.0)
        dstep = sx / jnp.maximum(step, 1e-37) + neg_rate[...] * drate
        draw = dstep * jax.nn.sigmoid(raw + step_bias[...])
        if with_bc:
            draw = draw + part_in[rsl, 2 * LANES : 3 * LANES]
            dconv_out[rsl, channels : channels + LANES] = draw.astype(BF16)
            step_grad[...] += fold8(draw)
        else:
            part_out[rsl, 2 * LANES : 3 * LANES] = draw
        decay_grad[...] += fold8(drate * rate)
        return carry

    lax.fori_loop(0, ROWS // CHUNK, chunk, 0)

    pos = lax.broadcasted_iota(jnp.int32, (ROWS, LANES), 0) + base
    seg = segment_of(pos, first_end, second_end)
    shift_mask = [
        (segment_of(pos + k, first_end, second_end) == seg).astype(F32) for k in range(1, 4)
    ]
    for ct in range(channels // LANES):
        cols = slice(ct * LANES, (ct + 1) * LANES)
        du = ext[0:ROWS, cols]
        if ct < pairs:
            source = conv_in[:, cols].astype(F32)
        else:
            source = cbc_in[:, (ct - pairs) * LANES : (ct - pairs + 1) * LANES].astype(F32)
        conv_b_grad[:, cols] += fold8(du)
        conv_w_grad[24:32, cols] += fold8(source * du)
        total = conv_w[3:4, cols] * du
        for k in range(1, 4):
            later = ext[k : k + ROWS, cols] * shift_mask[k - 1]
            total += conv_w[3 - k : 4 - k, cols] * later
            conv_w_grad[8 * (3 - k) : 8 * (4 - k), cols] += fold8(source * later)
        dconv_out[:, cols] = total.astype(BF16)
    ext[ROWS : ROWS + 8, :] = ext[0:8, :]
    halo[...] = ext[0:8, :]


def out_kernel(ends, tok, gated, w_out, block_out):
    pos = lax.broadcasted_iota(jnp.int32, (TAIL, 1), 0) + pl.program_id(0) * TAIL
    live = (pos < ends[1]).astype(F32)
    block_out[...] = (tok[...].astype(F32) + live * dot(gated[...], w_out[...])).astype(BF16)


def part_kernel(dgate, rest_a, w_gate, w_conv, grad):
    grad[...] = dot(dgate[...], w_gate[...], ((1,), (1,))) + dot(rest_a[...], w_conv[...], ((1,), (1,)))


def norm_kernel(tok, cot, part, rest_b, w_conv, norm_gain, grad_tokens):
    split = w_conv.shape[1] - rest_b.shape[1]
    grad = part[...] + dot(rest_b[...], w_conv[:, split:], ((1,), (1,)))
    rows = tok[...].astype(F32)
    r = lax.rsqrt(jnp.mean(rows * rows, axis=-1, keepdims=True) + 1e-05)
    n = rows * r
    weighted = norm_gain[...] * grad
    mean = jnp.mean(weighted * n, axis=-1, keepdims=True)
    grad_tokens[...] = (r * (weighted - n * mean) + cot[...].astype(F32)).astype(BF16)


def whole(shape):
    return pl.BlockSpec(shape, lambda i: (0,) * len(shape))


def params():
    return pltpu.CompilerParams(dimension_semantics=("arbitrary",), vmem_limit_bytes=VMEM_LIMIT)


def cost(flops, moved):
    return pl.CostEstimate(flops=flops, bytes_accessed=moved, transcendentals=20_000_000)


SMEM = pl.BlockSpec(memory_space=pltpu.SMEM)


def run_scan(ends, tok, w_local, w_far, w_near, norm_gain, conv_w, conv_b, step_bias, neg_rate, inner):
    count, width = tok.shape
    channels = conv_w.shape[1]
    per = ROWS // CHUNK

    def rows_of(n):
        return pl.BlockSpec((ROWS, n), lambda i: (i, 0))

    shape = jax.ShapeDtypeStruct
    return pl.pallas_call(
        scan_kernel,
        grid=(count // ROWS,),
        in_specs=[SMEM, rows_of(width)]
        + [
            whole(v.shape)
            for v in (w_local, w_far, w_near, norm_gain, conv_w, conv_b, step_bias, neg_rate)
        ],
        out_specs=[
            rows_of(width),
            rows_of(channels),
            rows_of(channels),
            rows_of(LANES),
            rows_of(inner),
            pl.BlockSpec((per, LANES, inner), lambda i: (i, 0, 0)),
            whole((width, channels + LANES)),
        ],
        out_shape=[
            shape((count, width), BF16),
            shape((count, channels), BF16),
            shape((count, channels), BF16),
            shape((count, LANES), F32),
            shape((count, inner), F32),
            shape((count // CHUNK, LANES, inner), BF16),
            shape((width, channels + LANES), BF16),
        ],
        scratch_shapes=[
            pltpu.VMEM((ROWS + 8, channels), F32),
            pltpu.VMEM((ROWS, inner), F32),
            pltpu.VMEM((ROWS, 2 * LANES), F32),
            pltpu.VMEM((CHUNK, inner), BF16),
            pltpu.VMEM((8, inner), F32),
            pltpu.VMEM((LANES, inner), F32),
        ],
        compiler_params=params(),
        cost_estimate=cost(50_000_000_000, 50_000_000),
        name="mixer_scan",
    )(ends, tok, w_local, w_far, w_near, norm_gain, conv_w, conv_b, step_bias, neg_rate)


def run_gate(ends, cot, normed, u, y, w_local, gate_far, gate_near, out_local, out_far, out_near, skip, gate_gain, heads):
    count, width = cot.shape
    inner = y.shape[1]

    def rows_of(n):
        return pl.BlockSpec((ROWS, n), lambda i: (i, 0))

    shape = jax.ShapeDtypeStruct
    return pl.pallas_call(
        gate_kernel,
        grid=(count // ROWS,),
        in_specs=[SMEM, rows_of(width), rows_of(width), rows_of(inner), rows_of(inner)]
        + [pl.BlockSpec((w_local.shape[0], inner), lambda i: (0, 0))]
        + [
            whole(v.shape)
            for v in (gate_far, gate_near, out_local, out_far, out_near, skip, gate_gain, heads)
        ],
        out_specs=[
            whole((width, inner)),
            whole((inner, width)),
            rows_of(inner),
            rows_of(width),
            rows_of(inner),
            rows_of(inner),
            rows_of(LANES),
            whole((8, inner)),
            whole((8, inner)),
        ],
        out_shape=[
            shape((width, inner), BF16),
            shape((inner, width), BF16),
            shape((count, inner), BF16),
            shape((count, width), BF16),
            shape((count, inner), BF16),
            shape((count, inner), BF16),
            shape((count, LANES), F32),
            shape((8, inner), F32),
            shape((8, inner), F32),
        ],
        scratch_shapes=[pltpu.VMEM((ROWS, inner), F32) for _ in range(4)],
        compiler_params=params(),
        cost_estimate=cost(35_000_000_000, 50_000_000),
        name="gate_both_ways",
    )(ends, cot, normed, u, y, w_local, gate_far, gate_near, out_local, out_far, out_near, skip, gate_gain, heads)


def run_backward(first_pair, pairs, part, carried, ends, u, conv_in, raw, dy, s1, states, conv_w, step_bias, neg_rate, skip, heads):
    count, full_channels = u.shape
    full_inner = dy.shape[1]
    with_bc = part is not None
    inner = pairs * LANES
    channels = inner + (2 * LANES if with_bc else 0)
    per = ROWS // CHUNK
    steps = count // ROWS // 2
    resumed = carried is not None
    last = steps - 1 if resumed else 2 * steps - 1
    at = first_pair // pairs
    bc_at = full_inner // (2 * LANES)
    if part is None:
        part = jnp.zeros((8, LANES), F32)
        part_spec = whole(part.shape)
        part_out_shape = (count, 3 * LANES)
        width_out = channels
        own_taps = conv_w[:, first_pair * LANES : first_pair * LANES + inner]
    else:
        part_spec = pl.BlockSpec((ROWS, 3 * LANES), lambda i: (last - i, 0))
        part_out_shape = (8, LANES)
        width_out = channels + LANES
        own_taps = conv_w[:, first_pair * LANES :]

    def rows_of(n, c=0):
        return pl.BlockSpec((ROWS, n), lambda i: (last - i, c))

    shape = jax.ShapeDtypeStruct
    sums = ((32, channels), (8, channels), (8, LANES), (8, LANES), (LANES, inner), (8, channels))
    in_specs = [
        SMEM,
        rows_of(inner, at),
        rows_of(inner, at),
        rows_of(2 * LANES, bc_at),
        rows_of(2 * LANES, bc_at),
        rows_of(LANES),
        rows_of(inner, at),
        rows_of(LANES),
        pl.BlockSpec((per, LANES, inner), lambda i: (last - i, 0, at)),
        part_spec,
        whole(own_taps.shape),
        whole(step_bias.shape),
        whole(neg_rate.shape),
        pl.BlockSpec((1, inner), lambda i: (0, at)),
        pl.BlockSpec((inner, LANES), lambda i: (at, 0)),
    ]
    args = [ends, u, conv_in, u, conv_in, raw, dy, s1, states, part, own_taps, step_bias, neg_rate, skip, heads]
    aliases = {}
    if resumed:
        aliases = {len(args): 0, len(args) + 1: 1}
        args += list(carried)
        in_specs += [pl.BlockSpec(memory_space=pl.ANY)] * 2 + [whole(s) for s in sums]
    return pl.pallas_call(
        functools.partial(backward_kernel, first_pair, pairs, with_bc, last, resumed),
        grid=(steps,),
        in_specs=in_specs,
        out_specs=[
            rows_of(width_out),
            whole(part_out_shape) if with_bc else rows_of(3 * LANES),
        ]
        + [whole(s) for s in sums],
        out_shape=[shape((count, width_out), BF16), shape(part_out_shape, F32)]
        + [shape(s, F32) for s in sums],
        scratch_shapes=[
            pltpu.VMEM((ROWS + 8, channels), F32),
            pltpu.VMEM((ROWS, inner), F32),
            pltpu.VMEM((ROWS, 2 * LANES), F32),
            pltpu.VMEM((ROWS, channels), F32),
            pltpu.VMEM((CHUNK, inner), F32),
            pltpu.VMEM((CHUNK, inner), F32),
            pltpu.VMEM((CHUNK, inner), BF16),
            pltpu.VMEM((CHUNK, inner), BF16),
            pltpu.VMEM((16, inner), F32),
        ],
        input_output_aliases=aliases,
        compiler_params=params(),
        cost_estimate=cost(25_000_000_000, 20_000_000),
        name=("backward_b" if with_bc else "backward_a") + ("_low" if resumed else "_high"),
    )(*args)


def tail_rows(n):
    return pl.BlockSpec((TAIL, n), lambda i: (i, 0))


def run_out(ends, tok, gated, w_out):
    count, width = tok.shape
    return pl.pallas_call(
        out_kernel,
        grid=(count // TAIL,),
        in_specs=[SMEM, tail_rows(width), tail_rows(gated.shape[1]), whole(w_out.shape)],
        out_specs=tail_rows(width),
        out_shape=jax.ShapeDtypeStruct((count, width), BF16),
        compiler_params=params(),
        cost_estimate=cost(8_000_000_000, 15_000_000),
        name="block_out",
    )(ends, tok, gated, w_out)


def run_part(dgate, rest_a, w_gate, w_conv):
    count = dgate.shape[0]
    width = w_conv.shape[0]
    return pl.pallas_call(
        part_kernel,
        grid=(count // TAIL,),
        in_specs=[
            tail_rows(dgate.shape[1]),
            tail_rows(rest_a.shape[1]),
            whole(w_gate.shape),
            pl.BlockSpec((width, rest_a.shape[1]), lambda i: (0, 0)),
        ],
        out_specs=tail_rows(width),
        out_shape=jax.ShapeDtypeStruct((count, width), F32),
        compiler_params=params(),
        cost_estimate=cost(10_000_000_000, 20_000_000),
        name="grad_normed_part",
    )(dgate, rest_a, w_gate, w_conv)


def run_norm(tok, cot, part, rest_b, w_conv, norm_gain):
    count, width = tok.shape
    return pl.pallas_call(
        norm_kernel,
        grid=(count // TAIL,),
        in_specs=[
            tail_rows(width),
            tail_rows(width),
            tail_rows(width),
            tail_rows(rest_b.shape[1]),
            whole(w_conv.shape),
            whole(norm_gain.shape),
        ],
        out_specs=tail_rows(width),
        out_shape=jax.ShapeDtypeStruct((count, width), BF16),
        compiler_params=params(),
        cost_estimate=cost(10_000_000_000, 20_000_000),
        name="norm_backward",
    )(tok, cot, part, rest_b, w_conv, norm_gain)


def pad_lanes(v):
    return jnp.pad(v, ((0, 0), (0, LANES - v.shape[1])))


def swap(v, mask):
    n = lax.axis_size("rep") * lax.axis_size("shard")
    return lax.ppermute(v, ("rep", "shard"), [(i, i ^ mask) for i in range(n)])


def place():
    return lax.axis_index("rep") * lax.axis_size("shard") + lax.axis_index("shard")


SHARD, CORE = 1, 2


def half_rows(v):
    half = v.shape[0] // 2
    core = (place() // CORE) % 2
    return lax.dynamic_slice_in_dim(v, core * half, half, 0)


def take(v, index):
    return lax.dynamic_index_in_dim(v, index, 0, keepdims=False)


def exchanges():
    n = lax.axis_size("rep") * lax.axis_size("shard")
    bits = [SHARD]
    bit = 2 * CORE
    while bit < n:
        bits.append(bit)
        bit *= 2
    return bits


def at_bit(bit):
    return (place() // bit) % 2


def cut(v, bit):
    if v.ndim == 2:
        v = v.reshape(2, v.shape[0] // 2, v.shape[1])
    me = at_bit(bit)
    return take(v, me), take(v, 1 - me).astype(BF16)


def add(kept, got):
    return kept + got.astype(F32)


def both_sum(low, bit):
    return (low.astype(F32) + swap(low, bit).astype(F32)).astype(BF16)


def join(low, got, bit):
    return jnp.where(at_bit(bit) == 0, jnp.concatenate([low, got], 0), jnp.concatenate([got, low], 0))


def core_sum(g):
    rows, n = g.shape
    v = g.reshape(2, 2, rows // 4, n)
    core = (place() // CORE) % 2
    other = lax.dynamic_index_in_dim(v, 1 - core, 1, keepdims=False).astype(BF16)
    kept = lax.dynamic_index_in_dim(v, core, 1, keepdims=False)
    return kept + swap(other, CORE).astype(F32)


def after(gate, *values):
    return lax.optimization_barrier((gate, *values))


def per_device(
    tokens,
    cotangent,
    seq_lengths,
    seq_device,
    norm_gain,
    in_weight,
    conv_weight,
    conv_bias,
    step_bias,
    decay_log,
    skip_gain,
    gate_gain,
    out_weight,
):
    shards = lax.axis_size("shard")
    shard = lax.axis_index("shard")
    device = lax.axis_index("rep") * shards + shard
    half_count = seq_lengths.shape[0] // 2
    owned = seq_device[:half_count] == device
    first_len = jnp.sum(jnp.where(owned, seq_lengths[:half_count], 0))
    second_len = jnp.sum(jnp.where(owned, seq_lengths[half_count:], 0))
    ends = jnp.stack(
        [first_len, first_len + second_len, lax.axis_index("rep") % 2, shard]
    ).astype(jnp.int32)
    count, width = tokens.shape
    inner = gate_gain.shape[0] * shards
    channels = conv_weight.shape[1] * shards
    head_count = step_bias.shape[0] * shards
    size = inner // head_count
    taps = conv_weight.shape[0]

    small = (norm_gain, conv_weight.reshape(-1), conv_bias, step_bias, decay_log, skip_gain, gate_gain)
    sizes = [v.shape[0] for v in small]
    own = jnp.concatenate(small)
    own = jnp.pad(own, (0, -own.shape[0] % 1024)).reshape(-1, LANES)
    in_half = half_rows(in_weight)
    conv_far = swap(in_half[:, inner:], SHARD)
    other = swap(own, SHARD)
    conv_near = swap(conv_far, CORE)
    conv_near, gate_send, out_send = after(conv_near, in_half[:, :inner], half_rows(out_weight))
    gate_far = swap(gate_send, SHARD)
    out_far = swap(out_send, SHARD)

    packed = jnp.where(shard == 0, jnp.stack([own, other]), jnp.stack([other, own])).reshape(2, -1)
    parts = []
    at = 0
    for n in sizes:
        parts.append(packed[:, at : at + n])
        at += n
    full_norm, _, full_shift, full_step, full_decay, full_skip, full_gate = [
        p.reshape(-1).astype(F32) for p in parts
    ]
    conv_w = parts[1].reshape(shards, taps, -1).transpose(1, 0, 2).reshape(taps, -1).astype(F32)
    conv_b = full_shift[None, :]
    norm_row = full_norm[None, :]
    gate_row = full_gate[None, :]
    lane_head = lax.broadcasted_iota(jnp.int32, (inner, LANES), 0) // size
    heads = (lane_head == lax.broadcasted_iota(jnp.int32, (inner, LANES), 1)).astype(BF16)
    skip = jnp.repeat(full_skip, size)[None, :]
    step_row = pad_lanes(full_step[None, :])
    neg_rate = pad_lanes(-jnp.exp(full_decay)[None, :])

    normed, u, conv_in, raw, y, states, w_conv = run_scan(
        ends, tokens, in_weight, conv_far, conv_near, norm_row, conv_w, conv_b, step_row, neg_rate, inner
    )
    normed, gate_far, out_far = after(normed, gate_far, out_far)
    gate_near = swap(gate_far, CORE)
    out_near = swap(out_far, CORE)
    w_gate, w_out, gated, masked, dy, dgate, s1, gain8, skip8 = run_gate(
        ends, cotangent, normed, u, y, in_weight, gate_far, gate_near, out_weight, out_far, out_near, skip, gate_row, heads
    )
    bits = exchanges()
    far, last_bit = bits[1:-1], bits[-1]
    g_out = dot(gated, masked, ((0,), (0,)))
    h_out = core_sum(g_out)
    g_out, normed = after(g_out, normed)
    g_gate = dot(normed, dgate, ((0,), (0,)))
    h_gate = core_sum(g_gate)
    quarter = h_out.shape[1] // 2
    held = jnp.concatenate([h_out[:, :quarter], h_out[:, quarter:], h_gate], axis=2)
    half_pairs = inner // LANES // 2
    shared = (s1, states, conv_w, step_row, neg_rate, skip, heads)

    kept, sent = cut(held, SHARD)
    dy, sent = after(dy, sent)
    got = swap(sent, SHARD)
    carry = run_backward(0, half_pairs, None, None, ends, u, conv_in, raw, dy, *shared)
    first_out, kept, got = after(carry[0], kept, got)
    kept, sent = cut(add(kept, got), far[0])
    dy, sent = after(dy, sent)
    got = swap(sent, far[0])
    rest_a, part, cw_a, cb_a, _, dl_a, _, _ = run_backward(
        0, half_pairs, None, (first_out, *carry[1:]), ends, u, conv_in, raw, dy, *shared
    )
    rest_a, kept, got = after(rest_a, kept, got)
    g_a = dot(normed, rest_a, ((0,), (0,)))
    held = add(kept, got)
    kept, sent = cut(held, far[1])
    kept_a, sent_a = cut(core_sum(g_a), SHARD)
    part, sent, sent_a = after(part, sent, sent_a)
    got = swap(sent, far[1])
    got_a = swap(sent_a, SHARD)
    carry = run_backward(half_pairs, half_pairs, part, None, ends, u, conv_in, raw, dy, *shared)
    first_out, kept, got, kept_a, got_a = after(carry[0], kept, got, kept_a, got_a)
    held = add(kept, got)
    for bit in far[2:]:
        kept, sent = cut(held, bit)
        held = add(kept, swap(sent, bit))
    low = held.astype(BF16)
    kept_a, sent_a = cut(add(kept_a, got_a), far[0])
    part, low, sent_a = after(part, low, sent_a)
    got = swap(low, last_bit)
    got_a = swap(sent_a, far[0])
    rest_b, _, cw_b, cb_b, sb_b, dl_b, _, _ = run_backward(
        half_pairs, half_pairs, part, (first_out, *carry[1:]), ends, u, conv_in, raw, dy, *shared
    )
    rest_b, low, got, kept_a, got_a = after(rest_b, low, got, kept_a, got_a)
    g_b = dot(normed, rest_b, ((0,), (0,)))

    split = channels - half_pairs * LANES
    g_conv = jnp.sum(jnp.concatenate([cw_a, cw_b], 1).reshape(taps, 8, channels), axis=1)
    g_shift = jnp.sum(jnp.concatenate([cb_a, cb_b], 1), axis=0)
    g_step = jnp.sum(sb_b, axis=0)[:head_count]
    g_decay = jnp.sum(dl_a + dl_b, axis=0)[:head_count]
    g_skip = jnp.sum(skip8.reshape(8, head_count, size), axis=(0, 2))
    g_gain = jnp.sum(gain8, axis=0)
    pieces = (
        g_conv.reshape(taps, shards, -1).transpose(1, 0, 2).reshape(shards, -1),
        g_shift.reshape(shards, -1),
        g_step.reshape(shards, -1),
        g_decay.reshape(shards, -1),
        g_skip.reshape(shards, -1),
        g_gain.reshape(shards, -1),
    )
    flat = jnp.concatenate(pieces, axis=1)
    own_rows = width // shards
    extra = -(-flat.shape[1] // own_rows)
    flat = jnp.pad(flat, ((0, 0), (0, extra * own_rows - flat.shape[1])))
    flat = flat.reshape(shards, extra, own_rows).transpose(0, 2, 1).reshape(width, extra)
    g_b = jnp.concatenate([g_b[:, : split + head_count], flat], axis=1)
    low = add(low.astype(F32), got).astype(BF16)
    held_a = add(kept_a, got_a)
    kept_b, sent_b = cut(core_sum(g_b), SHARD)
    backs = far[::-1] + [CORE]
    gated, low, sent_b = after(gated, low, sent_b)
    got = swap(low, backs[0])
    got_b = swap(sent_b, SHARD)
    block_out = run_out(ends, tokens, gated, w_out)
    block_out, low, got, kept_b, got_b = after(block_out, low, got, kept_b, got_b)
    low = join(low, got, backs[0])
    kept_b, sent_b = cut(add(kept_b, got_b), far[0])
    dgate, low, sent_b = after(dgate, low, sent_b)
    got = swap(low, backs[1])
    got_b = swap(sent_b, far[0])
    grad_part = run_part(dgate, rest_a, w_gate, w_conv)
    grad_part, low, got, kept_b, got_b = after(grad_part, low, got, kept_b, got_b)
    low = join(low, got, backs[1])
    held_b = jnp.concatenate([held_a, add(kept_b, got_b)], axis=1)
    kept_b, sent_b = cut(held_b, far[1])
    grad_part, low, sent_b = after(grad_part, low, sent_b)
    got = swap(low, backs[2])
    got_b = swap(sent_b, far[1])
    grad_tokens = run_norm(tokens, cotangent, grad_part, rest_b, w_conv, norm_row)
    grad_tokens, low, got, kept_b, got_b = after(grad_tokens, low, got, kept_b, got_b)
    low = join(low, got, backs[2])
    for bit in backs[3:]:
        low = join(low, swap(low, bit), bit)
    held_b = add(kept_b, got_b)
    for bit in far[2:]:
        kept_b, sent_b = cut(held_b, bit)
        held_b = add(kept_b, swap(sent_b, bit))
    low_b = both_sum(held_b.astype(BF16), last_bit)
    for bit in backs:
        low_b = join(low_b, swap(low_b, bit), bit)
    near = out_weight.shape[1]
    by_core = low.reshape(2, low.shape[0] // 2, low.shape[1])
    t_out = jnp.concatenate(
        [by_core[0, :, :near], by_core[0, :, near : 2 * near], by_core[1, :, :near], by_core[1, :, near : 2 * near]], axis=0
    )
    t_b = low_b[:, half_pairs * LANES :]
    t_in = jnp.concatenate(
        [low[:, 2 * near :], low_b[:, : half_pairs * LANES + split + head_count]], axis=1
    ).astype(F32)
    t_norm = jnp.sum(t_in * in_weight.astype(F32), axis=1) / norm_gain.astype(F32)
    mine = t_b[:, split + head_count :].T.reshape(-1).astype(F32)
    outs = []
    at = 0
    for n in sizes[1:]:
        outs.append(mine[at : at + n])
        at += n
    return (
        block_out,
        grad_tokens,
        t_norm,
        t_in,
        outs[0].reshape(taps, -1),
        outs[1],
        outs[2],
        outs[3],
        outs[4],
        outs[5],
        t_out.astype(F32),
    )


def solution(mesh):
    in_specs = (
        P(("rep", "shard"), None),
        P(("rep", "shard"), None),
        P(),
        P(),
        P("shard"),
        P("shard", None),
        P(None, "shard"),
        P("shard"),
        P("shard"),
        P("shard"),
        P("shard"),
        P("shard"),
        P("shard", None),
    )
    out_specs = (
        P(("rep", "shard"), None),
        P(("rep", "shard"), None),
        P("shard"),
        P("shard", None),
        P(None, "shard"),
        P("shard"),
        P("shard"),
        P("shard"),
        P("shard"),
        P("shard"),
        P("shard", None),
    )
    return jax.shard_map(
        per_device, mesh=mesh, in_specs=in_specs, out_specs=out_specs, check_vma=False
    )
```

```python
import functools

import jax
import jax.numpy as jnp
from jax import lax
from jax.experimental import pallas as pl
from jax.experimental.pallas import tpu as pltpu
from jax.sharding import PartitionSpec as P

ROWS = 256
CHUNK = 128
TAIL = 512
LANES = 128
LOG2E = 1.4426950408889634
F32 = jnp.float32
BF16 = jnp.bfloat16
HIGH = lax.Precision.HIGHEST
VMEM_LIMIT = 60 * 1024 * 1024


def dot(a, b, dims=((1,), (0,)), precision=None):
    return lax.dot_general(a, b, (dims, ((), ())), precision=precision, preferred_element_type=F32)


def fold8(v):
    return jnp.sum(v.reshape(v.shape[0] // 8, 8, v.shape[1]), axis=0)


def segment_of(position, first_end, second_end):
    return (position >= first_end).astype(jnp.int32) + (position >= second_end).astype(jnp.int32)


def softplus(v):
    return jnp.maximum(v, 0.0) + jnp.log1p(jnp.exp(-jnp.abs(v)))


def head_sums(v, heads):
    high = v.astype(BF16)
    low = (v - high.astype(F32)).astype(BF16)
    return dot(high, heads) + dot(low, heads)


def lane_pair(v, p, lane_low):
    shape = lane_low.shape
    a = jnp.broadcast_to(v[:, 2 * p : 2 * p + 1], shape)
    b = jnp.broadcast_to(v[:, 2 * p + 1 : 2 * p + 2], shape)
    return a, b


def split_rows(pair, lane_low):
    zero = jnp.zeros_like(pair)
    return jnp.concatenate(
        [jnp.where(lane_low, pair, zero), jnp.where(lane_low, zero, pair)], axis=0
    )


def chunk_setup(raw, step_bias, neg_rate, start, first_end, second_end):
    row = lax.broadcasted_iota(jnp.int32, (CHUNK, LANES), 0)
    col = lax.broadcasted_iota(jnp.int32, (CHUNK, LANES), 1)
    step = softplus(raw + step_bias)
    rate = neg_rate * step
    lower = (row >= col).astype(F32)
    cum = dot(lower, rate, precision=HIGH) * LOG2E
    seg_row = segment_of(row + start, first_end, second_end)
    seg_col = segment_of(col + start, first_end, second_end)
    last_seg = segment_of(start - 1, first_end, second_end)
    end_seg = segment_of(start + CHUNK - 1, first_end, second_end)
    entry = (seg_row == last_seg).astype(F32)
    tail = (seg_row == end_seg).astype(F32)
    keep = (last_seg == end_seg).astype(F32)
    same = seg_row == seg_col
    return row, col, step, rate, cum, same, entry, tail, keep


def place_rows(dst, width, local, far, near, core, shard):
    half = far.shape[0]
    own_at = pl.multiple_of(shard * (2 * half), half)
    other_at = (1 - shard) * (2 * half)
    dst[pl.ds(own_at, 2 * half), :width] = local
    dst[pl.ds(pl.multiple_of(other_at + core * half, half), half), :width] = far[...]
    dst[pl.ds(pl.multiple_of(other_at + (1 - core) * half, half), half), :width] = near[...]


def scan_kernel(
    ends,
    tok,
    w_local,
    w_far,
    w_near,
    norm_gain,
    conv_w,
    conv_b,
    step_bias,
    neg_rate,
    normed_out,
    u_out,
    conv_in_out,
    raw_out,
    y_out,
    state_out,
    w_conv,
    ext,
    xs,
    bc,
    wx_s,
    keep_s,
    state,
):
    step_id = pl.program_id(0)
    first_end = ends[0]
    second_end = ends[1]
    inner = xs.shape[1]
    channels = ext.shape[1]
    pairs = inner // LANES
    base = step_id * ROWS

    @pl.when(step_id == 0)
    def _():
        w_conv[:, channels:] = jnp.zeros((w_conv.shape[0], LANES), BF16)
        used = w_far.shape[1]
        place_rows(w_conv, used, w_local[:, inner:], w_far, w_near, ends[2], ends[3])
        ext[0:8, :] = jnp.zeros((8, channels), F32)
        state[...] = jnp.zeros_like(state)

    rows = tok[...].astype(F32)
    scale = lax.rsqrt(jnp.mean(rows * rows, axis=-1, keepdims=True) + 1e-05)
    normed = (rows * scale * norm_gain[...]).astype(BF16)
    normed_out[...] = normed
    conv_in = dot(normed, w_conv[:, :channels])
    ext[8 : 8 + ROWS, :] = conv_in
    conv_in_out[...] = conv_in.astype(BF16)
    raw_out[...] = dot(normed, w_conv[:, channels:])

    pos = lax.broadcasted_iota(jnp.int32, (ROWS, LANES), 0) + base
    seg = segment_of(pos, first_end, second_end)
    shift_mask = [
        ((segment_of(pos - k, first_end, second_end) == seg) & (pos >= k)).astype(F32)
        for k in range(1, 4)
    ]

    def conv_tile(ct):
        cols = slice(ct * LANES, (ct + 1) * LANES)
        total = conv_b[:, cols] + conv_w[3:4, cols] * ext[8 : 8 + ROWS, cols]
        for k in range(1, 4):
            total += (conv_w[3 - k : 4 - k, cols] * ext[8 - k : 8 - k + ROWS, cols]) * shift_mask[k - 1]
        u = total.astype(BF16)
        u_out[:, cols] = u
        half = 0.5 * u.astype(F32)
        return half + half * jnp.tanh(half)

    for ct in range(pairs):
        xs[:, ct * LANES : (ct + 1) * LANES] = conv_tile(ct)
    for ct in range(pairs, channels // LANES):
        bc[:, (ct - pairs) * LANES : (ct - pairs + 1) * LANES] = conv_tile(ct)
    ext[0:8, :] = ext[ROWS : ROWS + 8, :]

    def chunk(q, carry):
        r0 = pl.multiple_of(q * CHUNK, CHUNK)
        rsl = pl.ds(r0, CHUNK)
        row, col, step, rate, cum, same, entry, tail, keep = chunk_setup(
            raw_out[rsl, :], step_bias[...], neg_rate[...], base + r0, first_end, second_end
        )
        cum_t = cum.T
        lane_low = col < (LANES // 2)
        b_f = bc[rsl, 0:LANES]
        b_low = b_f.astype(BF16)
        c_low = bc[rsl, LANES : 2 * LANES].astype(BF16)
        gram = dot(c_low, b_low, ((1,), (1,)))
        gram = jnp.where(same & (row >= col), gram, 0.0)
        state_low = state[...].astype(BF16)
        state_out[q] = state_low
        y_out[rsl, :] = dot(c_low, state_low)
        for p in range(pairs):
            cols = slice(p * LANES, (p + 1) * LANES)
            ca, cb = lane_pair(cum, p, lane_low)
            sa, sb = lane_pair(step, p, lane_low)
            ma = (jnp.exp2(jnp.minimum(ca - cum_t[2 * p : 2 * p + 1, :], 0.0)) * gram).astype(BF16)
            mb = (jnp.exp2(jnp.minimum(cb - cum_t[2 * p + 1 : 2 * p + 2, :], 0.0)) * gram).astype(BF16)
            both = jnp.where(lane_low, ca, cb)
            xdt = xs[rsl, cols] * jnp.where(lane_low, sa, sb)
            xdt_low = xdt.astype(BF16)
            inner_y = dot(jnp.concatenate([ma, mb], axis=1), split_rows(xdt_low, lane_low))
            y_out[rsl, cols] = inner_y + y_out[rsl, cols] * (jnp.exp2(both) * entry)
            end = both[CHUNK - 1 : CHUNK, :]
            wx_s[:, cols] = (xdt * (jnp.exp2(end - both) * tail)).astype(BF16)
            keep_s[0:1, cols] = jnp.exp2(end) * keep
        state[...] = state[...] * keep_s[0:1, :] + dot(b_f.T.astype(BF16), wx_s[...])
        return carry

    lax.fori_loop(0, ROWS // CHUNK, chunk, 0)


def gate_kernel(
    ends,
    cot,
    normed,
    u_in,
    y_in,
    w_local,
    gate_far,
    gate_near,
    out_local,
    out_far,
    out_near,
    skip,
    gate_gain,
    heads,
    w_gate,
    w_out,
    gated_out,
    masked_out,
    dy_out,
    dgate_out,
    s1_out,
    gain_grad,
    skip_grad,
    gate_s,
    xs,
    prod_s,
    dg_s,
):
    step_id = pl.program_id(0)
    second_end = ends[1]
    inner = gate_s.shape[1]
    pairs = inner // LANES
    base = step_id * ROWS

    @pl.when(step_id == 0)
    def _():
        place_rows(w_gate, inner, w_local[...], gate_far, gate_near, ends[2], ends[3])
        place_rows(w_out, w_out.shape[1], out_local[...], out_far, out_near, ends[2], ends[3])
        gain_grad[...] = jnp.zeros_like(gain_grad)
        skip_grad[...] = jnp.zeros_like(skip_grad)

    gate_s[...] = dot(normed[...], w_gate[...])
    pos = lax.broadcasted_iota(jnp.int32, (ROWS, LANES), 0) + base
    live = (pos < second_end).astype(F32)
    masked = (cot[...].astype(F32) * live[:, 0:1]).astype(BF16)
    masked_out[...] = masked
    dg_s[...] = dot(masked, w_out[...], ((1,), (1,)))
    sq = jnp.zeros((ROWS, LANES), F32)
    cross = jnp.zeros((ROWS, LANES), F32)
    for ct in range(pairs):
        cols = slice(ct * LANES, (ct + 1) * LANES)
        half = 0.5 * gate_s[:, cols]
        half_u = 0.5 * u_in[:, cols].astype(F32)
        x = half_u + half_u * jnp.tanh(half_u)
        xs[:, cols] = x
        product = (y_in[:, cols] + skip[:, cols] * x) * (half + half * jnp.tanh(half))
        prod_s[:, cols] = product
        sq += product * product
        cross += dg_s[:, cols] * gate_gain[:, cols] * product
    r = lax.rsqrt(jnp.sum(sq, axis=1, keepdims=True) / inner + 1e-05)
    m = jnp.sum(cross, axis=1, keepdims=True) / inner
    r_wide = jnp.broadcast_to(r, (ROWS, LANES))
    m_wide = jnp.broadcast_to(r * r * r * m, (ROWS, LANES))
    for ct in range(pairs):
        cols = slice(ct * LANES, (ct + 1) * LANES)
        g = gate_s[:, cols]
        sig = 0.5 + 0.5 * jnp.tanh(0.5 * g)
        act = g * sig
        x = xs[:, cols]
        y = y_in[:, cols]
        product = prod_s[:, cols]
        pr = product * r_wide
        gated_out[:, cols] = (pr * gate_gain[:, cols]).astype(BF16)
        dg = dg_s[:, cols]
        gain_grad[:, cols] += fold8(dg * pr)
        dprod = r_wide * (dg * gate_gain[:, cols]) - product * m_wide
        dsc = dprod * act
        dgate_out[:, cols] = (
            dprod * (y + skip[:, cols] * x) * (sig + act * (1.0 - sig))
        ).astype(BF16)
        dy = dsc.astype(BF16)
        dy_out[:, cols] = dy
        skip_grad[:, cols] += fold8(dsc * x)
        prod_s[:, cols] = dy.astype(F32) * y
    s1_out[...] = head_sums(prod_s[...], heads[...])


def backward_kernel(
    first_pair,
    pairs,
    with_bc,
    last,
    resumed,
    ends,
    u_in,
    conv_in,
    ubc_in,
    cbc_in,
    raw_in,
    dy_in,
    s1_in,
    state_in,
    part_in,
    conv_w,
    step_bias,
    neg_rate,
    skip,
    heads,
    *refs,
):
    carried = refs[:8] if resumed else None
    refs = refs[8:] if resumed else refs
    (
        dconv_out,
        part_out,
        conv_w_grad,
        conv_b_grad,
        step_grad,
        decay_grad,
        dstate,
        halo,
        ext,
        xs,
        bc,
        slope,
        bds,
        q_s,
        dye_s,
        wx_s,
        rows_s,
    ) = refs
    step_id = pl.program_id(0)
    first_end = ends[0]
    second_end = ends[1]
    inner = pairs * LANES
    channels = ext.shape[1]
    base = (last - step_id) * ROWS

    @pl.when(step_id == 0)
    def _():
        sums = (conv_w_grad, conv_b_grad, step_grad, decay_grad, dstate, halo)
        for at, ref in enumerate(sums):
            ref[...] = carried[2 + at][...] if resumed else jnp.zeros_like(ref)
        ext[ROWS : ROWS + 8, :] = halo[...]
        rows_s[...] = jnp.zeros_like(rows_s)

    for ct in range(pairs + 2):
        if ct < pairs:
            u = u_in[:, ct * LANES : (ct + 1) * LANES].astype(F32)
        else:
            u = ubc_in[:, (ct - pairs) * LANES : (ct - pairs + 1) * LANES].astype(F32)
        sig = 0.5 + 0.5 * jnp.tanh(0.5 * u)
        act = u * sig
        if ct < pairs or with_bc:
            slope[:, ct * LANES : (ct + 1) * LANES] = sig + act * (1.0 - sig)
        if ct < pairs:
            xs[:, ct * LANES : (ct + 1) * LANES] = act
        else:
            bc[:, (ct - pairs) * LANES : (ct - pairs + 1) * LANES] = act

    def chunk(k, carry):
        q = ROWS // CHUNK - 1 - k
        r0 = pl.multiple_of(q * CHUNK, CHUNK)
        rsl = pl.ds(r0, CHUNK)
        raw = raw_in[rsl, :]
        row, col, step, rate, cum, same, entry, tail, keep = chunk_setup(
            raw, step_bias[...], neg_rate[...], base + r0, first_end, second_end
        )
        cum_t = cum.T
        lane_low = col < (LANES // 2)
        b_low = bc[rsl, 0:LANES].astype(BF16)
        c_f = bc[rsl, LANES : 2 * LANES]
        c_low = c_f.astype(BF16)
        allowed = same & (row <= col)
        gram = jnp.where(allowed, dot(b_low, c_low, ((1,), (1,))), 0.0)
        dstate_low = dstate[...].astype(BF16)
        bds[...] = dot(b_low, dstate_low)
        dgram = jnp.zeros((CHUNK, CHUNK), F32)
        for p in range(pairs):
            cols = slice(p * LANES, (p + 1) * LANES)
            head = 2 * (p + first_pair)
            ca, cb = lane_pair(cum, p + first_pair, lane_low)
            sa, sb = lane_pair(step, p + first_pair, lane_low)
            la = jnp.exp2(jnp.minimum(cum_t[head : head + 1, :] - ca, 0.0))
            lb = jnp.exp2(jnp.minimum(cum_t[head + 1 : head + 2, :] - cb, 0.0))
            both = jnp.where(lane_low, ca, cb)
            step_pair = jnp.where(lane_low, sa, sb)
            dy_low = dy_in[rsl, cols]
            dy = dy_low.astype(F32)
            dy2 = split_rows(dy_low, lane_low)
            xdt = xs[rsl, cols] * step_pair
            xdt_low = xdt.astype(BF16)
            mt = jnp.concatenate([(la * gram).astype(BF16), (lb * gram).astype(BF16)], axis=1)
            dmt = dot(xdt_low, dy2, ((1,), (1,)))
            dgram += dmt[:, :CHUNK] * la + dmt[:, CHUNK:] * lb
            end = both[CHUNK - 1 : CHUNK, :]
            weight = jnp.exp2(end - both) * tail
            gxs = weight * bds[:, cols]
            gx = dot(mt, dy2) + gxs
            xdt_r = xdt_low.astype(F32)
            q_s[:, cols] = xdt_r * gx
            ext[rsl, cols] = (step_pair * gx + skip[:, cols] * dy) * slope[rsl, cols]
            wx_s[:, cols] = (xdt * weight).astype(BF16)
            dye_s[:, cols] = (dy * (jnp.exp2(both) * entry)).astype(BF16)
            keep_row = jnp.exp2(end) * keep
            rows_s[8:9, cols] = keep_row
            rows_s[0:8, cols] = fold8(xdt_r * gxs) + keep_row * fold8(
                dstate[:, cols] * state_in[q, :, cols].astype(F32)
            )
        dgram = jnp.where(allowed, dgram, 0.0)
        dc = dot(dgram.T.astype(BF16), b_low) + dot(dye_s[...], state_in[q], ((1,), (1,)))
        db = dot(dgram.astype(BF16), c_low) + dot(wx_s[...], dstate_low, ((1,), (1,)))
        if with_bc:
            bsl = slice(inner, inner + LANES)
            csl = slice(inner + LANES, inner + 2 * LANES)
            ext[rsl, bsl] = (db + part_in[rsl, 0:LANES]) * slope[rsl, bsl]
            ext[rsl, csl] = (dc + part_in[rsl, LANES : 2 * LANES]) * slope[rsl, csl]
        else:
            part_out[rsl, 0:LANES] = db
            part_out[rsl, LANES : 2 * LANES] = dc
        dstate[...] = dstate[...] * rows_s[8:9, :] + dot(c_f.T.astype(BF16), dye_s[...])
        sx = head_sums(q_s[...], heads[...])
        end_term = jnp.sum(head_sums(rows_s[0:8, :], heads[...]), axis=0, keepdims=True)
        upper = (row <= col).astype(F32)
        drate = dot(upper, s1_in[rsl, :] - sx, precision=HIGH) + end_term
        own = (col >= 2 * first_pair) & (col < 2 * (first_pair + pairs))
        drate = jnp.where(own, drate, 0.0)
        dstep = sx / jnp.maximum(step, 1e-37) + neg_rate[...] * drate
        draw = dstep * jax.nn.sigmoid(raw + step_bias[...])
        if with_bc:
            draw = draw + part_in[rsl, 2 * LANES : 3 * LANES]
            dconv_out[rsl, channels : channels + LANES] = draw.astype(BF16)
            step_grad[...] += fold8(draw)
        else:
            part_out[rsl, 2 * LANES : 3 * LANES] = draw
        decay_grad[...] += fold8(drate * rate)
        return carry

    lax.fori_loop(0, ROWS // CHUNK, chunk, 0)

    pos = lax.broadcasted_iota(jnp.int32, (ROWS, LANES), 0) + base
    seg = segment_of(pos, first_end, second_end)
    shift_mask = [
        (segment_of(pos + k, first_end, second_end) == seg).astype(F32) for k in range(1, 4)
    ]
    for ct in range(channels // LANES):
        cols = slice(ct * LANES, (ct + 1) * LANES)
        du = ext[0:ROWS, cols]
        if ct < pairs:
            source = conv_in[:, cols].astype(F32)
        else:
            source = cbc_in[:, (ct - pairs) * LANES : (ct - pairs + 1) * LANES].astype(F32)
        conv_b_grad[:, cols] += fold8(du)
        conv_w_grad[24:32, cols] += fold8(source * du)
        total = conv_w[3:4, cols] * du
        for k in range(1, 4):
            later = ext[k : k + ROWS, cols] * shift_mask[k - 1]
            total += conv_w[3 - k : 4 - k, cols] * later
            conv_w_grad[8 * (3 - k) : 8 * (4 - k), cols] += fold8(source * later)
        dconv_out[:, cols] = total.astype(BF16)
    ext[ROWS : ROWS + 8, :] = ext[0:8, :]
    halo[...] = ext[0:8, :]


def out_kernel(ends, tok, gated, w_out, block_out):
    pos = lax.broadcasted_iota(jnp.int32, (TAIL, 1), 0) + pl.program_id(0) * TAIL
    live = (pos < ends[1]).astype(F32)
    block_out[...] = (tok[...].astype(F32) + live * dot(gated[...], w_out[...])).astype(BF16)


def part_kernel(dgate, rest_a, w_gate, w_conv, grad):
    grad[...] = dot(dgate[...], w_gate[...], ((1,), (1,))) + dot(rest_a[...], w_conv[...], ((1,), (1,)))


def norm_kernel(tok, cot, part, rest_b, w_conv, norm_gain, grad_tokens):
    split = w_conv.shape[1] - rest_b.shape[1]
    grad = part[...] + dot(rest_b[...], w_conv[:, split:], ((1,), (1,)))
    rows = tok[...].astype(F32)
    r = lax.rsqrt(jnp.mean(rows * rows, axis=-1, keepdims=True) + 1e-05)
    n = rows * r
    weighted = norm_gain[...] * grad
    mean = jnp.mean(weighted * n, axis=-1, keepdims=True)
    grad_tokens[...] = (r * (weighted - n * mean) + cot[...].astype(F32)).astype(BF16)


def whole(shape):
    return pl.BlockSpec(shape, lambda i: (0,) * len(shape))


def params():
    return pltpu.CompilerParams(dimension_semantics=("arbitrary",), vmem_limit_bytes=VMEM_LIMIT)


def cost(flops, moved):
    return pl.CostEstimate(flops=flops, bytes_accessed=moved, transcendentals=20_000_000)


SMEM = pl.BlockSpec(memory_space=pltpu.SMEM)


def run_scan(ends, tok, w_local, w_far, w_near, norm_gain, conv_w, conv_b, step_bias, neg_rate, inner):
    count, width = tok.shape
    channels = conv_w.shape[1]
    per = ROWS // CHUNK

    def rows_of(n):
        return pl.BlockSpec((ROWS, n), lambda i: (i, 0))

    shape = jax.ShapeDtypeStruct
    return pl.pallas_call(
        scan_kernel,
        grid=(count // ROWS,),
        in_specs=[SMEM, rows_of(width)]
        + [
            whole(v.shape)
            for v in (w_local, w_far, w_near, norm_gain, conv_w, conv_b, step_bias, neg_rate)
        ],
        out_specs=[
            rows_of(width),
            rows_of(channels),
            rows_of(channels),
            rows_of(LANES),
            rows_of(inner),
            pl.BlockSpec((per, LANES, inner), lambda i: (i, 0, 0)),
            whole((width, channels + LANES)),
        ],
        out_shape=[
            shape((count, width), BF16),
            shape((count, channels), BF16),
            shape((count, channels), BF16),
            shape((count, LANES), F32),
            shape((count, inner), F32),
            shape((count // CHUNK, LANES, inner), BF16),
            shape((width, channels + LANES), BF16),
        ],
        scratch_shapes=[
            pltpu.VMEM((ROWS + 8, channels), F32),
            pltpu.VMEM((ROWS, inner), F32),
            pltpu.VMEM((ROWS, 2 * LANES), F32),
            pltpu.VMEM((CHUNK, inner), BF16),
            pltpu.VMEM((8, inner), F32),
            pltpu.VMEM((LANES, inner), F32),
        ],
        compiler_params=params(),
        cost_estimate=cost(50_000_000_000, 50_000_000),
        name="mixer_scan",
    )(ends, tok, w_local, w_far, w_near, norm_gain, conv_w, conv_b, step_bias, neg_rate)


def run_gate(ends, cot, normed, u, y, w_local, gate_far, gate_near, out_local, out_far, out_near, skip, gate_gain, heads):
    count, width = cot.shape
    inner = y.shape[1]

    def rows_of(n):
        return pl.BlockSpec((ROWS, n), lambda i: (i, 0))

    shape = jax.ShapeDtypeStruct
    return pl.pallas_call(
        gate_kernel,
        grid=(count // ROWS,),
        in_specs=[SMEM, rows_of(width), rows_of(width), rows_of(inner), rows_of(inner)]
        + [pl.BlockSpec((w_local.shape[0], inner), lambda i: (0, 0))]
        + [
            whole(v.shape)
            for v in (gate_far, gate_near, out_local, out_far, out_near, skip, gate_gain, heads)
        ],
        out_specs=[
            whole((width, inner)),
            whole((inner, width)),
            rows_of(inner),
            rows_of(width),
            rows_of(inner),
            rows_of(inner),
            rows_of(LANES),
            whole((8, inner)),
            whole((8, inner)),
        ],
        out_shape=[
            shape((width, inner), BF16),
            shape((inner, width), BF16),
            shape((count, inner), BF16),
            shape((count, width), BF16),
            shape((count, inner), BF16),
            shape((count, inner), BF16),
            shape((count, LANES), F32),
            shape((8, inner), F32),
            shape((8, inner), F32),
        ],
        scratch_shapes=[pltpu.VMEM((ROWS, inner), F32) for _ in range(4)],
        compiler_params=params(),
        cost_estimate=cost(35_000_000_000, 50_000_000),
        name="gate_both_ways",
    )(ends, cot, normed, u, y, w_local, gate_far, gate_near, out_local, out_far, out_near, skip, gate_gain, heads)


def run_backward(first_pair, pairs, part, carried, ends, u, conv_in, raw, dy, s1, states, conv_w, step_bias, neg_rate, skip, heads):
    count, full_channels = u.shape
    full_inner = dy.shape[1]
    with_bc = part is not None
    inner = pairs * LANES
    channels = inner + (2 * LANES if with_bc else 0)
    per = ROWS // CHUNK
    steps = count // ROWS // 2
    resumed = carried is not None
    last = steps - 1 if resumed else 2 * steps - 1
    at = first_pair // pairs
    bc_at = full_inner // (2 * LANES)
    if part is None:
        part = jnp.zeros((8, LANES), F32)
        part_spec = whole(part.shape)
        part_out_shape = (count, 3 * LANES)
        width_out = channels
        own_taps = conv_w[:, first_pair * LANES : first_pair * LANES + inner]
    else:
        part_spec = pl.BlockSpec((ROWS, 3 * LANES), lambda i: (last - i, 0))
        part_out_shape = (8, LANES)
        width_out = channels + LANES
        own_taps = conv_w[:, first_pair * LANES :]

    def rows_of(n, c=0):
        return pl.BlockSpec((ROWS, n), lambda i: (last - i, c))

    shape = jax.ShapeDtypeStruct
    sums = ((32, channels), (8, channels), (8, LANES), (8, LANES), (LANES, inner), (8, channels))
    in_specs = [
        SMEM,
        rows_of(inner, at),
        rows_of(inner, at),
        rows_of(2 * LANES, bc_at),
        rows_of(2 * LANES, bc_at),
        rows_of(LANES),
        rows_of(inner, at),
        rows_of(LANES),
        pl.BlockSpec((per, LANES, inner), lambda i: (last - i, 0, at)),
        part_spec,
        whole(own_taps.shape),
        whole(step_bias.shape),
        whole(neg_rate.shape),
        pl.BlockSpec((1, inner), lambda i: (0, at)),
        pl.BlockSpec((inner, LANES), lambda i: (at, 0)),
    ]
    args = [ends, u, conv_in, u, conv_in, raw, dy, s1, states, part, own_taps, step_bias, neg_rate, skip, heads]
    aliases = {}
    if resumed:
        aliases = {len(args): 0, len(args) + 1: 1}
        args += list(carried)
        in_specs += [pl.BlockSpec(memory_space=pl.ANY)] * 2 + [whole(s) for s in sums]
    return pl.pallas_call(
        functools.partial(backward_kernel, first_pair, pairs, with_bc, last, resumed),
        grid=(steps,),
        in_specs=in_specs,
        out_specs=[
            rows_of(width_out),
            whole(part_out_shape) if with_bc else rows_of(3 * LANES),
        ]
        + [whole(s) for s in sums],
        out_shape=[shape((count, width_out), BF16), shape(part_out_shape, F32)]
        + [shape(s, F32) for s in sums],
        scratch_shapes=[
            pltpu.VMEM((ROWS + 8, channels), F32),
            pltpu.VMEM((ROWS, inner), F32),
            pltpu.VMEM((ROWS, 2 * LANES), F32),
            pltpu.VMEM((ROWS, channels), F32),
            pltpu.VMEM((CHUNK, inner), F32),
            pltpu.VMEM((CHUNK, inner), F32),
            pltpu.VMEM((CHUNK, inner), BF16),
            pltpu.VMEM((CHUNK, inner), BF16),
            pltpu.VMEM((16, inner), F32),
        ],
        input_output_aliases=aliases,
        compiler_params=params(),
        cost_estimate=cost(25_000_000_000, 20_000_000),
        name=("backward_b" if with_bc else "backward_a") + ("_low" if resumed else "_high"),
    )(*args)


def tail_rows(n):
    return pl.BlockSpec((TAIL, n), lambda i: (i, 0))


def run_out(ends, tok, gated, w_out):
    count, width = tok.shape
    return pl.pallas_call(
        out_kernel,
        grid=(count // TAIL,),
        in_specs=[SMEM, tail_rows(width), tail_rows(gated.shape[1]), whole(w_out.shape)],
        out_specs=tail_rows(width),
        out_shape=jax.ShapeDtypeStruct((count, width), BF16),
        compiler_params=params(),
        cost_estimate=cost(8_000_000_000, 15_000_000),
        name="block_out",
    )(ends, tok, gated, w_out)


def run_part(dgate, rest_a, w_gate, w_conv):
    count = dgate.shape[0]
    width = w_conv.shape[0]
    return pl.pallas_call(
        part_kernel,
        grid=(count // TAIL,),
        in_specs=[
            tail_rows(dgate.shape[1]),
            tail_rows(rest_a.shape[1]),
            whole(w_gate.shape),
            pl.BlockSpec((width, rest_a.shape[1]), lambda i: (0, 0)),
        ],
        out_specs=tail_rows(width),
        out_shape=jax.ShapeDtypeStruct((count, width), F32),
        compiler_params=params(),
        cost_estimate=cost(10_000_000_000, 20_000_000),
        name="grad_normed_part",
    )(dgate, rest_a, w_gate, w_conv)


def run_norm(tok, cot, part, rest_b, w_conv, norm_gain):
    count, width = tok.shape
    return pl.pallas_call(
        norm_kernel,
        grid=(count // TAIL,),
        in_specs=[
            tail_rows(width),
            tail_rows(width),
            tail_rows(width),
            tail_rows(rest_b.shape[1]),
            whole(w_conv.shape),
            whole(norm_gain.shape),
        ],
        out_specs=tail_rows(width),
        out_shape=jax.ShapeDtypeStruct((count, width), BF16),
        compiler_params=params(),
        cost_estimate=cost(10_000_000_000, 20_000_000),
        name="norm_backward",
    )(tok, cot, part, rest_b, w_conv, norm_gain)


def pad_lanes(v):
    return jnp.pad(v, ((0, 0), (0, LANES - v.shape[1])))


def swap(v, mask):
    n = lax.axis_size("rep") * lax.axis_size("shard")
    return lax.ppermute(v, ("rep", "shard"), [(i, i ^ mask) for i in range(n)])


def place():
    return lax.axis_index("rep") * lax.axis_size("shard") + lax.axis_index("shard")


SHARD, CORE = 1, 2


def half_rows(v):
    half = v.shape[0] // 2
    core = (place() // CORE) % 2
    return lax.dynamic_slice_in_dim(v, core * half, half, 0)


def take(v, index):
    return lax.dynamic_index_in_dim(v, index, 0, keepdims=False)


def exchanges():
    n = lax.axis_size("rep") * lax.axis_size("shard")
    bits = [SHARD]
    bit = 2 * CORE
    while bit < n:
        bits.append(bit)
        bit *= 2
    return bits


def at_bit(bit):
    return (place() // bit) % 2


def cut(v, bit):
    if v.ndim == 2:
        v = v.reshape(2, v.shape[0] // 2, v.shape[1])
    me = at_bit(bit)
    return take(v, me), take(v, 1 - me).astype(BF16)


def add(kept, got):
    return kept + got.astype(F32)


def both_sum(low, bit):
    return (low.astype(F32) + swap(low, bit).astype(F32)).astype(BF16)


def join(low, got, bit):
    return jnp.where(at_bit(bit) == 0, jnp.concatenate([low, got], 0), jnp.concatenate([got, low], 0))


def core_sum(g):
    rows, n = g.shape
    v = g.reshape(2, 2, rows // 4, n)
    core = (place() // CORE) % 2
    other = lax.dynamic_index_in_dim(v, 1 - core, 1, keepdims=False).astype(BF16)
    kept = lax.dynamic_index_in_dim(v, core, 1, keepdims=False)
    return kept + swap(other, CORE).astype(F32)


def after(gate, *values):
    return lax.optimization_barrier((gate, *values))


def per_device(
    tokens,
    cotangent,
    seq_lengths,
    seq_device,
    norm_gain,
    in_weight,
    conv_weight,
    conv_bias,
    step_bias,
    decay_log,
    skip_gain,
    gate_gain,
    out_weight,
):
    shards = lax.axis_size("shard")
    shard = lax.axis_index("shard")
    device = lax.axis_index("rep") * shards + shard
    half_count = seq_lengths.shape[0] // 2
    owned = seq_device[:half_count] == device
    first_len = jnp.sum(jnp.where(owned, seq_lengths[:half_count], 0))
    second_len = jnp.sum(jnp.where(owned, seq_lengths[half_count:], 0))
    ends = jnp.stack(
        [first_len, first_len + second_len, lax.axis_index("rep") % 2, shard]
    ).astype(jnp.int32)
    count, width = tokens.shape
    inner = gate_gain.shape[0] * shards
    channels = conv_weight.shape[1] * shards
    head_count = step_bias.shape[0] * shards
    size = inner // head_count
    taps = conv_weight.shape[0]

    small = (norm_gain, conv_weight.reshape(-1), conv_bias, step_bias, decay_log, skip_gain, gate_gain)
    sizes = [v.shape[0] for v in small]
    own = jnp.concatenate(small)
    own = jnp.pad(own, (0, -own.shape[0] % 1024)).reshape(-1, LANES)
    in_half = half_rows(in_weight)
    conv_far = swap(in_half[:, inner:], SHARD)
    other = swap(own, SHARD)
    conv_near = swap(conv_far, CORE)
    conv_near, gate_send, out_send = after(conv_near, in_half[:, :inner], half_rows(out_weight))
    gate_far = swap(gate_send, SHARD)
    out_far = swap(out_send, SHARD)

    packed = jnp.where(shard == 0, jnp.stack([own, other]), jnp.stack([other, own])).reshape(2, -1)
    parts = []
    at = 0
    for n in sizes:
        parts.append(packed[:, at : at + n])
        at += n
    full_norm, _, full_shift, full_step, full_decay, full_skip, full_gate = [
        p.reshape(-1).astype(F32) for p in parts
    ]
    conv_w = parts[1].reshape(shards, taps, -1).transpose(1, 0, 2).reshape(taps, -1).astype(F32)
    conv_b = full_shift[None, :]
    norm_row = full_norm[None, :]
    gate_row = full_gate[None, :]
    lane_head = lax.broadcasted_iota(jnp.int32, (inner, LANES), 0) // size
    heads = (lane_head == lax.broadcasted_iota(jnp.int32, (inner, LANES), 1)).astype(BF16)
    skip = jnp.repeat(full_skip, size)[None, :]
    step_row = pad_lanes(full_step[None, :])
    neg_rate = pad_lanes(-jnp.exp(full_decay)[None, :])

    normed, u, conv_in, raw, y, states, w_conv = run_scan(
        ends, tokens, in_weight, conv_far, conv_near, norm_row, conv_w, conv_b, step_row, neg_rate, inner
    )
    normed, gate_far, out_far = after(normed, gate_far, out_far)
    gate_near = swap(gate_far, CORE)
    out_near = swap(out_far, CORE)
    w_gate, w_out, gated, masked, dy, dgate, s1, gain8, skip8 = run_gate(
        ends, cotangent, normed, u, y, in_weight, gate_far, gate_near, out_weight, out_far, out_near, skip, gate_row, heads
    )
    bits = exchanges()
    far, last_bit = bits[1:-1], bits[-1]
    g_out = dot(gated, masked, ((0,), (0,)))
    h_out = core_sum(g_out)
    g_out, normed = after(g_out, normed)
    g_gate = dot(normed, dgate, ((0,), (0,)))
    h_gate = core_sum(g_gate)
    quarter = h_out.shape[1] // 2
    held = jnp.concatenate([h_out[:, :quarter], h_out[:, quarter:], h_gate], axis=2)
    half_pairs = inner // LANES // 2
    shared = (s1, states, conv_w, step_row, neg_rate, skip, heads)

    kept, sent = cut(held, SHARD)
    dy, sent = after(dy, sent)
    got = swap(sent, SHARD)
    carry = run_backward(0, half_pairs, None, None, ends, u, conv_in, raw, dy, *shared)
    first_out, kept, got = after(carry[0], kept, got)
    kept, sent = cut(add(kept, got), far[0])
    dy, sent = after(dy, sent)
    got = swap(sent, far[0])
    rest_a, part, cw_a, cb_a, _, dl_a, _, _ = run_backward(
        0, half_pairs, None, (first_out, *carry[1:]), ends, u, conv_in, raw, dy, *shared
    )
    rest_a, kept, got = after(rest_a, kept, got)
    g_a = dot(normed, rest_a, ((0,), (0,)))
    held = add(kept, got)
    kept, sent = cut(held, far[1])
    kept_a, sent_a = cut(core_sum(g_a), SHARD)
    part, sent, sent_a = after(part, sent, sent_a)
    got = swap(sent, far[1])
    got_a = swap(sent_a, SHARD)
    carry = run_backward(half_pairs, half_pairs, part, None, ends, u, conv_in, raw, dy, *shared)
    first_out, kept, got, kept_a, got_a = after(carry[0], kept, got, kept_a, got_a)
    held = add(kept, got)
    for bit in far[2:]:
        kept, sent = cut(held, bit)
        held = add(kept, swap(sent, bit))
    low = held.astype(BF16)
    kept_a, sent_a = cut(add(kept_a, got_a), far[0])
    part, low, sent_a = after(part, low, sent_a)
    got = swap(low, last_bit)
    got_a = swap(sent_a, far[0])
    rest_b, _, cw_b, cb_b, sb_b, dl_b, _, _ = run_backward(
        half_pairs, half_pairs, part, (first_out, *carry[1:]), ends, u, conv_in, raw, dy, *shared
    )
    rest_b, low, got, kept_a, got_a = after(rest_b, low, got, kept_a, got_a)
    g_b = dot(normed, rest_b, ((0,), (0,)))

    split = channels - half_pairs * LANES
    g_conv = jnp.sum(jnp.concatenate([cw_a, cw_b], 1).reshape(taps, 8, channels), axis=1)
    g_shift = jnp.sum(jnp.concatenate([cb_a, cb_b], 1), axis=0)
    g_step = jnp.sum(sb_b, axis=0)[:head_count]
    g_decay = jnp.sum(dl_a + dl_b, axis=0)[:head_count]
    g_skip = jnp.sum(skip8.reshape(8, head_count, size), axis=(0, 2))
    g_gain = jnp.sum(gain8, axis=0)
    pieces = (
        g_conv.reshape(taps, shards, -1).transpose(1, 0, 2).reshape(shards, -1),
        g_shift.reshape(shards, -1),
        g_step.reshape(shards, -1),
        g_decay.reshape(shards, -1),
        g_skip.reshape(shards, -1),
        g_gain.reshape(shards, -1),
    )
    flat = jnp.concatenate(pieces, axis=1)
    own_rows = width // shards
    extra = -(-flat.shape[1] // own_rows)
    flat = jnp.pad(flat, ((0, 0), (0, extra * own_rows - flat.shape[1])))
    flat = flat.reshape(width, extra)
    g_b = jnp.concatenate([g_b[:, : split + head_count], flat], axis=1)
    low = add(low.astype(F32), got).astype(BF16)
    held_a = add(kept_a, got_a)
    kept_b, sent_b = cut(core_sum(g_b), SHARD)
    backs = far[::-1] + [CORE]
    gated, low, sent_b = after(gated, low, sent_b)
    got = swap(low, backs[0])
    got_b = swap(sent_b, SHARD)
    block_out = run_out(ends, tokens, gated, w_out)
    block_out, low, got, kept_b, got_b = after(block_out, low, got, kept_b, got_b)
    low = join(low, got, backs[0])
    kept_b, sent_b = cut(add(kept_b, got_b), far[0])
    dgate, low, sent_b = after(dgate, low, sent_b)
    got = swap(low, backs[1])
    got_b = swap(sent_b, far[0])
    grad_part = run_part(dgate, rest_a, w_gate, w_conv)
    grad_part, low, got, kept_b, got_b = after(grad_part, low, got, kept_b, got_b)
    low = join(low, got, backs[1])
    held_b = jnp.concatenate([held_a, add(kept_b, got_b)], axis=1)
    kept_b, sent_b = cut(held_b, far[1])
    grad_part, low, sent_b = after(grad_part, low, sent_b)
    got = swap(low, backs[2])
    got_b = swap(sent_b, far[1])
    grad_tokens = run_norm(tokens, cotangent, grad_part, rest_b, w_conv, norm_row)
    grad_tokens, low, got, kept_b, got_b = after(grad_tokens, low, got, kept_b, got_b)
    low = join(low, got, backs[2])
    for bit in backs[3:]:
        low = join(low, swap(low, bit), bit)
    held_b = add(kept_b, got_b)
    for bit in far[2:]:
        kept_b, sent_b = cut(held_b, bit)
        held_b = add(kept_b, swap(sent_b, bit))
    low_b = both_sum(held_b.astype(BF16), last_bit)
    for bit in backs:
        low_b = join(low_b, swap(low_b, bit), bit)
    near = out_weight.shape[1]
    by_core = low.reshape(2, low.shape[0] // 2, low.shape[1])
    t_out = jnp.concatenate(
        [by_core[0, :, :near], by_core[0, :, near : 2 * near], by_core[1, :, :near], by_core[1, :, near : 2 * near]], axis=0
    )
    t_b = low_b[:, half_pairs * LANES :]
    t_in = jnp.concatenate(
        [low[:, 2 * near :], low_b[:, : half_pairs * LANES + split + head_count]], axis=1
    ).astype(F32)
    t_norm = jnp.sum(t_in * in_weight.astype(F32), axis=1) / norm_gain.astype(F32)
    mine = t_b[:, split + head_count :].reshape(-1).astype(F32)
    outs = []
    at = 0
    for n in sizes[1:]:
        outs.append(mine[at : at + n])
        at += n
    return (
        block_out,
        grad_tokens,
        t_norm,
        t_in,
        outs[0].reshape(taps, -1),
        outs[1],
        outs[2],
        outs[3],
        outs[4],
        outs[5],
        t_out.astype(F32),
    )


def solution(mesh):
    in_specs = (
        P(("rep", "shard"), None),
        P(("rep", "shard"), None),
        P(),
        P(),
        P("shard"),
        P("shard", None),
        P(None, "shard"),
        P("shard"),
        P("shard"),
        P("shard"),
        P("shard"),
        P("shard"),
        P("shard", None),
    )
    out_specs = (
        P(("rep", "shard"), None),
        P(("rep", "shard"), None),
        P("shard"),
        P("shard", None),
        P(None, "shard"),
        P("shard"),
        P("shard"),
        P("shard"),
        P("shard"),
        P("shard"),
        P("shard", None),
    )
    return jax.shard_map(
        per_device, mesh=mesh, in_specs=in_specs, out_specs=out_specs, check_vma=False
    )
```

```python
import functools

import jax
import jax.numpy as jnp
from jax import lax
from jax.experimental import pallas as pl
from jax.experimental.pallas import tpu as pltpu
from jax.sharding import PartitionSpec as P

ROWS = 256
CHUNK = 128
TAIL = 512
LANES = 128
LOG2E = 1.4426950408889634
F32 = jnp.float32
BF16 = jnp.bfloat16
HIGH = lax.Precision.HIGHEST
VMEM_LIMIT = 32 * 1024 * 1024


def dot(a, b, dims=((1,), (0,)), precision=None):
    return lax.dot_general(a, b, (dims, ((), ())), precision=precision, preferred_element_type=F32)


def fold8(v):
    return jnp.sum(v.reshape(v.shape[0] // 8, 8, v.shape[1]), axis=0)


def segment_of(position, first_end, second_end):
    return (position >= first_end).astype(jnp.int32) + (position >= second_end).astype(jnp.int32)


def softplus(v):
    return jnp.maximum(v, 0.0) + jnp.log1p(jnp.exp(-jnp.abs(v)))


def head_sums(v, heads):
    high = v.astype(BF16)
    low = (v - high.astype(F32)).astype(BF16)
    return dot(high, heads) + dot(low, heads)


def lane_pair(v, p, lane_low):
    shape = lane_low.shape
    a = jnp.broadcast_to(v[:, 2 * p : 2 * p + 1], shape)
    b = jnp.broadcast_to(v[:, 2 * p + 1 : 2 * p + 2], shape)
    return a, b


def split_rows(pair, lane_low):
    zero = jnp.zeros_like(pair)
    return jnp.concatenate(
        [jnp.where(lane_low, pair, zero), jnp.where(lane_low, zero, pair)], axis=0
    )


def chunk_setup(raw, step_bias, neg_rate, start, first_end, second_end):
    row = lax.broadcasted_iota(jnp.int32, (CHUNK, LANES), 0)
    col = lax.broadcasted_iota(jnp.int32, (CHUNK, LANES), 1)
    step = softplus(raw + step_bias)
    rate = neg_rate * step
    lower = (row >= col).astype(F32)
    cum = dot(lower, rate, precision=HIGH) * LOG2E
    seg_row = segment_of(row + start, first_end, second_end)
    seg_col = segment_of(col + start, first_end, second_end)
    last_seg = segment_of(start - 1, first_end, second_end)
    end_seg = segment_of(start + CHUNK - 1, first_end, second_end)
    entry = (seg_row == last_seg).astype(F32)
    tail = (seg_row == end_seg).astype(F32)
    keep = (last_seg == end_seg).astype(F32)
    same = seg_row == seg_col
    return row, col, step, rate, cum, same, entry, tail, keep


def place_rows(dst, width, local, far, near, core, shard):
    half = far.shape[0]
    own_at = pl.multiple_of(shard * (2 * half), half)
    other_at = (1 - shard) * (2 * half)
    dst[pl.ds(own_at, 2 * half), :width] = local
    dst[pl.ds(pl.multiple_of(other_at + core * half, half), half), :width] = far[...]
    dst[pl.ds(pl.multiple_of(other_at + (1 - core) * half, half), half), :width] = near[...]


def scan_kernel(
    ends,
    tok,
    w_local,
    w_far,
    w_near,
    norm_gain,
    conv_w,
    conv_b,
    step_bias,
    neg_rate,
    normed_out,
    u_out,
    conv_in_out,
    raw_out,
    y_out,
    state_out,
    w_conv,
    ext,
    xs,
    bc,
    wx_s,
    keep_s,
    state,
):
    step_id = pl.program_id(0)
    first_end = ends[0]
    second_end = ends[1]
    inner = xs.shape[1]
    channels = ext.shape[0] * LANES
    pairs = inner // LANES
    base = step_id * ROWS

    @pl.when(step_id == 0)
    def _():
        w_conv[:, channels:] = jnp.zeros((w_conv.shape[0], LANES), BF16)
        used = w_far.shape[1]
        place_rows(w_conv, used, w_local[:, inner:], w_far, w_near, ends[2], ends[3])
        ext[:, 0:8, :] = jnp.zeros((channels // LANES, 8, LANES), F32)
        state[...] = jnp.zeros_like(state)

    rows = tok[...].astype(F32)
    scale = lax.rsqrt(jnp.mean(rows * rows, axis=-1, keepdims=True) + 1e-05)
    normed = (rows * scale * norm_gain[...]).astype(BF16)
    normed_out[...] = normed
    raw_out[...] = dot(normed, w_conv[:, channels:])

    pos = lax.broadcasted_iota(jnp.int32, (ROWS, LANES), 0) + base
    seg = segment_of(pos, first_end, second_end)
    shift_mask = [
        ((segment_of(pos - k, first_end, second_end) == seg) & (pos >= k)).astype(F32)
        for k in range(1, 4)
    ]

    def conv_tile(ct):
        cols = slice(ct * LANES, (ct + 1) * LANES)
        if ct % 2 == 0:
            wide = slice(ct * LANES, (ct + 2) * LANES)
            conv_in = dot(normed, w_conv[:, wide])
            ext[ct, 8 : 8 + ROWS, :] = conv_in[:, :LANES]
            ext[ct + 1, 8 : 8 + ROWS, :] = conv_in[:, LANES:]
            conv_in_out[:, wide] = conv_in.astype(BF16)
        total = conv_b[:, cols] + conv_w[3:4, cols] * ext[ct, 8 : 8 + ROWS, :]
        for k in range(1, 4):
            total += (conv_w[3 - k : 4 - k, cols] * ext[ct, 8 - k : 8 - k + ROWS, :]) * shift_mask[k - 1]
        u = total.astype(BF16)
        u_out[:, cols] = u
        half = 0.5 * u.astype(F32)
        return half + half * jnp.tanh(half)

    for ct in range(pairs):
        xs[:, ct * LANES : (ct + 1) * LANES] = conv_tile(ct)
    for ct in range(pairs, channels // LANES):
        bc[:, (ct - pairs) * LANES : (ct - pairs + 1) * LANES] = conv_tile(ct)
    ext[:, 0:8, :] = ext[:, ROWS : ROWS + 8, :]

    def chunk(q, carry):
        r0 = pl.multiple_of(q * CHUNK, CHUNK)
        rsl = pl.ds(r0, CHUNK)
        row, col, step, rate, cum, same, entry, tail, keep = chunk_setup(
            raw_out[rsl, :], step_bias[...], neg_rate[...], base + r0, first_end, second_end
        )
        cum_t = cum.T
        shift_t = cum_t - jnp.log2(step.T)
        tail_t = (segment_of(col + (base + r0), first_end, second_end) == segment_of(base + r0 + CHUNK - 1, first_end, second_end)).astype(F32)
        weight_t = jnp.exp2(cum_t[:, CHUNK - 1 : CHUNK] - shift_t) * tail_t
        lane_low = col < (LANES // 2)
        b_f = bc[rsl, 0:LANES]
        b_t = b_f.T
        b_low = b_f.astype(BF16)
        c_low = bc[rsl, LANES : 2 * LANES].astype(BF16)
        gram = dot(c_low, b_low, ((1,), (1,)))
        gram = jnp.where(same & (row >= col), gram, 0.0)
        state_low = state[...].astype(BF16)
        state_out[q] = state_low
        y_out[rsl, :] = dot(c_low, state_low)
        for p in range(pairs):
            cols = slice(p * LANES, (p + 1) * LANES)
            ca, cb = lane_pair(cum, p, lane_low)
            ma = (jnp.exp2(jnp.minimum(ca - shift_t[2 * p : 2 * p + 1, :], 100.0)) * gram).astype(BF16)
            mb = (jnp.exp2(jnp.minimum(cb - shift_t[2 * p + 1 : 2 * p + 2, :], 100.0)) * gram).astype(BF16)
            ba = (b_t * weight_t[2 * p : 2 * p + 1, :]).astype(BF16)
            bb = (b_t * weight_t[2 * p + 1 : 2 * p + 2, :]).astype(BF16)
            x2 = split_rows(xs[rsl, cols].astype(BF16), lane_low)
            left = jnp.concatenate(
                [jnp.concatenate([ma, mb], axis=1), jnp.concatenate([ba, bb], axis=1)], axis=0
            )
            both_out = dot(left, x2)
            decay = jnp.exp2(jnp.where(lane_low, ca, cb))
            y_out[rsl, cols] = both_out[:CHUNK] + y_out[rsl, cols] * (decay * entry)
            state[:, cols] = state[:, cols] * (decay[CHUNK - 1 : CHUNK, :] * keep) + both_out[CHUNK:]
        return carry

    for at in range(ROWS // CHUNK):
        chunk(at, 0)


def gate_kernel(
    ends,
    cot,
    normed,
    u_in,
    y_in,
    w_local,
    gate_far,
    gate_near,
    out_local,
    out_far,
    out_near,
    skip,
    gate_gain,
    heads,
    w_gate,
    w_out,
    gated_out,
    masked_out,
    dy_out,
    dgate_out,
    s1_out,
    gain_grad,
    skip_grad,
    gate_s,
    xs,
    prod_s,
    dg_s,
):
    step_id = pl.program_id(0)
    second_end = ends[1]
    inner = gate_s.shape[1]
    pairs = inner // LANES
    base = step_id * ROWS

    @pl.when(step_id == 0)
    def _():
        place_rows(w_gate, inner, w_local[...], gate_far, gate_near, ends[2], ends[3])
        place_rows(w_out, w_out.shape[1], out_local[...], out_far, out_near, ends[2], ends[3])
        gain_grad[...] = jnp.zeros_like(gain_grad)
        skip_grad[...] = jnp.zeros_like(skip_grad)

    pos = lax.broadcasted_iota(jnp.int32, (ROWS, LANES), 0) + base
    live = (pos < second_end).astype(F32)
    masked = (cot[...].astype(F32) * live[:, 0:1]).astype(BF16)
    masked_out[...] = masked
    sq = jnp.zeros((ROWS, LANES), F32)
    cross = jnp.zeros((ROWS, LANES), F32)
    for ct in range(pairs):
        cols = slice(ct * LANES, (ct + 1) * LANES)
        if ct % 2 == 0:
            wide = slice(ct * LANES, (ct + 2) * LANES)
            gate_s[:, wide] = dot(normed[...], w_gate[:, wide])
            dg_s[:, wide] = dot(masked, w_out[wide, :], ((1,), (1,)))
        half = 0.5 * gate_s[:, cols]
        half_u = 0.5 * u_in[:, cols].astype(F32)
        x = half_u + half_u * jnp.tanh(half_u)
        xs[:, cols] = x
        product = (y_in[:, cols] + skip[:, cols] * x) * (half + half * jnp.tanh(half))
        prod_s[:, cols] = product
        sq += product * product
        cross += dg_s[:, cols] * gate_gain[:, cols] * product
    r = lax.rsqrt(jnp.sum(sq, axis=1, keepdims=True) / inner + 1e-05)
    m = jnp.sum(cross, axis=1, keepdims=True) / inner
    r_wide = jnp.broadcast_to(r, (ROWS, LANES))
    m_wide = jnp.broadcast_to(r * r * r * m, (ROWS, LANES))
    for ct in range(pairs):
        cols = slice(ct * LANES, (ct + 1) * LANES)
        g = gate_s[:, cols]
        sig = 0.5 + 0.5 * jnp.tanh(0.5 * g)
        act = g * sig
        x = xs[:, cols]
        y = y_in[:, cols]
        product = prod_s[:, cols]
        pr = product * r_wide
        gated_out[:, cols] = (pr * gate_gain[:, cols]).astype(BF16)
        dg = dg_s[:, cols]
        gain_grad[:, cols] += fold8(dg * pr)
        dprod = r_wide * (dg * gate_gain[:, cols]) - product * m_wide
        dsc = dprod * act
        dgate_out[:, cols] = (
            dprod * (y + skip[:, cols] * x) * (sig + act * (1.0 - sig))
        ).astype(BF16)
        dy = dsc.astype(BF16)
        dy_out[:, cols] = dy
        skip_grad[:, cols] += fold8(dsc * x)
        prod_s[:, cols] = dy.astype(F32) * y
    s1_out[...] = head_sums(prod_s[...], heads[...])


def backward_kernel(
    first_pair,
    pairs,
    with_bc,
    last,
    resumed,
    ends,
    u_in,
    conv_in,
    ubc_in,
    cbc_in,
    raw_in,
    dy_in,
    s1_in,
    state_in,
    part_in,
    conv_w,
    step_bias,
    neg_rate,
    skip,
    heads,
    *refs,
):
    carried = refs[:8] if resumed else None
    refs = refs[8:] if resumed else refs
    (
        dconv_out,
        part_out,
        conv_w_grad,
        conv_b_grad,
        step_grad,
        decay_grad,
        dstate,
        halo,
        ext,
        xs,
        bc,
        slope,
        bds,
        q_s,
        wx_s,
        rows_s,
    ) = refs
    step_id = pl.program_id(0)
    first_end = ends[0]
    second_end = ends[1]
    inner = pairs * LANES
    channels = ext.shape[0] * LANES
    base = (last - step_id) * ROWS

    @pl.when(step_id == 0)
    def _():
        sums = (conv_w_grad, conv_b_grad, step_grad, decay_grad, dstate, halo)
        for at, ref in enumerate(sums):
            ref[...] = carried[2 + at][...] if resumed else jnp.zeros_like(ref)
        for ct in range(channels // LANES):
            ext[ct, ROWS : ROWS + 8, :] = halo[:, ct * LANES : (ct + 1) * LANES]
        rows_s[...] = jnp.zeros_like(rows_s)

    for ct in range(pairs + 2):
        if ct < pairs:
            u = u_in[:, ct * LANES : (ct + 1) * LANES].astype(F32)
        else:
            u = ubc_in[:, (ct - pairs) * LANES : (ct - pairs + 1) * LANES].astype(F32)
        sig = 0.5 + 0.5 * jnp.tanh(0.5 * u)
        act = u * sig
        if ct < pairs or with_bc:
            slope[:, ct * LANES : (ct + 1) * LANES] = sig + act * (1.0 - sig)
        if ct < pairs:
            xs[:, ct * LANES : (ct + 1) * LANES] = act.astype(BF16)
        else:
            bc[:, (ct - pairs) * LANES : (ct - pairs + 1) * LANES] = act

    def chunk(k, carry):
        q = ROWS // CHUNK - 1 - k
        r0 = pl.multiple_of(q * CHUNK, CHUNK)
        rsl = pl.ds(r0, CHUNK)
        raw = raw_in[rsl, :]
        row, col, step, rate, cum, same, entry, tail, keep = chunk_setup(
            raw, step_bias[...], neg_rate[...], base + r0, first_end, second_end
        )
        cum_t = cum.T
        shift = cum - jnp.log2(step)
        last_seg = segment_of(base + r0 - 1, first_end, second_end)
        entry_t = (segment_of(col + (base + r0), first_end, second_end) == last_seg).astype(F32)
        enter_t = jnp.exp2(cum_t) * entry_t
        lane_low = col < (LANES // 2)
        b_f = bc[rsl, 0:LANES]
        b_low = b_f.astype(BF16)
        c_f = bc[rsl, LANES : 2 * LANES]
        c_low = c_f.astype(BF16)
        c_t = c_f.T
        allowed = same & (row <= col)
        gram = jnp.where(allowed, dot(b_low, c_low, ((1,), (1,))), 0.0)
        dstate_low = dstate[...].astype(BF16)
        bds[...] = dot(b_low, dstate_low)
        dgram = jnp.zeros((CHUNK, CHUNK), F32)
        dc_t = jnp.zeros((LANES, CHUNK), F32)
        for p in range(pairs):
            cols = slice(p * LANES, (p + 1) * LANES)
            head = 2 * (p + first_pair)
            ca, cb = lane_pair(shift, p + first_pair, lane_low)
            la = jnp.exp2(jnp.minimum(cum_t[head : head + 1, :] - ca, 100.0))
            lb = jnp.exp2(jnp.minimum(cum_t[head + 1 : head + 2, :] - cb, 100.0))
            both = jnp.where(lane_low, ca, cb)
            ea, eb = lane_pair(cum[CHUNK - 1 : CHUNK, :], p + first_pair, lane_low[0:1, :])
            end = jnp.where(lane_low[0:1, :], ea, eb)
            dy_low = dy_in[rsl, cols]
            dy = dy_low.astype(F32)
            dy2 = split_rows(dy_low, lane_low)
            x_low = xs[rsl, cols]
            state_low = state_in[q, :, cols]
            top = dot(jnp.concatenate([x_low, state_low], axis=0), dy2, ((1,), (1,)))
            enter_a = enter_t[head : head + 1, :]
            enter_b = enter_t[head + 1 : head + 2, :]
            dgram += top[:CHUNK, :CHUNK] * la + top[:CHUNK, CHUNK:] * lb
            dc_t += top[CHUNK:, :CHUNK] * enter_a + top[CHUNK:, CHUNK:] * enter_b
            left = jnp.concatenate(
                [
                    jnp.concatenate([(la * gram).astype(BF16), (lb * gram).astype(BF16)], axis=1),
                    jnp.concatenate([(c_t * enter_a).astype(BF16), (c_t * enter_b).astype(BF16)], axis=1),
                ],
                axis=0,
            )
            down = dot(left, dy2)
            weight = jnp.exp2(end - both) * tail
            gxs = weight * bds[:, cols]
            gx = down[:CHUNK] + gxs
            x = x_low.astype(F32)
            q_s[:, cols] = x * gx
            ext[p, rsl, :] = (gx + skip[:, cols] * dy) * slope[rsl, cols]
            wx_s[:, cols] = (x * weight).astype(BF16)
            keep_row = jnp.exp2(end) * keep
            old = dstate[:, cols]
            rows_s[0:8, cols] = fold8(x * gxs) + keep_row * fold8(old * state_low.astype(F32))
            dstate[:, cols] = old * keep_row + down[CHUNK:]
        dgram = jnp.where(allowed, dgram, 0.0)
        dc = (dc_t + dot(b_f.T.astype(BF16), dgram.astype(BF16))).T
        db = dot(dgram.astype(BF16), c_low) + dot(wx_s[...], dstate_low, ((1,), (1,)))
        if with_bc:
            bsl = slice(inner, inner + LANES)
            csl = slice(inner + LANES, inner + 2 * LANES)
            ext[pairs, rsl, :] = (db + part_in[rsl, 0:LANES]) * slope[rsl, bsl]
            ext[pairs + 1, rsl, :] = (dc + part_in[rsl, LANES : 2 * LANES]) * slope[rsl, csl]
        else:
            part_out[rsl, 0:LANES] = db
            part_out[rsl, LANES : 2 * LANES] = dc
        sx = head_sums(q_s[...], heads[...])
        end_term = jnp.sum(head_sums(rows_s[0:8, :], heads[...]), axis=0, keepdims=True)
        upper = (row <= col).astype(F32)
        drate = dot(upper, s1_in[rsl, :] - sx, precision=HIGH) + end_term
        own = (col >= 2 * first_pair) & (col < 2 * (first_pair + pairs))
        drate = jnp.where(own, drate, 0.0)
        dstep = sx / jnp.maximum(step, 1e-37) + neg_rate[...] * drate
        draw = dstep * jax.nn.sigmoid(raw + step_bias[...])
        if with_bc:
            draw = draw + part_in[rsl, 2 * LANES : 3 * LANES]
            dconv_out[rsl, channels : channels + LANES] = draw.astype(BF16)
            step_grad[...] += fold8(draw)
        else:
            part_out[rsl, 2 * LANES : 3 * LANES] = draw
        decay_grad[...] += fold8(drate * rate)
        return carry

    for at in range(ROWS // CHUNK):
        chunk(at, 0)

    pos = lax.broadcasted_iota(jnp.int32, (ROWS, LANES), 0) + base
    seg = segment_of(pos, first_end, second_end)
    shift_mask = [
        (segment_of(pos + k, first_end, second_end) == seg).astype(F32) for k in range(1, 4)
    ]
    for ct in range(channels // LANES):
        cols = slice(ct * LANES, (ct + 1) * LANES)
        du = ext[ct, 0:ROWS, :]
        if ct < pairs:
            source = conv_in[:, cols].astype(F32)
        else:
            source = cbc_in[:, (ct - pairs) * LANES : (ct - pairs + 1) * LANES].astype(F32)
        conv_b_grad[:, cols] += fold8(du)
        conv_w_grad[24:32, cols] += fold8(source * du)
        total = conv_w[3:4, cols] * du
        for k in range(1, 4):
            later = ext[ct, k : k + ROWS, :] * shift_mask[k - 1]
            total += conv_w[3 - k : 4 - k, cols] * later
            conv_w_grad[8 * (3 - k) : 8 * (4 - k), cols] += fold8(source * later)
        dconv_out[:, cols] = total.astype(BF16)
    for ct in range(channels // LANES):
        first = ext[ct, 0:8, :]
        ext[ct, ROWS : ROWS + 8, :] = first
        halo[:, ct * LANES : (ct + 1) * LANES] = first


def out_kernel(ends, tok, gated, w_out, block_out):
    pos = lax.broadcasted_iota(jnp.int32, (TAIL, 1), 0) + pl.program_id(0) * TAIL
    live = (pos < ends[1]).astype(F32)
    block_out[...] = (tok[...].astype(F32) + live * dot(gated[...], w_out[...])).astype(BF16)


def part_kernel(dgate, rest_a, w_gate, w_conv, grad):
    grad[...] = dot(dgate[...], w_gate[...], ((1,), (1,))) + dot(rest_a[...], w_conv[...], ((1,), (1,)))


def norm_kernel(tok, cot, part, rest_b, w_conv, norm_gain, grad_tokens):
    split = w_conv.shape[1] - rest_b.shape[1]
    grad = part[...] + dot(rest_b[...], w_conv[:, split:], ((1,), (1,)))
    rows = tok[...].astype(F32)
    r = lax.rsqrt(jnp.mean(rows * rows, axis=-1, keepdims=True) + 1e-05)
    n = rows * r
    weighted = norm_gain[...] * grad
    mean = jnp.mean(weighted * n, axis=-1, keepdims=True)
    grad_tokens[...] = (r * (weighted - n * mean) + cot[...].astype(F32)).astype(BF16)


def whole(shape):
    return pl.BlockSpec(shape, lambda i: (0,) * len(shape))


def params():
    return pltpu.CompilerParams(dimension_semantics=("arbitrary",), vmem_limit_bytes=VMEM_LIMIT)


def cost(flops, moved):
    return pl.CostEstimate(flops=flops, bytes_accessed=moved, transcendentals=20_000_000)


SMEM = pl.BlockSpec(memory_space=pltpu.SMEM)


def run_scan(ends, tok, w_local, w_far, w_near, norm_gain, conv_w, conv_b, step_bias, neg_rate, inner):
    count, width = tok.shape
    channels = conv_w.shape[1]
    per = ROWS // CHUNK

    def rows_of(n):
        return pl.BlockSpec((ROWS, n), lambda i: (i, 0))

    shape = jax.ShapeDtypeStruct
    return pl.pallas_call(
        scan_kernel,
        grid=(count // ROWS,),
        in_specs=[SMEM, rows_of(width)]
        + [
            whole(v.shape)
            for v in (w_local, w_far, w_near, norm_gain, conv_w, conv_b, step_bias, neg_rate)
        ],
        out_specs=[
            rows_of(width),
            rows_of(channels),
            rows_of(channels),
            rows_of(LANES),
            rows_of(inner),
            pl.BlockSpec((per, LANES, inner), lambda i: (i, 0, 0)),
            whole((width, channels + LANES)),
        ],
        out_shape=[
            shape((count, width), BF16),
            shape((count, channels), BF16),
            shape((count, channels), BF16),
            shape((count, LANES), F32),
            shape((count, inner), F32),
            shape((count // CHUNK, LANES, inner), BF16),
            shape((width, channels + LANES), BF16),
        ],
        scratch_shapes=[
            pltpu.VMEM((channels // LANES, ROWS + 8, LANES), F32),
            pltpu.VMEM((ROWS, inner), F32),
            pltpu.VMEM((ROWS, 2 * LANES), F32),
            pltpu.VMEM((CHUNK, inner), BF16),
            pltpu.VMEM((8, inner), F32),
            pltpu.VMEM((LANES, inner), F32),
        ],
        compiler_params=params(),
        cost_estimate=cost(50_000_000_000, 50_000_000),
        name="mixer_scan",
    )(ends, tok, w_local, w_far, w_near, norm_gain, conv_w, conv_b, step_bias, neg_rate)


def run_gate(ends, cot, normed, u, y, w_local, gate_far, gate_near, out_local, out_far, out_near, skip, gate_gain, heads):
    count, width = cot.shape
    inner = y.shape[1]

    def rows_of(n):
        return pl.BlockSpec((ROWS, n), lambda i: (i, 0))

    shape = jax.ShapeDtypeStruct
    return pl.pallas_call(
        gate_kernel,
        grid=(count // ROWS,),
        in_specs=[SMEM, rows_of(width), rows_of(width), rows_of(inner), rows_of(inner)]
        + [pl.BlockSpec((w_local.shape[0], inner), lambda i: (0, 0))]
        + [
            whole(v.shape)
            for v in (gate_far, gate_near, out_local, out_far, out_near, skip, gate_gain, heads)
        ],
        out_specs=[
            whole((width, inner)),
            whole((inner, width)),
            rows_of(inner),
            rows_of(width),
            rows_of(inner),
            rows_of(inner),
            rows_of(LANES),
            whole((8, inner)),
            whole((8, inner)),
        ],
        out_shape=[
            shape((width, inner), BF16),
            shape((inner, width), BF16),
            shape((count, inner), BF16),
            shape((count, width), BF16),
            shape((count, inner), BF16),
            shape((count, inner), BF16),
            shape((count, LANES), F32),
            shape((8, inner), F32),
            shape((8, inner), F32),
        ],
        scratch_shapes=[pltpu.VMEM((ROWS, inner), F32) for _ in range(4)],
        compiler_params=params(),
        cost_estimate=cost(35_000_000_000, 50_000_000),
        name="gate_both_ways",
    )(ends, cot, normed, u, y, w_local, gate_far, gate_near, out_local, out_far, out_near, skip, gate_gain, heads)


def run_backward(first_pair, pairs, part, carried, ends, u, conv_in, raw, dy, s1, states, conv_w, step_bias, neg_rate, skip, heads):
    count, full_channels = u.shape
    full_inner = dy.shape[1]
    with_bc = part is not None
    inner = pairs * LANES
    channels = inner + (2 * LANES if with_bc else 0)
    per = ROWS // CHUNK
    steps = count // ROWS // 2
    resumed = carried is not None
    last = steps - 1 if resumed else 2 * steps - 1
    at = first_pair // pairs
    bc_at = full_inner // (2 * LANES)
    if part is None:
        part = jnp.zeros((8, LANES), F32)
        part_spec = whole(part.shape)
        part_out_shape = (count, 3 * LANES)
        width_out = channels
        own_taps = conv_w[:, first_pair * LANES : first_pair * LANES + inner]
    else:
        part_spec = pl.BlockSpec((ROWS, 3 * LANES), lambda i: (last - i, 0))
        part_out_shape = (8, LANES)
        width_out = channels + LANES
        own_taps = conv_w[:, first_pair * LANES :]

    def rows_of(n, c=0):
        return pl.BlockSpec((ROWS, n), lambda i: (last - i, c))

    shape = jax.ShapeDtypeStruct
    sums = ((32, channels), (8, channels), (8, LANES), (8, LANES), (LANES, inner), (8, channels))
    in_specs = [
        SMEM,
        rows_of(inner, at),
        rows_of(inner, at),
        rows_of(2 * LANES, bc_at),
        rows_of(2 * LANES, bc_at),
        rows_of(LANES),
        rows_of(inner, at),
        rows_of(LANES),
        pl.BlockSpec((per, LANES, inner), lambda i: (last - i, 0, at)),
        part_spec,
        whole(own_taps.shape),
        whole(step_bias.shape),
        whole(neg_rate.shape),
        pl.BlockSpec((1, inner), lambda i: (0, at)),
        pl.BlockSpec((inner, LANES), lambda i: (at, 0)),
    ]
    args = [ends, u, conv_in, u, conv_in, raw, dy, s1, states, part, own_taps, step_bias, neg_rate, skip, heads]
    aliases = {}
    if resumed:
        aliases = {len(args): 0, len(args) + 1: 1}
        args += list(carried)
        in_specs += [pl.BlockSpec(memory_space=pl.ANY)] * 2 + [whole(s) for s in sums]
    return pl.pallas_call(
        functools.partial(backward_kernel, first_pair, pairs, with_bc, last, resumed),
        grid=(steps,),
        in_specs=in_specs,
        out_specs=[
            rows_of(width_out),
            whole(part_out_shape) if with_bc else rows_of(3 * LANES),
        ]
        + [whole(s) for s in sums],
        out_shape=[shape((count, width_out), BF16), shape(part_out_shape, F32)]
        + [shape(s, F32) for s in sums],
        scratch_shapes=[
            pltpu.VMEM((channels // LANES, ROWS + 8, LANES), F32),
            pltpu.VMEM((ROWS, inner), BF16),
            pltpu.VMEM((ROWS, 2 * LANES), F32),
            pltpu.VMEM((ROWS, channels), F32),
            pltpu.VMEM((CHUNK, inner), F32),
            pltpu.VMEM((CHUNK, inner), F32),
            pltpu.VMEM((CHUNK, inner), BF16),
            pltpu.VMEM((16, inner), F32),
        ],
        input_output_aliases=aliases,
        compiler_params=params(),
        cost_estimate=cost(25_000_000_000, 20_000_000),
        name=("backward_b" if with_bc else "backward_a") + ("_low" if resumed else "_high"),
    )(*args)


def tail_rows(n):
    return pl.BlockSpec((TAIL, n), lambda i: (i, 0))


def run_out(ends, tok, gated, w_out):
    count, width = tok.shape
    return pl.pallas_call(
        out_kernel,
        grid=(count // TAIL,),
        in_specs=[SMEM, tail_rows(width), tail_rows(gated.shape[1]), whole(w_out.shape)],
        out_specs=tail_rows(width),
        out_shape=jax.ShapeDtypeStruct((count, width), BF16),
        compiler_params=params(),
        cost_estimate=cost(8_000_000_000, 15_000_000),
        name="block_out",
    )(ends, tok, gated, w_out)


def run_part(dgate, rest_a, w_gate, w_conv):
    count = dgate.shape[0]
    width = w_conv.shape[0]
    return pl.pallas_call(
        part_kernel,
        grid=(count // TAIL,),
        in_specs=[
            tail_rows(dgate.shape[1]),
            tail_rows(rest_a.shape[1]),
            whole(w_gate.shape),
            pl.BlockSpec((width, rest_a.shape[1]), lambda i: (0, 0)),
        ],
        out_specs=tail_rows(width),
        out_shape=jax.ShapeDtypeStruct((count, width), F32),
        compiler_params=params(),
        cost_estimate=cost(10_000_000_000, 20_000_000),
        name="grad_normed_part",
    )(dgate, rest_a, w_gate, w_conv)


def run_norm(tok, cot, part, rest_b, w_conv, norm_gain):
    count, width = tok.shape
    return pl.pallas_call(
        norm_kernel,
        grid=(count // TAIL,),
        in_specs=[
            tail_rows(width),
            tail_rows(width),
            tail_rows(width),
            tail_rows(rest_b.shape[1]),
            whole(w_conv.shape),
            whole(norm_gain.shape),
        ],
        out_specs=tail_rows(width),
        out_shape=jax.ShapeDtypeStruct((count, width), BF16),
        compiler_params=params(),
        cost_estimate=cost(10_000_000_000, 20_000_000),
        name="norm_backward",
    )(tok, cot, part, rest_b, w_conv, norm_gain)


def pad_lanes(v):
    return jnp.pad(v, ((0, 0), (0, LANES - v.shape[1])))


def swap(v, mask):
    n = lax.axis_size("rep") * lax.axis_size("shard")
    return lax.ppermute(v, ("rep", "shard"), [(i, i ^ mask) for i in range(n)])


def place():
    return lax.axis_index("rep") * lax.axis_size("shard") + lax.axis_index("shard")


SHARD, CORE = 1, 2


def half_rows(v):
    half = v.shape[0] // 2
    core = (place() // CORE) % 2
    return lax.dynamic_slice_in_dim(v, core * half, half, 0)


def take(v, index):
    return lax.dynamic_index_in_dim(v, index, 0, keepdims=False)


def exchanges():
    n = lax.axis_size("rep") * lax.axis_size("shard")
    bits = [SHARD]
    bit = 2 * CORE
    while bit < n:
        bits.append(bit)
        bit *= 2
    return bits


def at_bit(bit):
    return (place() // bit) % 2


def cut(v, bit):
    if v.ndim == 2:
        v = v.reshape(2, v.shape[0] // 2, v.shape[1])
    me = at_bit(bit)
    return take(v, me), take(v, 1 - me).astype(BF16)


def add(kept, got):
    return kept + got.astype(F32)


def both_sum(low, bit):
    return (low.astype(F32) + swap(low, bit).astype(F32)).astype(BF16)


def join(low, got, bit):
    return jnp.where(at_bit(bit) == 0, jnp.concatenate([low, got], 0), jnp.concatenate([got, low], 0))


def core_sum(g):
    rows, n = g.shape
    v = g.reshape(2, 2, rows // 4, n)
    core = (place() // CORE) % 2
    other = lax.dynamic_index_in_dim(v, 1 - core, 1, keepdims=False).astype(BF16)
    kept = lax.dynamic_index_in_dim(v, core, 1, keepdims=False)
    return kept + swap(other, CORE).astype(F32)


def after(gate, *values):
    return lax.optimization_barrier((gate, *values))


def per_device(
    tokens,
    cotangent,
    seq_lengths,
    seq_device,
    norm_gain,
    in_weight,
    conv_weight,
    conv_bias,
    step_bias,
    decay_log,
    skip_gain,
    gate_gain,
    out_weight,
):
    shards = lax.axis_size("shard")
    shard = lax.axis_index("shard")
    device = lax.axis_index("rep") * shards + shard
    half_count = seq_lengths.shape[0] // 2
    owned = seq_device[:half_count] == device
    first_len = jnp.sum(jnp.where(owned, seq_lengths[:half_count], 0))
    second_len = jnp.sum(jnp.where(owned, seq_lengths[half_count:], 0))
    ends = jnp.stack(
        [first_len, first_len + second_len, lax.axis_index("rep") % 2, shard]
    ).astype(jnp.int32)
    count, width = tokens.shape
    inner = gate_gain.shape[0] * shards
    channels = conv_weight.shape[1] * shards
    head_count = step_bias.shape[0] * shards
    size = inner // head_count
    taps = conv_weight.shape[0]

    small = (norm_gain, conv_weight.reshape(-1), conv_bias, step_bias, decay_log, skip_gain, gate_gain)
    sizes = [v.shape[0] for v in small]
    own = jnp.concatenate(small)
    own = jnp.pad(own, (0, -own.shape[0] % 1024)).reshape(-1, LANES)
    in_half = half_rows(in_weight)
    conv_far = swap(in_half[:, inner:], SHARD)
    other = swap(own, SHARD)
    conv_near = swap(conv_far, CORE)
    conv_near, gate_send, out_send = after(conv_near, in_half[:, :inner], half_rows(out_weight))
    gate_far = swap(gate_send, SHARD)
    out_far = swap(out_send, SHARD)

    packed = jnp.where(shard == 0, jnp.stack([own, other]), jnp.stack([other, own])).reshape(2, -1)
    parts = []
    at = 0
    for n in sizes:
        parts.append(packed[:, at : at + n])
        at += n
    full_norm, _, full_shift, full_step, full_decay, full_skip, full_gate = [
        p.reshape(-1).astype(F32) for p in parts
    ]
    conv_w = parts[1].reshape(shards, taps, -1).transpose(1, 0, 2).reshape(taps, -1).astype(F32)
    conv_b = full_shift[None, :]
    norm_row = full_norm[None, :]
    gate_row = full_gate[None, :]
    lane_head = lax.broadcasted_iota(jnp.int32, (inner, LANES), 0) // size
    heads = (lane_head == lax.broadcasted_iota(jnp.int32, (inner, LANES), 1)).astype(BF16)
    skip = jnp.repeat(full_skip, size)[None, :]
    step_row = pad_lanes(full_step[None, :])
    neg_rate = pad_lanes(-jnp.exp(full_decay)[None, :])

    normed, u, conv_in, raw, y, states, w_conv = run_scan(
        ends, tokens, in_weight, conv_far, conv_near, norm_row, conv_w, conv_b, step_row, neg_rate, inner
    )
    normed, gate_far, out_far = after(normed, gate_far, out_far)
    gate_near = swap(gate_far, CORE)
    out_near = swap(out_far, CORE)
    w_gate, w_out, gated, masked, dy, dgate, s1, gain8, skip8 = run_gate(
        ends, cotangent, normed, u, y, in_weight, gate_far, gate_near, out_weight, out_far, out_near, skip, gate_row, heads
    )
    bits = exchanges()
    far, last_bit = bits[1:-1], bits[-1]
    g_out = dot(gated, masked, ((0,), (0,)))
    h_out = core_sum(g_out)
    g_out, normed = after(g_out, normed)
    g_gate = dot(normed, dgate, ((0,), (0,)))
    h_gate = core_sum(g_gate)
    quarter = h_out.shape[1] // 2
    held = jnp.concatenate([h_out[:, :quarter], h_out[:, quarter:], h_gate], axis=2)
    half_pairs = inner // LANES // 2
    shared = (s1, states, conv_w, step_row, neg_rate, skip, heads)

    kept, sent = cut(held, SHARD)
    dy, sent = after(dy, sent)
    got = swap(sent, SHARD)
    carry = run_backward(0, half_pairs, None, None, ends, u, conv_in, raw, dy, *shared)
    first_out, kept, got = after(carry[0], kept, got)
    kept, sent = cut(add(kept, got), far[0])
    dy, sent = after(dy, sent)
    got = swap(sent, far[0])
    rest_a, part, cw_a, cb_a, _, dl_a, _, _ = run_backward(
        0, half_pairs, None, (first_out, *carry[1:]), ends, u, conv_in, raw, dy, *shared
    )
    rest_a, kept, got = after(rest_a, kept, got)
    g_a = dot(normed, rest_a, ((0,), (0,)))
    held = add(kept, got)
    kept, sent = cut(held, far[1])
    kept_a, sent_a = cut(core_sum(g_a), SHARD)
    part, sent, sent_a = after(part, sent, sent_a)
    got = swap(sent, far[1])
    got_a = swap(sent_a, SHARD)
    carry = run_backward(half_pairs, half_pairs, part, None, ends, u, conv_in, raw, dy, *shared)
    first_out, kept, got, kept_a, got_a = after(carry[0], kept, got, kept_a, got_a)
    held = add(kept, got)
    for bit in far[2:]:
        kept, sent = cut(held, bit)
        held = add(kept, swap(sent, bit))
    low = held.astype(BF16)
    kept_a, sent_a = cut(add(kept_a, got_a), far[0])
    part, low, sent_a = after(part, low, sent_a)
    got = swap(low, last_bit)
    got_a = swap(sent_a, far[0])
    rest_b, _, cw_b, cb_b, sb_b, dl_b, _, _ = run_backward(
        half_pairs, half_pairs, part, (first_out, *carry[1:]), ends, u, conv_in, raw, dy, *shared
    )
    rest_b, low, got, kept_a, got_a = after(rest_b, low, got, kept_a, got_a)
    g_b = dot(normed, rest_b, ((0,), (0,)))

    split = channels - half_pairs * LANES
    g_conv = jnp.sum(jnp.concatenate([cw_a, cw_b], 1).reshape(taps, 8, channels), axis=1)
    g_shift = jnp.sum(jnp.concatenate([cb_a, cb_b], 1), axis=0)
    g_step = jnp.sum(sb_b, axis=0)[:head_count]
    g_decay = jnp.sum(dl_a + dl_b, axis=0)[:head_count]
    g_skip = jnp.sum(skip8.reshape(8, head_count, size), axis=(0, 2))
    g_gain = jnp.sum(gain8, axis=0)
    pieces = (
        g_conv.reshape(taps, shards, -1).transpose(1, 0, 2).reshape(shards, -1),
        g_shift.reshape(shards, -1),
        g_step.reshape(shards, -1),
        g_decay.reshape(shards, -1),
        g_skip.reshape(shards, -1),
        g_gain.reshape(shards, -1),
    )
    flat = jnp.concatenate(pieces, axis=1)
    own_rows = width // shards
    extra = -(-flat.shape[1] // own_rows)
    flat = jnp.pad(flat, ((0, 0), (0, extra * own_rows - flat.shape[1])))
    flat = flat.reshape(width, extra)
    g_b = jnp.concatenate([g_b[:, : split + head_count], flat], axis=1)
    low = add(low.astype(F32), got).astype(BF16)
    held_a = add(kept_a, got_a)
    kept_b, sent_b = cut(core_sum(g_b), SHARD)
    backs = far[::-1] + [CORE]
    gated, low, sent_b = after(gated, low, sent_b)
    got = swap(low, backs[0])
    got_b = swap(sent_b, SHARD)
    block_out = run_out(ends, tokens, gated, w_out)
    block_out, low, got, kept_b, got_b = after(block_out, low, got, kept_b, got_b)
    low = join(low, got, backs[0])
    kept_b, sent_b = cut(add(kept_b, got_b), far[0])
    dgate, low, sent_b = after(dgate, low, sent_b)
    got = swap(low, backs[1])
    got_b = swap(sent_b, far[0])
    grad_part = run_part(dgate, rest_a, w_gate, w_conv)
    grad_part, low, got, kept_b, got_b = after(grad_part, low, got, kept_b, got_b)
    low = join(low, got, backs[1])
    held_b = jnp.concatenate([held_a, add(kept_b, got_b)], axis=1)
    kept_b, sent_b = cut(held_b, far[1])
    grad_part, low, sent_b = after(grad_part, low, sent_b)
    got = swap(low, backs[2])
    got_b = swap(sent_b, far[1])
    grad_tokens = run_norm(tokens, cotangent, grad_part, rest_b, w_conv, norm_row)
    grad_tokens, low, got, kept_b, got_b = after(grad_tokens, low, got, kept_b, got_b)
    low = join(low, got, backs[2])
    for bit in backs[3:]:
        low = join(low, swap(low, bit), bit)
    held_b = add(kept_b, got_b)
    for bit in far[2:]:
        kept_b, sent_b = cut(held_b, bit)
        held_b = add(kept_b, swap(sent_b, bit))
    low_b = both_sum(held_b.astype(BF16), last_bit)
    for bit in backs:
        low_b = join(low_b, swap(low_b, bit), bit)
    near = out_weight.shape[1]
    by_core = low.reshape(2, low.shape[0] // 2, low.shape[1])
    t_out = jnp.concatenate(
        [by_core[0, :, :near], by_core[0, :, near : 2 * near], by_core[1, :, :near], by_core[1, :, near : 2 * near]], axis=0
    )
    t_b = low_b[:, half_pairs * LANES :]
    t_in = jnp.concatenate(
        [low[:, 2 * near :], low_b[:, : half_pairs * LANES + split + head_count]], axis=1
    ).astype(F32)
    t_norm = jnp.sum(t_in * in_weight.astype(F32), axis=1) / norm_gain.astype(F32)
    mine = t_b[:, split + head_count :].reshape(-1).astype(F32)
    outs = []
    at = 0
    for n in sizes[1:]:
        outs.append(mine[at : at + n])
        at += n
    return (
        block_out,
        grad_tokens,
        t_norm,
        t_in,
        outs[0].reshape(taps, -1),
        outs[1],
        outs[2],
        outs[3],
        outs[4],
        outs[5],
        t_out.astype(F32),
    )


def solution(mesh):
    in_specs = (
        P(("rep", "shard"), None),
        P(("rep", "shard"), None),
        P(),
        P(),
        P("shard"),
        P("shard", None),
        P(None, "shard"),
        P("shard"),
        P("shard"),
        P("shard"),
        P("shard"),
        P("shard"),
        P("shard", None),
    )
    out_specs = (
        P(("rep", "shard"), None),
        P(("rep", "shard"), None),
        P("shard"),
        P("shard", None),
        P(None, "shard"),
        P("shard"),
        P("shard"),
        P("shard"),
        P("shard"),
        P("shard"),
        P("shard", None),
    )
    return jax.shard_map(
        per_device, mesh=mesh, in_specs=in_specs, out_specs=out_specs, check_vma=False
    )
```

```python
import functools

import jax
import jax.numpy as jnp
from jax import lax
from jax.experimental import pallas as pl
from jax.experimental.pallas import tpu as pltpu
from jax.sharding import PartitionSpec as P

ROWS = 256
CHUNK = 128
TAIL = 512
LANES = 128
LOG2E = 1.4426950408889634
F32 = jnp.float32
BF16 = jnp.bfloat16
HIGH = lax.Precision.HIGHEST
VMEM_LIMIT = 60 * 1024 * 1024


def dot(a, b, dims=((1,), (0,)), precision=None):
    return lax.dot_general(a, b, (dims, ((), ())), precision=precision, preferred_element_type=F32)


def fold8(v):
    return jnp.sum(v.reshape(v.shape[0] // 8, 8, v.shape[1]), axis=0)


def segment_of(position, first_end, second_end):
    return (position >= first_end).astype(jnp.int32) + (position >= second_end).astype(jnp.int32)


def softplus(v):
    return jnp.maximum(v, 0.0) + jnp.log1p(jnp.exp(-jnp.abs(v)))


def head_sums(v, heads):
    high = v.astype(BF16)
    low = (v - high.astype(F32)).astype(BF16)
    return dot(high, heads) + dot(low, heads)


def lane_pair(v, p, lane_low):
    shape = lane_low.shape
    a = jnp.broadcast_to(v[:, 2 * p : 2 * p + 1], shape)
    b = jnp.broadcast_to(v[:, 2 * p + 1 : 2 * p + 2], shape)
    return a, b


def split_rows(pair, lane_low):
    zero = jnp.zeros_like(pair)
    return jnp.concatenate(
        [jnp.where(lane_low, pair, zero), jnp.where(lane_low, zero, pair)], axis=0
    )


def chunk_setup(raw, step_bias, neg_rate, start, first_end, second_end):
    row = lax.broadcasted_iota(jnp.int32, (CHUNK, LANES), 0)
    col = lax.broadcasted_iota(jnp.int32, (CHUNK, LANES), 1)
    step = softplus(raw + step_bias)
    rate = neg_rate * step
    lower = (row >= col).astype(F32)
    cum = dot(lower, rate, precision=HIGH) * LOG2E
    seg_row = segment_of(row + start, first_end, second_end)
    seg_col = segment_of(col + start, first_end, second_end)
    last_seg = segment_of(start - 1, first_end, second_end)
    end_seg = segment_of(start + CHUNK - 1, first_end, second_end)
    entry = (seg_row == last_seg).astype(F32)
    tail = (seg_row == end_seg).astype(F32)
    keep = (last_seg == end_seg).astype(F32)
    same = seg_row == seg_col
    return row, col, step, rate, cum, same, entry, tail, keep


def place_rows(dst, width, local, far, near, core, shard):
    half = far.shape[0]
    own_at = pl.multiple_of(shard * (2 * half), half)
    other_at = (1 - shard) * (2 * half)
    dst[pl.ds(own_at, 2 * half), :width] = local
    dst[pl.ds(pl.multiple_of(other_at + core * half, half), half), :width] = far[...]
    dst[pl.ds(pl.multiple_of(other_at + (1 - core) * half, half), half), :width] = near[...]


def scan_kernel(
    ends,
    tok,
    w_local,
    w_far,
    w_near,
    norm_gain,
    conv_w,
    conv_b,
    step_bias,
    neg_rate,
    normed_out,
    u_out,
    conv_in_out,
    raw_out,
    y_out,
    state_out,
    w_conv,
    ext,
    xs,
    bc,
    wx_s,
    keep_s,
    state,
):
    step_id = pl.program_id(0)
    first_end = ends[0]
    second_end = ends[1]
    inner = xs.shape[1]
    channels = ext.shape[0] * LANES
    pairs = inner // LANES
    base = step_id * ROWS

    @pl.when(step_id == 0)
    def _():
        w_conv[:, channels:] = jnp.zeros((w_conv.shape[0], LANES), BF16)
        used = w_far.shape[1]
        place_rows(w_conv, used, w_local[:, inner:], w_far, w_near, ends[2], ends[3])
        ext[:, 0:8, :] = jnp.zeros((channels // LANES, 8, LANES), F32)
        state[...] = jnp.zeros_like(state)

    rows = tok[...].astype(F32)
    scale = lax.rsqrt(jnp.mean(rows * rows, axis=-1, keepdims=True) + 1e-05)
    normed = (rows * scale * norm_gain[...]).astype(BF16)
    normed_out[...] = normed
    raw_out[...] = dot(normed, w_conv[:, channels:])

    pos = lax.broadcasted_iota(jnp.int32, (ROWS, LANES), 0) + base
    seg = segment_of(pos, first_end, second_end)
    shift_mask = [
        ((segment_of(pos - k, first_end, second_end) == seg) & (pos >= k)).astype(F32)
        for k in range(1, 4)
    ]

    def conv_tile(ct):
        cols = slice(ct * LANES, (ct + 1) * LANES)
        if ct % 2 == 0:
            wide = slice(ct * LANES, (ct + 2) * LANES)
            conv_in = dot(normed, w_conv[:, wide])
            ext[ct, 8 : 8 + ROWS, :] = conv_in[:, :LANES]
            ext[ct + 1, 8 : 8 + ROWS, :] = conv_in[:, LANES:]
            conv_in_out[:, wide] = conv_in.astype(BF16)
        total = conv_b[:, cols] + conv_w[3:4, cols] * ext[ct, 8 : 8 + ROWS, :]
        for k in range(1, 4):
            total += (conv_w[3 - k : 4 - k, cols] * ext[ct, 8 - k : 8 - k + ROWS, :]) * shift_mask[k - 1]
        u = total.astype(BF16)
        u_out[:, cols] = u
        half = 0.5 * u.astype(F32)
        return half + half * jnp.tanh(half)

    for ct in range(pairs):
        xs[:, ct * LANES : (ct + 1) * LANES] = conv_tile(ct)
    for ct in range(pairs, channels // LANES):
        bc[:, (ct - pairs) * LANES : (ct - pairs + 1) * LANES] = conv_tile(ct)
    ext[:, 0:8, :] = ext[:, ROWS : ROWS + 8, :]

    def chunk(q, carry):
        r0 = pl.multiple_of(q * CHUNK, CHUNK)
        rsl = pl.ds(r0, CHUNK)
        row, col, step, rate, cum, same, entry, tail, keep = chunk_setup(
            raw_out[rsl, :], step_bias[...], neg_rate[...], base + r0, first_end, second_end
        )
        cum_t = cum.T
        shift_t = cum_t - jnp.log2(step.T)
        tail_t = (segment_of(col + (base + r0), first_end, second_end) == segment_of(base + r0 + CHUNK - 1, first_end, second_end)).astype(F32)
        weight_t = jnp.exp2(cum_t[:, CHUNK - 1 : CHUNK] - shift_t) * tail_t
        lane_low = col < (LANES // 2)
        b_f = bc[rsl, 0:LANES]
        b_t = b_f.T
        b_low = b_f.astype(BF16)
        c_low = bc[rsl, LANES : 2 * LANES].astype(BF16)
        gram = dot(c_low, b_low, ((1,), (1,)))
        gram = jnp.where(same & (row >= col), gram, 0.0)
        state_low = state[...].astype(BF16)
        state_out[q] = state_low
        y_out[rsl, :] = dot(c_low, state_low)
        for p in range(pairs):
            cols = slice(p * LANES, (p + 1) * LANES)
            ca, cb = lane_pair(cum, p, lane_low)
            ma = (jnp.exp2(jnp.minimum(ca - shift_t[2 * p : 2 * p + 1, :], 100.0)) * gram).astype(BF16)
            mb = (jnp.exp2(jnp.minimum(cb - shift_t[2 * p + 1 : 2 * p + 2, :], 100.0)) * gram).astype(BF16)
            ba = (b_t * weight_t[2 * p : 2 * p + 1, :]).astype(BF16)
            bb = (b_t * weight_t[2 * p + 1 : 2 * p + 2, :]).astype(BF16)
            x2 = split_rows(xs[rsl, cols].astype(BF16), lane_low)
            left = jnp.concatenate(
                [jnp.concatenate([ma, mb], axis=1), jnp.concatenate([ba, bb], axis=1)], axis=0
            )
            both_out = dot(left, x2)
            decay = jnp.exp2(jnp.where(lane_low, ca, cb))
            y_out[rsl, cols] = both_out[:CHUNK] + y_out[rsl, cols] * (decay * entry)
            state[:, cols] = state[:, cols] * (decay[CHUNK - 1 : CHUNK, :] * keep) + both_out[CHUNK:]
        return carry

    for at in range(ROWS // CHUNK):
        chunk(at, 0)


def gate_kernel(
    ends,
    cot,
    normed,
    u_in,
    y_in,
    w_local,
    gate_far,
    gate_near,
    out_local,
    out_far,
    out_near,
    skip,
    gate_gain,
    heads,
    w_gate,
    w_out,
    gated_out,
    masked_out,
    dy_out,
    dgate_out,
    s1_out,
    gain_grad,
    skip_grad,
    gate_s,
    xs,
    prod_s,
    dg_s,
):
    step_id = pl.program_id(0)
    second_end = ends[1]
    inner = gate_s.shape[1]
    pairs = inner // LANES
    base = step_id * ROWS

    @pl.when(step_id == 0)
    def _():
        place_rows(w_gate, inner, w_local[...], gate_far, gate_near, ends[2], ends[3])
        place_rows(w_out, w_out.shape[1], out_local[...], out_far, out_near, ends[2], ends[3])
        gain_grad[...] = jnp.zeros_like(gain_grad)
        skip_grad[...] = jnp.zeros_like(skip_grad)

    pos = lax.broadcasted_iota(jnp.int32, (ROWS, LANES), 0) + base
    live = (pos < second_end).astype(F32)
    masked = (cot[...].astype(F32) * live[:, 0:1]).astype(BF16)
    masked_out[...] = masked
    sq = jnp.zeros((ROWS, LANES), F32)
    cross = jnp.zeros((ROWS, LANES), F32)
    for ct in range(pairs):
        cols = slice(ct * LANES, (ct + 1) * LANES)
        if ct % 2 == 0:
            wide = slice(ct * LANES, (ct + 2) * LANES)
            gate_s[:, wide] = dot(normed[...], w_gate[:, wide])
            dg_s[:, wide] = dot(masked, w_out[wide, :], ((1,), (1,)))
        half = 0.5 * gate_s[:, cols]
        half_u = 0.5 * u_in[:, cols].astype(F32)
        x = half_u + half_u * jnp.tanh(half_u)
        xs[:, cols] = x
        product = (y_in[:, cols] + skip[:, cols] * x) * (half + half * jnp.tanh(half))
        prod_s[:, cols] = product
        sq += product * product
        cross += dg_s[:, cols] * gate_gain[:, cols] * product
    r = lax.rsqrt(jnp.sum(sq, axis=1, keepdims=True) / inner + 1e-05)
    m = jnp.sum(cross, axis=1, keepdims=True) / inner
    r_wide = jnp.broadcast_to(r, (ROWS, LANES))
    m_wide = jnp.broadcast_to(r * r * r * m, (ROWS, LANES))
    for ct in range(pairs):
        cols = slice(ct * LANES, (ct + 1) * LANES)
        g = gate_s[:, cols]
        sig = 0.5 + 0.5 * jnp.tanh(0.5 * g)
        act = g * sig
        x = xs[:, cols]
        y = y_in[:, cols]
        product = prod_s[:, cols]
        pr = product * r_wide
        gated_out[:, cols] = (pr * gate_gain[:, cols]).astype(BF16)
        dg = dg_s[:, cols]
        gain_grad[:, cols] += fold8(dg * pr)
        dprod = r_wide * (dg * gate_gain[:, cols]) - product * m_wide
        dsc = dprod * act
        dgate_out[:, cols] = (
            dprod * (y + skip[:, cols] * x) * (sig + act * (1.0 - sig))
        ).astype(BF16)
        dy = dsc.astype(BF16)
        dy_out[:, cols] = dy
        skip_grad[:, cols] += fold8(dsc * x)
        prod_s[:, cols] = dy.astype(F32) * y
    s1_out[...] = head_sums(prod_s[...], heads[...])


def backward_kernel(
    first_pair,
    pairs,
    with_bc,
    last,
    resumed,
    ends,
    u_in,
    conv_in,
    ubc_in,
    cbc_in,
    raw_in,
    dy_in,
    s1_in,
    state_in,
    part_in,
    conv_w,
    step_bias,
    neg_rate,
    skip,
    heads,
    *refs,
):
    carried = refs[:8] if resumed else None
    refs = refs[8:] if resumed else refs
    (
        dconv_out,
        part_out,
        conv_w_grad,
        conv_b_grad,
        step_grad,
        decay_grad,
        dstate,
        halo,
        ext,
        xs,
        bc,
        slope,
        bds,
        q_s,
        wx_s,
        rows_s,
    ) = refs
    step_id = pl.program_id(0)
    first_end = ends[0]
    second_end = ends[1]
    inner = pairs * LANES
    channels = ext.shape[0] * LANES
    base = (last - step_id) * ROWS

    @pl.when(step_id == 0)
    def _():
        sums = (conv_w_grad, conv_b_grad, step_grad, decay_grad, dstate, halo)
        for at, ref in enumerate(sums):
            ref[...] = carried[2 + at][...] if resumed else jnp.zeros_like(ref)
        for ct in range(channels // LANES):
            ext[ct, ROWS : ROWS + 8, :] = halo[:, ct * LANES : (ct + 1) * LANES]
        rows_s[...] = jnp.zeros_like(rows_s)

    for ct in range(pairs + 2):
        if ct < pairs:
            u = u_in[:, ct * LANES : (ct + 1) * LANES].astype(F32)
        else:
            u = ubc_in[:, (ct - pairs) * LANES : (ct - pairs + 1) * LANES].astype(F32)
        sig = 0.5 + 0.5 * jnp.tanh(0.5 * u)
        act = u * sig
        if ct < pairs or with_bc:
            slope[:, ct * LANES : (ct + 1) * LANES] = sig + act * (1.0 - sig)
        if ct < pairs:
            xs[:, ct * LANES : (ct + 1) * LANES] = act.astype(BF16)
        else:
            bc[:, (ct - pairs) * LANES : (ct - pairs + 1) * LANES] = act

    def chunk(k, carry):
        q = ROWS // CHUNK - 1 - k
        r0 = pl.multiple_of(q * CHUNK, CHUNK)
        rsl = pl.ds(r0, CHUNK)
        raw = raw_in[rsl, :]
        row, col, step, rate, cum, same, entry, tail, keep = chunk_setup(
            raw, step_bias[...], neg_rate[...], base + r0, first_end, second_end
        )
        cum_t = cum.T
        shift = cum - jnp.log2(step)
        last_seg = segment_of(base + r0 - 1, first_end, second_end)
        entry_t = (segment_of(col + (base + r0), first_end, second_end) == last_seg).astype(F32)
        enter_t = jnp.exp2(cum_t) * entry_t
        lane_low = col < (LANES // 2)
        b_f = bc[rsl, 0:LANES]
        b_low = b_f.astype(BF16)
        c_f = bc[rsl, LANES : 2 * LANES]
        c_low = c_f.astype(BF16)
        c_t = c_f.T
        allowed = same & (row <= col)
        gram = jnp.where(allowed, dot(b_low, c_low, ((1,), (1,))), 0.0)
        dstate_low = dstate[...].astype(BF16)
        bds[...] = dot(b_low, dstate_low)
        dgram = jnp.zeros((CHUNK, CHUNK), F32)
        dc_t = jnp.zeros((LANES, CHUNK), F32)
        for p in range(pairs):
            cols = slice(p * LANES, (p + 1) * LANES)
            head = 2 * (p + first_pair)
            ca, cb = lane_pair(shift, p + first_pair, lane_low)
            la = jnp.exp2(jnp.minimum(cum_t[head : head + 1, :] - ca, 100.0))
            lb = jnp.exp2(jnp.minimum(cum_t[head + 1 : head + 2, :] - cb, 100.0))
            both = jnp.where(lane_low, ca, cb)
            ea, eb = lane_pair(cum[CHUNK - 1 : CHUNK, :], p + first_pair, lane_low[0:1, :])
            end = jnp.where(lane_low[0:1, :], ea, eb)
            dy_low = dy_in[rsl, cols]
            dy = dy_low.astype(F32)
            dy2 = split_rows(dy_low, lane_low)
            x_low = xs[rsl, cols]
            state_low = state_in[q, :, cols]
            top = dot(jnp.concatenate([x_low, state_low], axis=0), dy2, ((1,), (1,)))
            enter_a = enter_t[head : head + 1, :]
            enter_b = enter_t[head + 1 : head + 2, :]
            dgram += top[:CHUNK, :CHUNK] * la + top[:CHUNK, CHUNK:] * lb
            dc_t += top[CHUNK:, :CHUNK] * enter_a + top[CHUNK:, CHUNK:] * enter_b
            left = jnp.concatenate(
                [
                    jnp.concatenate([(la * gram).astype(BF16), (lb * gram).astype(BF16)], axis=1),
                    jnp.concatenate([(c_t * enter_a).astype(BF16), (c_t * enter_b).astype(BF16)], axis=1),
                ],
                axis=0,
            )
            down = dot(left, dy2)
            weight = jnp.exp2(end - both) * tail
            gxs = weight * bds[:, cols]
            gx = down[:CHUNK] + gxs
            x = x_low.astype(F32)
            q_s[:, cols] = x * gx
            ext[p, rsl, :] = (gx + skip[:, cols] * dy) * slope[rsl, cols]
            wx_s[:, cols] = (x * weight).astype(BF16)
            keep_row = jnp.exp2(end) * keep
            old = dstate[:, cols]
            rows_s[0:8, cols] = fold8(x * gxs) + keep_row * fold8(old * state_low.astype(F32))
            dstate[:, cols] = old * keep_row + down[CHUNK:]
        dgram = jnp.where(allowed, dgram, 0.0)
        dc = (dc_t + dot(b_f.T.astype(BF16), dgram.astype(BF16))).T
        db = dot(dgram.astype(BF16), c_low) + dot(wx_s[...], dstate_low, ((1,), (1,)))
        if with_bc:
            bsl = slice(inner, inner + LANES)
            csl = slice(inner + LANES, inner + 2 * LANES)
            ext[pairs, rsl, :] = (db + part_in[rsl, 0:LANES]) * slope[rsl, bsl]
            ext[pairs + 1, rsl, :] = (dc + part_in[rsl, LANES : 2 * LANES]) * slope[rsl, csl]
        else:
            part_out[rsl, 0:LANES] = db
            part_out[rsl, LANES : 2 * LANES] = dc
        sx = head_sums(q_s[...], heads[...])
        end_term = jnp.sum(head_sums(rows_s[0:8, :], heads[...]), axis=0, keepdims=True)
        upper = (row <= col).astype(F32)
        drate = dot(upper, s1_in[rsl, :] - sx, precision=HIGH) + end_term
        own = (col >= 2 * first_pair) & (col < 2 * (first_pair + pairs))
        drate = jnp.where(own, drate, 0.0)
        dstep = sx / jnp.maximum(step, 1e-37) + neg_rate[...] * drate
        draw = dstep * jax.nn.sigmoid(raw + step_bias[...])
        if with_bc:
            draw = draw + part_in[rsl, 2 * LANES : 3 * LANES]
            dconv_out[rsl, channels : channels + LANES] = draw.astype(BF16)
            step_grad[...] += fold8(draw)
        else:
            part_out[rsl, 2 * LANES : 3 * LANES] = draw
        decay_grad[...] += fold8(drate * rate)
        return carry

    for at in range(ROWS // CHUNK):
        chunk(at, 0)

    pos = lax.broadcasted_iota(jnp.int32, (ROWS, LANES), 0) + base
    seg = segment_of(pos, first_end, second_end)
    shift_mask = [
        (segment_of(pos + k, first_end, second_end) == seg).astype(F32) for k in range(1, 4)
    ]
    for ct in range(channels // LANES):
        cols = slice(ct * LANES, (ct + 1) * LANES)
        du = ext[ct, 0:ROWS, :]
        if ct < pairs:
            source = conv_in[:, cols].astype(F32)
        else:
            source = cbc_in[:, (ct - pairs) * LANES : (ct - pairs + 1) * LANES].astype(F32)
        conv_b_grad[:, cols] += fold8(du)
        conv_w_grad[24:32, cols] += fold8(source * du)
        total = conv_w[3:4, cols] * du
        for k in range(1, 4):
            later = ext[ct, k : k + ROWS, :] * shift_mask[k - 1]
            total += conv_w[3 - k : 4 - k, cols] * later
            conv_w_grad[8 * (3 - k) : 8 * (4 - k), cols] += fold8(source * later)
        dconv_out[:, cols] = total.astype(BF16)
    for ct in range(channels // LANES):
        first = ext[ct, 0:8, :]
        ext[ct, ROWS : ROWS + 8, :] = first
        halo[:, ct * LANES : (ct + 1) * LANES] = first


def out_kernel(ends, tok, gated, w_out, block_out):
    pos = lax.broadcasted_iota(jnp.int32, (TAIL, 1), 0) + pl.program_id(0) * TAIL
    live = (pos < ends[1]).astype(F32)
    block_out[...] = (tok[...].astype(F32) + live * dot(gated[...], w_out[...])).astype(BF16)


def part_kernel(dgate, rest_a, w_gate, w_conv, grad):
    grad[...] = dot(dgate[...], w_gate[...], ((1,), (1,))) + dot(rest_a[...], w_conv[...], ((1,), (1,)))


def norm_kernel(tok, cot, part, rest_b, w_conv, norm_gain, grad_tokens):
    split = w_conv.shape[1] - rest_b.shape[1]
    grad = part[...] + dot(rest_b[...], w_conv[:, split:], ((1,), (1,)))
    rows = tok[...].astype(F32)
    r = lax.rsqrt(jnp.mean(rows * rows, axis=-1, keepdims=True) + 1e-05)
    n = rows * r
    weighted = norm_gain[...] * grad
    mean = jnp.mean(weighted * n, axis=-1, keepdims=True)
    grad_tokens[...] = (r * (weighted - n * mean) + cot[...].astype(F32)).astype(BF16)


def whole(shape):
    return pl.BlockSpec(shape, lambda i: (0,) * len(shape))


def params():
    return pltpu.CompilerParams(dimension_semantics=("arbitrary",), vmem_limit_bytes=VMEM_LIMIT)


def cost(flops, moved):
    return pl.CostEstimate(flops=flops, bytes_accessed=moved, transcendentals=20_000_000)


SMEM = pl.BlockSpec(memory_space=pltpu.SMEM)


def run_scan(ends, tok, w_local, w_far, w_near, norm_gain, conv_w, conv_b, step_bias, neg_rate, inner):
    count, width = tok.shape
    channels = conv_w.shape[1]
    per = ROWS // CHUNK

    def rows_of(n):
        return pl.BlockSpec((ROWS, n), lambda i: (i, 0))

    shape = jax.ShapeDtypeStruct
    return pl.pallas_call(
        scan_kernel,
        grid=(count // ROWS,),
        in_specs=[SMEM, rows_of(width)]
        + [
            whole(v.shape)
            for v in (w_local, w_far, w_near, norm_gain, conv_w, conv_b, step_bias, neg_rate)
        ],
        out_specs=[
            rows_of(width),
            rows_of(channels),
            rows_of(channels),
            rows_of(LANES),
            rows_of(inner),
            pl.BlockSpec((per, LANES, inner), lambda i: (i, 0, 0)),
            whole((width, channels + LANES)),
        ],
        out_shape=[
            shape((count, width), BF16),
            shape((count, channels), BF16),
            shape((count, channels), BF16),
            shape((count, LANES), F32),
            shape((count, inner), F32),
            shape((count // CHUNK, LANES, inner), BF16),
            shape((width, channels + LANES), BF16),
        ],
        scratch_shapes=[
            pltpu.VMEM((channels // LANES, ROWS + 8, LANES), F32),
            pltpu.VMEM((ROWS, inner), F32),
            pltpu.VMEM((ROWS, 2 * LANES), F32),
            pltpu.VMEM((CHUNK, inner), BF16),
            pltpu.VMEM((8, inner), F32),
            pltpu.VMEM((LANES, inner), F32),
        ],
        compiler_params=params(),
        cost_estimate=cost(50_000_000_000, 50_000_000),
        name="mixer_scan",
    )(ends, tok, w_local, w_far, w_near, norm_gain, conv_w, conv_b, step_bias, neg_rate)


def run_gate(ends, cot, normed, u, y, w_local, gate_far, gate_near, out_local, out_far, out_near, skip, gate_gain, heads):
    count, width = cot.shape
    inner = y.shape[1]

    def rows_of(n):
        return pl.BlockSpec((ROWS, n), lambda i: (i, 0))

    shape = jax.ShapeDtypeStruct
    return pl.pallas_call(
        gate_kernel,
        grid=(count // ROWS,),
        in_specs=[SMEM, rows_of(width), rows_of(width), rows_of(inner), rows_of(inner)]
        + [pl.BlockSpec((w_local.shape[0], inner), lambda i: (0, 0))]
        + [
            whole(v.shape)
            for v in (gate_far, gate_near, out_local, out_far, out_near, skip, gate_gain, heads)
        ],
        out_specs=[
            whole((width, inner)),
            whole((inner, width)),
            rows_of(inner),
            rows_of(width),
            rows_of(inner),
            rows_of(inner),
            rows_of(LANES),
            whole((8, inner)),
            whole((8, inner)),
        ],
        out_shape=[
            shape((width, inner), BF16),
            shape((inner, width), BF16),
            shape((count, inner), BF16),
            shape((count, width), BF16),
            shape((count, inner), BF16),
            shape((count, inner), BF16),
            shape((count, LANES), F32),
            shape((8, inner), F32),
            shape((8, inner), F32),
        ],
        scratch_shapes=[pltpu.VMEM((ROWS, inner), F32) for _ in range(4)],
        compiler_params=params(),
        cost_estimate=cost(35_000_000_000, 50_000_000),
        name="gate_both_ways",
    )(ends, cot, normed, u, y, w_local, gate_far, gate_near, out_local, out_far, out_near, skip, gate_gain, heads)


def run_backward(first_pair, pairs, part, carried, ends, u, conv_in, raw, dy, s1, states, conv_w, step_bias, neg_rate, skip, heads):
    count, full_channels = u.shape
    full_inner = dy.shape[1]
    with_bc = part is not None
    inner = pairs * LANES
    channels = inner + (2 * LANES if with_bc else 0)
    per = ROWS // CHUNK
    steps = count // ROWS // 2
    resumed = carried is not None
    last = steps - 1 if resumed else 2 * steps - 1
    at = first_pair // pairs
    bc_at = full_inner // (2 * LANES)
    if part is None:
        part = jnp.zeros((8, LANES), F32)
        part_spec = whole(part.shape)
        part_out_shape = (count, 3 * LANES)
        width_out = channels
        own_taps = conv_w[:, first_pair * LANES : first_pair * LANES + inner]
    else:
        part_spec = pl.BlockSpec((ROWS, 3 * LANES), lambda i: (last - i, 0))
        part_out_shape = (8, LANES)
        width_out = channels + LANES
        own_taps = conv_w[:, first_pair * LANES :]

    def rows_of(n, c=0):
        return pl.BlockSpec((ROWS, n), lambda i: (last - i, c))

    shape = jax.ShapeDtypeStruct
    sums = ((32, channels), (8, channels), (8, LANES), (8, LANES), (LANES, inner), (8, channels))
    in_specs = [
        SMEM,
        rows_of(inner, at),
        rows_of(inner, at),
        rows_of(2 * LANES, bc_at),
        rows_of(2 * LANES, bc_at),
        rows_of(LANES),
        rows_of(inner, at),
        rows_of(LANES),
        pl.BlockSpec((per, LANES, inner), lambda i: (last - i, 0, at)),
        part_spec,
        whole(own_taps.shape),
        whole(step_bias.shape),
        whole(neg_rate.shape),
        pl.BlockSpec((1, inner), lambda i: (0, at)),
        pl.BlockSpec((inner, LANES), lambda i: (at, 0)),
    ]
    args = [ends, u, conv_in, u, conv_in, raw, dy, s1, states, part, own_taps, step_bias, neg_rate, skip, heads]
    aliases = {}
    if resumed:
        aliases = {len(args): 0, len(args) + 1: 1}
        args += list(carried)
        in_specs += [pl.BlockSpec(memory_space=pl.ANY)] * 2 + [whole(s) for s in sums]
    return pl.pallas_call(
        functools.partial(backward_kernel, first_pair, pairs, with_bc, last, resumed),
        grid=(steps,),
        in_specs=in_specs,
        out_specs=[
            rows_of(width_out),
            whole(part_out_shape) if with_bc else rows_of(3 * LANES),
        ]
        + [whole(s) for s in sums],
        out_shape=[shape((count, width_out), BF16), shape(part_out_shape, F32)]
        + [shape(s, F32) for s in sums],
        scratch_shapes=[
            pltpu.VMEM((channels // LANES, ROWS + 8, LANES), F32),
            pltpu.VMEM((ROWS, inner), BF16),
            pltpu.VMEM((ROWS, 2 * LANES), F32),
            pltpu.VMEM((ROWS, channels), F32),
            pltpu.VMEM((CHUNK, inner), F32),
            pltpu.VMEM((CHUNK, inner), F32),
            pltpu.VMEM((CHUNK, inner), BF16),
            pltpu.VMEM((16, inner), F32),
        ],
        input_output_aliases=aliases,
        compiler_params=params(),
        cost_estimate=cost(25_000_000_000, 20_000_000),
        name=("backward_b" if with_bc else "backward_a") + ("_low" if resumed else "_high"),
    )(*args)


def tail_rows(n):
    return pl.BlockSpec((TAIL, n), lambda i: (i, 0))


def run_out(ends, tok, gated, w_out):
    count, width = tok.shape
    return pl.pallas_call(
        out_kernel,
        grid=(count // TAIL,),
        in_specs=[SMEM, tail_rows(width), tail_rows(gated.shape[1]), whole(w_out.shape)],
        out_specs=tail_rows(width),
        out_shape=jax.ShapeDtypeStruct((count, width), BF16),
        compiler_params=params(),
        cost_estimate=cost(8_000_000_000, 15_000_000),
        name="block_out",
    )(ends, tok, gated, w_out)


def run_part(dgate, rest_a, w_gate, w_conv):
    count = dgate.shape[0]
    width = w_conv.shape[0]
    return pl.pallas_call(
        part_kernel,
        grid=(count // TAIL,),
        in_specs=[
            tail_rows(dgate.shape[1]),
            tail_rows(rest_a.shape[1]),
            whole(w_gate.shape),
            pl.BlockSpec((width, rest_a.shape[1]), lambda i: (0, 0)),
        ],
        out_specs=tail_rows(width),
        out_shape=jax.ShapeDtypeStruct((count, width), F32),
        compiler_params=params(),
        cost_estimate=cost(10_000_000_000, 20_000_000),
        name="grad_normed_part",
    )(dgate, rest_a, w_gate, w_conv)


def run_norm(tok, cot, part, rest_b, w_conv, norm_gain):
    count, width = tok.shape
    return pl.pallas_call(
        norm_kernel,
        grid=(count // TAIL,),
        in_specs=[
            tail_rows(width),
            tail_rows(width),
            tail_rows(width),
            tail_rows(rest_b.shape[1]),
            whole(w_conv.shape),
            whole(norm_gain.shape),
        ],
        out_specs=tail_rows(width),
        out_shape=jax.ShapeDtypeStruct((count, width), BF16),
        compiler_params=params(),
        cost_estimate=cost(10_000_000_000, 20_000_000),
        name="norm_backward",
    )(tok, cot, part, rest_b, w_conv, norm_gain)


def pad_lanes(v):
    return jnp.pad(v, ((0, 0), (0, LANES - v.shape[1])))


def swap(v, mask):
    n = lax.axis_size("rep") * lax.axis_size("shard")
    return lax.ppermute(v, ("rep", "shard"), [(i, i ^ mask) for i in range(n)])


def place():
    return lax.axis_index("rep") * lax.axis_size("shard") + lax.axis_index("shard")


SHARD, CORE = 1, 2


def half_rows(v):
    half = v.shape[0] // 2
    core = (place() // CORE) % 2
    return lax.dynamic_slice_in_dim(v, core * half, half, 0)


def take(v, index):
    return lax.dynamic_index_in_dim(v, index, 0, keepdims=False)


def exchanges():
    n = lax.axis_size("rep") * lax.axis_size("shard")
    bits = [SHARD]
    bit = 2 * CORE
    while bit < n:
        bits.append(bit)
        bit *= 2
    return bits


def at_bit(bit):
    return (place() // bit) % 2


def cut(v, bit):
    if v.ndim == 2:
        v = v.reshape(2, v.shape[0] // 2, v.shape[1])
    me = at_bit(bit)
    return take(v, me), take(v, 1 - me).astype(BF16)


def add(kept, got):
    return kept + got.astype(F32)


def both_sum(low, bit):
    return (low.astype(F32) + swap(low, bit).astype(F32)).astype(BF16)


def join(low, got, bit):
    return jnp.where(at_bit(bit) == 0, jnp.concatenate([low, got], 0), jnp.concatenate([got, low], 0))


def core_sum(g):
    rows, n = g.shape
    v = g.reshape(2, 2, rows // 4, n)
    core = (place() // CORE) % 2
    other = lax.dynamic_index_in_dim(v, 1 - core, 1, keepdims=False).astype(BF16)
    kept = lax.dynamic_index_in_dim(v, core, 1, keepdims=False)
    return kept + swap(other, CORE).astype(F32)


def after(gate, *values):
    return lax.optimization_barrier((gate, *values))


def per_device(
    tokens,
    cotangent,
    seq_lengths,
    seq_device,
    norm_gain,
    in_weight,
    conv_weight,
    conv_bias,
    step_bias,
    decay_log,
    skip_gain,
    gate_gain,
    out_weight,
):
    shards = lax.axis_size("shard")
    shard = lax.axis_index("shard")
    device = lax.axis_index("rep") * shards + shard
    half_count = seq_lengths.shape[0] // 2
    owned = seq_device[:half_count] == device
    first_len = jnp.sum(jnp.where(owned, seq_lengths[:half_count], 0))
    second_len = jnp.sum(jnp.where(owned, seq_lengths[half_count:], 0))
    ends = jnp.stack(
        [first_len, first_len + second_len, lax.axis_index("rep") % 2, shard]
    ).astype(jnp.int32)
    count, width = tokens.shape
    inner = gate_gain.shape[0] * shards
    channels = conv_weight.shape[1] * shards
    head_count = step_bias.shape[0] * shards
    size = inner // head_count
    taps = conv_weight.shape[0]

    small = (norm_gain, conv_weight.reshape(-1), conv_bias, step_bias, decay_log, skip_gain, gate_gain)
    sizes = [v.shape[0] for v in small]
    own = jnp.concatenate(small)
    own = jnp.pad(own, (0, -own.shape[0] % 1024)).reshape(-1, LANES)
    in_half = half_rows(in_weight)
    conv_far = swap(in_half[:, inner:], SHARD)
    other = swap(own, SHARD)
    conv_near = swap(conv_far, CORE)
    conv_near, gate_send, out_send = after(conv_near, in_half[:, :inner], half_rows(out_weight))
    gate_far = swap(gate_send, SHARD)
    out_far = swap(out_send, SHARD)

    packed = jnp.where(shard == 0, jnp.stack([own, other]), jnp.stack([other, own])).reshape(2, -1)
    parts = []
    at = 0
    for n in sizes:
        parts.append(packed[:, at : at + n])
        at += n
    full_norm, _, full_shift, full_step, full_decay, full_skip, full_gate = [
        p.reshape(-1).astype(F32) for p in parts
    ]
    conv_w = parts[1].reshape(shards, taps, -1).transpose(1, 0, 2).reshape(taps, -1).astype(F32)
    conv_b = full_shift[None, :]
    norm_row = full_norm[None, :]
    gate_row = full_gate[None, :]
    lane_head = lax.broadcasted_iota(jnp.int32, (inner, LANES), 0) // size
    heads = (lane_head == lax.broadcasted_iota(jnp.int32, (inner, LANES), 1)).astype(BF16)
    skip = jnp.repeat(full_skip, size)[None, :]
    step_row = pad_lanes(full_step[None, :])
    neg_rate = pad_lanes(-jnp.exp(full_decay)[None, :])

    normed, u, conv_in, raw, y, states, w_conv = run_scan(
        ends, tokens, in_weight, conv_far, conv_near, norm_row, conv_w, conv_b, step_row, neg_rate, inner
    )
    normed, gate_far, out_far = after(normed, gate_far, out_far)
    gate_near = swap(gate_far, CORE)
    out_near = swap(out_far, CORE)
    w_gate, w_out, gated, masked, dy, dgate, s1, gain8, skip8 = run_gate(
        ends, cotangent, normed, u, y, in_weight, gate_far, gate_near, out_weight, out_far, out_near, skip, gate_row, heads
    )
    bits = exchanges()
    far, last_bit = bits[1:-1], bits[-1]
    g_out = dot(gated, masked, ((0,), (0,)))
    h_out = core_sum(g_out)
    g_out, normed = after(g_out, normed)
    g_gate = dot(normed, dgate, ((0,), (0,)))
    h_gate = core_sum(g_gate)
    quarter = h_out.shape[1] // 2
    held = jnp.concatenate([h_out[:, :quarter], h_out[:, quarter:], h_gate], axis=2)
    half_pairs = inner // LANES // 2
    shared = (s1, states, conv_w, step_row, neg_rate, skip, heads)

    kept, sent = cut(held, SHARD)
    dy, sent = after(dy, sent)
    got = swap(sent, SHARD)
    carry = run_backward(0, half_pairs, None, None, ends, u, conv_in, raw, dy, *shared)
    first_out, kept, got = after(carry[0], kept, got)
    kept, sent = cut(add(kept, got), far[0])
    dy, sent = after(dy, sent)
    got = swap(sent, far[0])
    rest_a, part, cw_a, cb_a, _, dl_a, _, _ = run_backward(
        0, half_pairs, None, (first_out, *carry[1:]), ends, u, conv_in, raw, dy, *shared
    )
    rest_a, kept, got = after(rest_a, kept, got)
    g_a = dot(normed, rest_a, ((0,), (0,)))
    held = add(kept, got)
    kept, sent = cut(held, far[1])
    kept_a, sent_a = cut(core_sum(g_a), SHARD)
    part, sent, sent_a = after(part, sent, sent_a)
    got = swap(sent, far[1])
    got_a = swap(sent_a, SHARD)
    carry = run_backward(half_pairs, half_pairs, part, None, ends, u, conv_in, raw, dy, *shared)
    first_out, kept, got, kept_a, got_a = after(carry[0], kept, got, kept_a, got_a)
    held = add(kept, got)
    for bit in far[2:]:
        kept, sent = cut(held, bit)
        held = add(kept, swap(sent, bit))
    low = held.astype(BF16)
    kept_a, sent_a = cut(add(kept_a, got_a), far[0])
    part, low, sent_a = after(part, low, sent_a)
    got = swap(low, last_bit)
    got_a = swap(sent_a, far[0])
    rest_b, _, cw_b, cb_b, sb_b, dl_b, _, _ = run_backward(
        half_pairs, half_pairs, part, (first_out, *carry[1:]), ends, u, conv_in, raw, dy, *shared
    )
    rest_b, low, got, kept_a, got_a = after(rest_b, low, got, kept_a, got_a)
    g_b = dot(normed, rest_b, ((0,), (0,)))

    g_conv = jnp.sum(jnp.concatenate([cw_a, cw_b], 1).reshape(taps, 8, channels), axis=1)
    g_shift = jnp.sum(jnp.concatenate([cb_a, cb_b], 1), axis=0)
    g_step = jnp.sum(sb_b, axis=0)[:head_count]
    g_decay = jnp.sum(dl_a + dl_b, axis=0)[:head_count]
    g_skip = jnp.sum(skip8.reshape(8, head_count, size), axis=(0, 2))
    g_gain = jnp.sum(gain8, axis=0)
    pieces = (
        g_conv.reshape(taps, shards, -1).transpose(1, 0, 2).reshape(shards, -1),
        g_shift.reshape(shards, -1),
        g_step.reshape(shards, -1),
        g_decay.reshape(shards, -1),
        g_skip.reshape(shards, -1),
        g_gain.reshape(shards, -1),
    )
    flat = jnp.concatenate(pieces, axis=1)
    flat = jnp.pad(flat, ((0, 0), (0, -flat.shape[1] % 1024))).reshape(shards, -1, LANES)
    rest_b, flat = after(rest_b, flat)
    flat = flat + swap(flat, CORE)
    low = add(low.astype(F32), got).astype(BF16)
    held_a = add(kept_a, got_a)
    kept_b, sent_b = cut(core_sum(g_b), SHARD)
    backs = far[::-1] + [CORE]
    mine, sent_s = take(flat, at_bit(SHARD)), take(flat, 1 - at_bit(SHARD))
    gated, low, sent_b, sent_s = after(gated, low, sent_b, sent_s)
    got_s = swap(sent_s, SHARD)
    got = swap(low, backs[0])
    got_b = swap(sent_b, SHARD)
    block_out = run_out(ends, tokens, gated, w_out)
    block_out, low, got, kept_b, got_b, got_s = after(block_out, low, got, kept_b, got_b, got_s)
    mine = mine + got_s
    low = join(low, got, backs[0])
    kept_b, sent_b = cut(add(kept_b, got_b), far[0])
    dgate, low, sent_b, mine = after(dgate, low, sent_b, mine)
    got_s = swap(mine, far[0])
    got = swap(low, backs[1])
    got_b = swap(sent_b, far[0])
    grad_part = run_part(dgate, rest_a, w_gate, w_conv)
    grad_part, low, got, kept_b, got_b, got_s = after(grad_part, low, got, kept_b, got_b, got_s)
    mine = mine + got_s
    low = join(low, got, backs[1])
    held_b = jnp.concatenate([held_a, add(kept_b, got_b)], axis=1)
    kept_b, sent_b = cut(held_b, far[1])
    grad_part, low, sent_b, mine = after(grad_part, low, sent_b, mine)
    got_s = swap(mine, far[1])
    got = swap(low, backs[2])
    got_b = swap(sent_b, far[1])
    grad_tokens = run_norm(tokens, cotangent, grad_part, rest_b, w_conv, norm_row)
    grad_tokens, low, got, kept_b, got_b, got_s = after(grad_tokens, low, got, kept_b, got_b, got_s)
    mine = mine + got_s
    for bit in far[2:] + [last_bit]:
        mine = mine + swap(mine, bit)
    low = join(low, got, backs[2])
    for bit in backs[3:]:
        low = join(low, swap(low, bit), bit)
    held_b = add(kept_b, got_b)
    for bit in far[2:]:
        kept_b, sent_b = cut(held_b, bit)
        held_b = add(kept_b, swap(sent_b, bit))
    low_b = both_sum(held_b.astype(BF16), last_bit)
    for bit in backs:
        low_b = join(low_b, swap(low_b, bit), bit)
    near = out_weight.shape[1]
    by_core = low.reshape(2, low.shape[0] // 2, low.shape[1])
    t_out = jnp.concatenate(
        [by_core[0, :, :near], by_core[0, :, near : 2 * near], by_core[1, :, :near], by_core[1, :, near : 2 * near]], axis=0
    )
    gate_sum = low[:, 2 * near :]
    rest_sum = low_b[:, : channels + head_count]
    t_in = jnp.concatenate([gate_sum, rest_sum], axis=1).astype(F32)
    t_norm = jnp.sum(gate_sum.astype(F32) * in_weight[:, :inner].astype(F32), axis=1)
    t_norm = t_norm + jnp.sum(rest_sum.astype(F32) * in_weight[:, inner:].astype(F32), axis=1)
    t_norm = t_norm / norm_gain.astype(F32)
    mine = mine.reshape(-1)
    outs = []
    at = 0
    for n in sizes[1:]:
        outs.append(mine[at : at + n])
        at += n
    return (
        block_out,
        grad_tokens,
        t_norm,
        t_in,
        outs[0].reshape(taps, -1),
        outs[1],
        outs[2],
        outs[3],
        outs[4],
        outs[5],
        t_out.astype(F32),
    )


def solution(mesh):
    in_specs = (
        P(("rep", "shard"), None),
        P(("rep", "shard"), None),
        P(),
        P(),
        P("shard"),
        P("shard", None),
        P(None, "shard"),
        P("shard"),
        P("shard"),
        P("shard"),
        P("shard"),
        P("shard"),
        P("shard", None),
    )
    out_specs = (
        P(("rep", "shard"), None),
        P(("rep", "shard"), None),
        P("shard"),
        P("shard", None),
        P(None, "shard"),
        P("shard"),
        P("shard"),
        P("shard"),
        P("shard"),
        P("shard"),
        P("shard", None),
    )
    return jax.shard_map(
        per_device, mesh=mesh, in_specs=in_specs, out_specs=out_specs, check_vma=False
    )
```

```python
import functools

import jax
import jax.numpy as jnp
from jax import lax
from jax.experimental import pallas as pl
from jax.experimental.pallas import tpu as pltpu
from jax.sharding import PartitionSpec as P

ROWS = 256
CHUNK = 128
TAIL = 512
LANES = 128
LOG2E = 1.4426950408889634
F32 = jnp.float32
BF16 = jnp.bfloat16
HIGH = lax.Precision.HIGHEST
VMEM_LIMIT = 60 * 1024 * 1024


def dot(a, b, dims=((1,), (0,)), precision=None):
    return lax.dot_general(a, b, (dims, ((), ())), precision=precision, preferred_element_type=F32)


def fold8(v):
    return jnp.sum(v.reshape(v.shape[0] // 8, 8, v.shape[1]), axis=0)


def segment_of(position, first_end, second_end):
    return (position >= first_end).astype(jnp.int32) + (position >= second_end).astype(jnp.int32)


def softplus(v):
    return jnp.maximum(v, 0.0) + jnp.log1p(jnp.exp(-jnp.abs(v)))


def head_sums(v, heads):
    high = v.astype(BF16)
    low = (v - high.astype(F32)).astype(BF16)
    return dot(high, heads) + dot(low, heads)


def lane_pair(v, p, lane_low):
    shape = lane_low.shape
    a = jnp.broadcast_to(v[:, 2 * p : 2 * p + 1], shape)
    b = jnp.broadcast_to(v[:, 2 * p + 1 : 2 * p + 2], shape)
    return a, b


def split_rows(pair, lane_low):
    zero = jnp.zeros_like(pair)
    return jnp.concatenate(
        [jnp.where(lane_low, pair, zero), jnp.where(lane_low, zero, pair)], axis=0
    )


def chunk_setup(raw, step_bias, neg_rate, start, first_end, second_end):
    row = lax.broadcasted_iota(jnp.int32, (CHUNK, LANES), 0)
    col = lax.broadcasted_iota(jnp.int32, (CHUNK, LANES), 1)
    step = softplus(raw + step_bias)
    rate = neg_rate * step
    lower = (row >= col).astype(F32)
    cum = dot(lower, rate, precision=HIGH) * LOG2E
    seg_row = segment_of(row + start, first_end, second_end)
    seg_col = segment_of(col + start, first_end, second_end)
    last_seg = segment_of(start - 1, first_end, second_end)
    end_seg = segment_of(start + CHUNK - 1, first_end, second_end)
    entry = (seg_row == last_seg).astype(F32)
    tail = (seg_row == end_seg).astype(F32)
    keep = (last_seg == end_seg).astype(F32)
    same = seg_row == seg_col
    return row, col, step, rate, cum, same, entry, tail, keep


def place_rows(dst, width, local, far, near, core, shard):
    half = far.shape[0]
    own_at = pl.multiple_of(shard * (2 * half), half)
    other_at = (1 - shard) * (2 * half)
    dst[pl.ds(own_at, 2 * half), :width] = local
    dst[pl.ds(pl.multiple_of(other_at + core * half, half), half), :width] = far[...]
    dst[pl.ds(pl.multiple_of(other_at + (1 - core) * half, half), half), :width] = near[...]


def scan_kernel(
    ends,
    tok,
    w_local,
    w_far,
    w_near,
    norm_gain,
    conv_w,
    conv_b,
    step_bias,
    neg_rate,
    normed_out,
    u_out,
    conv_in_out,
    raw_out,
    y_out,
    state_out,
    w_conv,
    ext,
    xs,
    bc,
    wx_s,
    keep_s,
    state,
):
    step_id = pl.program_id(0)
    first_end = ends[0]
    second_end = ends[1]
    inner = xs.shape[1]
    channels = ext.shape[0] * LANES
    pairs = inner // LANES
    base = step_id * ROWS

    @pl.when(step_id == 0)
    def _():
        w_conv[:, channels:] = jnp.zeros((w_conv.shape[0], LANES), BF16)
        used = w_far.shape[1]
        place_rows(w_conv, used, w_local[:, inner:], w_far, w_near, ends[2], ends[3])
        ext[:, 0:8, :] = jnp.zeros((channels // LANES, 8, LANES), F32)
        state[...] = jnp.zeros_like(state)

    rows = tok[...].astype(F32)
    scale = lax.rsqrt(jnp.mean(rows * rows, axis=-1, keepdims=True) + 1e-05)
    normed = (rows * scale * norm_gain[...]).astype(BF16)
    normed_out[...] = normed
    raw_out[...] = dot(normed, w_conv[:, channels:])

    pos = lax.broadcasted_iota(jnp.int32, (ROWS, LANES), 0) + base
    seg = segment_of(pos, first_end, second_end)
    shift_mask = [
        ((segment_of(pos - k, first_end, second_end) == seg) & (pos >= k)).astype(F32)
        for k in range(1, 4)
    ]

    def conv_tile(ct):
        cols = slice(ct * LANES, (ct + 1) * LANES)
        if ct % 2 == 0:
            wide = slice(ct * LANES, (ct + 2) * LANES)
            conv_in = dot(normed, w_conv[:, wide])
            ext[ct, 8 : 8 + ROWS, :] = conv_in[:, :LANES]
            ext[ct + 1, 8 : 8 + ROWS, :] = conv_in[:, LANES:]
            conv_in_out[:, wide] = conv_in.astype(BF16)
        total = conv_b[:, cols] + conv_w[3:4, cols] * ext[ct, 8 : 8 + ROWS, :]
        for k in range(1, 4):
            total += (conv_w[3 - k : 4 - k, cols] * ext[ct, 8 - k : 8 - k + ROWS, :]) * shift_mask[k - 1]
        u = total.astype(BF16)
        u_out[:, cols] = u
        half = 0.5 * u.astype(F32)
        return half + half * jnp.tanh(half)

    for ct in range(pairs):
        xs[:, ct * LANES : (ct + 1) * LANES] = conv_tile(ct)
    for ct in range(pairs, channels // LANES):
        bc[:, (ct - pairs) * LANES : (ct - pairs + 1) * LANES] = conv_tile(ct)
    ext[:, 0:8, :] = ext[:, ROWS : ROWS + 8, :]

    def chunk(q, carry):
        r0 = pl.multiple_of(q * CHUNK, CHUNK)
        rsl = pl.ds(r0, CHUNK)
        row, col, step, rate, cum, same, entry, tail, keep = chunk_setup(
            raw_out[rsl, :], step_bias[...], neg_rate[...], base + r0, first_end, second_end
        )
        cum_t = cum.T
        shift_t = cum_t - jnp.log2(step.T)
        tail_t = (segment_of(col + (base + r0), first_end, second_end) == segment_of(base + r0 + CHUNK - 1, first_end, second_end)).astype(F32)
        weight_t = jnp.exp2(cum_t[:, CHUNK - 1 : CHUNK] - shift_t) * tail_t
        lane_low = col < (LANES // 2)
        b_f = bc[rsl, 0:LANES]
        b_t = b_f.T
        b_low = b_f.astype(BF16)
        c_low = bc[rsl, LANES : 2 * LANES].astype(BF16)
        gram = dot(c_low, b_low, ((1,), (1,)))
        gram = jnp.where(same & (row >= col), gram, 0.0)
        state_low = state[...].astype(BF16)
        state_out[q] = state_low
        y_out[rsl, :] = dot(c_low, state_low)
        for p in range(pairs):
            cols = slice(p * LANES, (p + 1) * LANES)
            ca, cb = lane_pair(cum, p, lane_low)
            ma = (jnp.exp2(jnp.minimum(ca - shift_t[2 * p : 2 * p + 1, :], 100.0)) * gram).astype(BF16)
            mb = (jnp.exp2(jnp.minimum(cb - shift_t[2 * p + 1 : 2 * p + 2, :], 100.0)) * gram).astype(BF16)
            ba = (b_t * weight_t[2 * p : 2 * p + 1, :]).astype(BF16)
            bb = (b_t * weight_t[2 * p + 1 : 2 * p + 2, :]).astype(BF16)
            x2 = split_rows(xs[rsl, cols].astype(BF16), lane_low)
            left = jnp.concatenate(
                [jnp.concatenate([ma, mb], axis=1), jnp.concatenate([ba, bb], axis=1)], axis=0
            )
            both_out = dot(left, x2)
            decay = jnp.exp2(jnp.where(lane_low, ca, cb))
            y_out[rsl, cols] = both_out[:CHUNK] + y_out[rsl, cols] * (decay * entry)
            state[:, cols] = state[:, cols] * (decay[CHUNK - 1 : CHUNK, :] * keep) + both_out[CHUNK:]
        return carry

    for at in range(ROWS // CHUNK):
        chunk(at, 0)


def gate_kernel(
    ends,
    cot,
    normed,
    u_in,
    y_in,
    w_local,
    gate_far,
    gate_near,
    out_local,
    out_far,
    out_near,
    skip,
    gate_gain,
    heads,
    w_gate,
    w_out,
    gated_out,
    masked_out,
    dy_out,
    dgate_out,
    s1_out,
    gain_grad,
    skip_grad,
    gate_s,
    xs,
    prod_s,
    dg_s,
):
    step_id = pl.program_id(0)
    second_end = ends[1]
    inner = gate_s.shape[1]
    pairs = inner // LANES
    base = step_id * ROWS

    @pl.when(step_id == 0)
    def _():
        place_rows(w_gate, inner, w_local[...], gate_far, gate_near, ends[2], ends[3])
        place_rows(w_out, w_out.shape[1], out_local[...], out_far, out_near, ends[2], ends[3])
        gain_grad[...] = jnp.zeros_like(gain_grad)
        skip_grad[...] = jnp.zeros_like(skip_grad)

    pos = lax.broadcasted_iota(jnp.int32, (ROWS, LANES), 0) + base
    live = (pos < second_end).astype(F32)
    masked = (cot[...].astype(F32) * live[:, 0:1]).astype(BF16)
    masked_out[...] = masked
    sq = jnp.zeros((ROWS, LANES), F32)
    cross = jnp.zeros((ROWS, LANES), F32)
    for ct in range(pairs):
        cols = slice(ct * LANES, (ct + 1) * LANES)
        if ct % 2 == 0:
            wide = slice(ct * LANES, (ct + 2) * LANES)
            gate_s[:, wide] = dot(normed[...], w_gate[:, wide])
            dg_s[:, wide] = dot(masked, w_out[wide, :], ((1,), (1,)))
        half = 0.5 * gate_s[:, cols]
        half_u = 0.5 * u_in[:, cols].astype(F32)
        x = half_u + half_u * jnp.tanh(half_u)
        xs[:, cols] = x
        product = (y_in[:, cols] + skip[:, cols] * x) * (half + half * jnp.tanh(half))
        prod_s[:, cols] = product
        sq += product * product
        cross += dg_s[:, cols] * gate_gain[:, cols] * product
    r = lax.rsqrt(jnp.sum(sq, axis=1, keepdims=True) / inner + 1e-05)
    m = jnp.sum(cross, axis=1, keepdims=True) / inner
    r_wide = jnp.broadcast_to(r, (ROWS, LANES))
    m_wide = jnp.broadcast_to(r * r * r * m, (ROWS, LANES))
    for ct in range(pairs):
        cols = slice(ct * LANES, (ct + 1) * LANES)
        g = gate_s[:, cols]
        sig = 0.5 + 0.5 * jnp.tanh(0.5 * g)
        act = g * sig
        x = xs[:, cols]
        y = y_in[:, cols]
        product = prod_s[:, cols]
        pr = product * r_wide
        gated_out[:, cols] = (pr * gate_gain[:, cols]).astype(BF16)
        dg = dg_s[:, cols]
        gain_grad[:, cols] += fold8(dg * pr)
        dprod = r_wide * (dg * gate_gain[:, cols]) - product * m_wide
        dsc = dprod * act
        dgate_out[:, cols] = (
            dprod * (y + skip[:, cols] * x) * (sig + act * (1.0 - sig))
        ).astype(BF16)
        dy = dsc.astype(BF16)
        dy_out[:, cols] = dy
        skip_grad[:, cols] += fold8(dsc * x)
        prod_s[:, cols] = dy.astype(F32) * y
    s1_out[...] = head_sums(prod_s[...], heads[...])


def backward_kernel(
    first_pair,
    pairs,
    with_bc,
    last,
    resumed,
    ends,
    u_in,
    conv_in,
    ubc_in,
    cbc_in,
    raw_in,
    dy_in,
    s1_in,
    state_in,
    part_in,
    conv_w,
    step_bias,
    neg_rate,
    skip,
    heads,
    *refs,
):
    carried = refs[:8] if resumed else None
    refs = refs[8:] if resumed else refs
    (
        dconv_out,
        part_out,
        conv_w_grad,
        conv_b_grad,
        step_grad,
        decay_grad,
        dstate,
        halo,
        ext,
        xs,
        bc,
        slope,
        bds,
        q_s,
        wx_s,
        rows_s,
    ) = refs
    step_id = pl.program_id(0)
    first_end = ends[0]
    second_end = ends[1]
    inner = pairs * LANES
    channels = ext.shape[0] * LANES
    base = (last - step_id) * ROWS

    @pl.when(step_id == 0)
    def _():
        sums = (conv_w_grad, conv_b_grad, step_grad, decay_grad, dstate, halo)
        for at, ref in enumerate(sums):
            ref[...] = carried[2 + at][...] if resumed else jnp.zeros_like(ref)
        for ct in range(channels // LANES):
            ext[ct, ROWS : ROWS + 8, :] = halo[:, ct * LANES : (ct + 1) * LANES]
        rows_s[...] = jnp.zeros_like(rows_s)

    for ct in range(pairs + 2):
        if ct < pairs:
            u = u_in[:, ct * LANES : (ct + 1) * LANES].astype(F32)
        else:
            u = ubc_in[:, (ct - pairs) * LANES : (ct - pairs + 1) * LANES].astype(F32)
        sig = 0.5 + 0.5 * jnp.tanh(0.5 * u)
        act = u * sig
        if ct < pairs or with_bc:
            slope[:, ct * LANES : (ct + 1) * LANES] = sig + act * (1.0 - sig)
        if ct < pairs:
            xs[:, ct * LANES : (ct + 1) * LANES] = act.astype(BF16)
        else:
            bc[:, (ct - pairs) * LANES : (ct - pairs + 1) * LANES] = act

    def chunk(k, carry):
        q = ROWS // CHUNK - 1 - k
        r0 = pl.multiple_of(q * CHUNK, CHUNK)
        rsl = pl.ds(r0, CHUNK)
        raw = raw_in[rsl, :]
        row, col, step, rate, cum, same, entry, tail, keep = chunk_setup(
            raw, step_bias[...], neg_rate[...], base + r0, first_end, second_end
        )
        cum_t = cum.T
        shift = cum - jnp.log2(step)
        last_seg = segment_of(base + r0 - 1, first_end, second_end)
        entry_t = (segment_of(col + (base + r0), first_end, second_end) == last_seg).astype(F32)
        enter_t = jnp.exp2(cum_t) * entry_t
        lane_low = col < (LANES // 2)
        b_f = bc[rsl, 0:LANES]
        b_low = b_f.astype(BF16)
        c_f = bc[rsl, LANES : 2 * LANES]
        c_low = c_f.astype(BF16)
        c_t = c_f.T
        allowed = same & (row <= col)
        gram = jnp.where(allowed, dot(b_low, c_low, ((1,), (1,))), 0.0)
        dstate_low = dstate[...].astype(BF16)
        bds[...] = dot(b_low, dstate_low)
        dgram = jnp.zeros((CHUNK, CHUNK), F32)
        dc_t = jnp.zeros((LANES, CHUNK), F32)
        for p in range(pairs):
            cols = slice(p * LANES, (p + 1) * LANES)
            head = 2 * (p + first_pair)
            ca, cb = lane_pair(shift, p + first_pair, lane_low)
            la = jnp.exp2(jnp.minimum(cum_t[head : head + 1, :] - ca, 100.0))
            lb = jnp.exp2(jnp.minimum(cum_t[head + 1 : head + 2, :] - cb, 100.0))
            both = jnp.where(lane_low, ca, cb)
            ea, eb = lane_pair(cum[CHUNK - 1 : CHUNK, :], p + first_pair, lane_low[0:1, :])
            end = jnp.where(lane_low[0:1, :], ea, eb)
            dy_low = dy_in[rsl, cols]
            dy = dy_low.astype(F32)
            dy2 = split_rows(dy_low, lane_low)
            x_low = xs[rsl, cols]
            state_low = state_in[q, :, cols]
            top = dot(jnp.concatenate([x_low, state_low], axis=0), dy2, ((1,), (1,)))
            enter_a = enter_t[head : head + 1, :]
            enter_b = enter_t[head + 1 : head + 2, :]
            dgram += top[:CHUNK, :CHUNK] * la + top[:CHUNK, CHUNK:] * lb
            dc_t += top[CHUNK:, :CHUNK] * enter_a + top[CHUNK:, CHUNK:] * enter_b
            left = jnp.concatenate(
                [
                    jnp.concatenate([(la * gram).astype(BF16), (lb * gram).astype(BF16)], axis=1),
                    jnp.concatenate([(c_t * enter_a).astype(BF16), (c_t * enter_b).astype(BF16)], axis=1),
                ],
                axis=0,
            )
            down = dot(left, dy2)
            weight = jnp.exp2(end - both) * tail
            gxs = weight * bds[:, cols]
            gx = down[:CHUNK] + gxs
            x = x_low.astype(F32)
            q_s[:, cols] = x * gx
            ext[p, rsl, :] = (gx + skip[:, cols] * dy) * slope[rsl, cols]
            wx_s[:, cols] = (x * weight).astype(BF16)
            keep_row = jnp.exp2(end) * keep
            old = dstate[:, cols]
            rows_s[0:8, cols] = fold8(x * gxs) + keep_row * fold8(old * state_low.astype(F32))
            dstate[:, cols] = old * keep_row + down[CHUNK:]
        dgram = jnp.where(allowed, dgram, 0.0)
        dc = (dc_t + dot(b_f.T.astype(BF16), dgram.astype(BF16))).T
        db = dot(dgram.astype(BF16), c_low) + dot(wx_s[...], dstate_low, ((1,), (1,)))
        if with_bc:
            bsl = slice(inner, inner + LANES)
            csl = slice(inner + LANES, inner + 2 * LANES)
            ext[pairs, rsl, :] = (db + part_in[rsl, 0:LANES]) * slope[rsl, bsl]
            ext[pairs + 1, rsl, :] = (dc + part_in[rsl, LANES : 2 * LANES]) * slope[rsl, csl]
        else:
            part_out[rsl, 0:LANES] = db
            part_out[rsl, LANES : 2 * LANES] = dc
        sx = head_sums(q_s[...], heads[...])
        end_term = jnp.sum(head_sums(rows_s[0:8, :], heads[...]), axis=0, keepdims=True)
        upper = (row <= col).astype(F32)
        drate = dot(upper, s1_in[rsl, :] - sx, precision=HIGH) + end_term
        own = (col >= 2 * first_pair) & (col < 2 * (first_pair + pairs))
        drate = jnp.where(own, drate, 0.0)
        dstep = sx / jnp.maximum(step, 1e-37) + neg_rate[...] * drate
        draw = dstep * jax.nn.sigmoid(raw + step_bias[...])
        if with_bc:
            draw = draw + part_in[rsl, 2 * LANES : 3 * LANES]
            dconv_out[rsl, channels : channels + LANES] = draw.astype(BF16)
            step_grad[...] += fold8(draw)
        else:
            part_out[rsl, 2 * LANES : 3 * LANES] = draw
        decay_grad[...] += fold8(drate * rate)
        return carry

    for at in range(ROWS // CHUNK):
        chunk(at, 0)

    pos = lax.broadcasted_iota(jnp.int32, (ROWS, LANES), 0) + base
    seg = segment_of(pos, first_end, second_end)
    shift_mask = [
        (segment_of(pos + k, first_end, second_end) == seg).astype(F32) for k in range(1, 4)
    ]
    for ct in range(channels // LANES):
        cols = slice(ct * LANES, (ct + 1) * LANES)
        du = ext[ct, 0:ROWS, :]
        if ct < pairs:
            source = conv_in[:, cols].astype(F32)
        else:
            source = cbc_in[:, (ct - pairs) * LANES : (ct - pairs + 1) * LANES].astype(F32)
        conv_b_grad[:, cols] += fold8(du)
        conv_w_grad[24:32, cols] += fold8(source * du)
        total = conv_w[3:4, cols] * du
        for k in range(1, 4):
            later = ext[ct, k : k + ROWS, :] * shift_mask[k - 1]
            total += conv_w[3 - k : 4 - k, cols] * later
            conv_w_grad[8 * (3 - k) : 8 * (4 - k), cols] += fold8(source * later)
        dconv_out[:, cols] = total.astype(BF16)
    for ct in range(channels // LANES):
        first = ext[ct, 0:8, :]
        ext[ct, ROWS : ROWS + 8, :] = first
        halo[:, ct * LANES : (ct + 1) * LANES] = first


def out_kernel(ends, tok, gated, w_out, block_out):
    pos = lax.broadcasted_iota(jnp.int32, (TAIL, 1), 0) + pl.program_id(0) * TAIL
    live = (pos < ends[1]).astype(F32)
    block_out[...] = (tok[...].astype(F32) + live * dot(gated[...], w_out[...])).astype(BF16)


def part_kernel(dgate, rest_a, w_gate, w_conv, grad):
    grad[...] = dot(dgate[...], w_gate[...], ((1,), (1,))) + dot(rest_a[...], w_conv[...], ((1,), (1,)))


def norm_kernel(tok, cot, part, rest_b, w_conv, norm_gain, grad_tokens):
    split = w_conv.shape[1] - rest_b.shape[1]
    grad = part[...] + dot(rest_b[...], w_conv[:, split:], ((1,), (1,)))
    rows = tok[...].astype(F32)
    r = lax.rsqrt(jnp.mean(rows * rows, axis=-1, keepdims=True) + 1e-05)
    n = rows * r
    weighted = norm_gain[...] * grad
    mean = jnp.mean(weighted * n, axis=-1, keepdims=True)
    grad_tokens[...] = (r * (weighted - n * mean) + cot[...].astype(F32)).astype(BF16)


def whole(shape):
    return pl.BlockSpec(shape, lambda i: (0,) * len(shape))


def params():
    return pltpu.CompilerParams(dimension_semantics=("arbitrary",), vmem_limit_bytes=VMEM_LIMIT)


def cost(flops, moved):
    return pl.CostEstimate(flops=flops, bytes_accessed=moved, transcendentals=20_000_000)


SMEM = pl.BlockSpec(memory_space=pltpu.SMEM)


def run_scan(ends, tok, w_local, w_far, w_near, norm_gain, conv_w, conv_b, step_bias, neg_rate, inner):
    count, width = tok.shape
    channels = conv_w.shape[1]
    per = ROWS // CHUNK

    def rows_of(n):
        return pl.BlockSpec((ROWS, n), lambda i: (i, 0))

    shape = jax.ShapeDtypeStruct
    return pl.pallas_call(
        scan_kernel,
        grid=(count // ROWS,),
        in_specs=[SMEM, rows_of(width)]
        + [
            whole(v.shape)
            for v in (w_local, w_far, w_near, norm_gain, conv_w, conv_b, step_bias, neg_rate)
        ],
        out_specs=[
            rows_of(width),
            rows_of(channels),
            rows_of(channels),
            rows_of(LANES),
            rows_of(inner),
            pl.BlockSpec((per, LANES, inner), lambda i: (i, 0, 0)),
            whole((width, channels + LANES)),
        ],
        out_shape=[
            shape((count, width), BF16),
            shape((count, channels), BF16),
            shape((count, channels), BF16),
            shape((count, LANES), F32),
            shape((count, inner), F32),
            shape((count // CHUNK, LANES, inner), BF16),
            shape((width, channels + LANES), BF16),
        ],
        scratch_shapes=[
            pltpu.VMEM((channels // LANES, ROWS + 8, LANES), F32),
            pltpu.VMEM((ROWS, inner), F32),
            pltpu.VMEM((ROWS, 2 * LANES), F32),
            pltpu.VMEM((CHUNK, inner), BF16),
            pltpu.VMEM((8, inner), F32),
            pltpu.VMEM((LANES, inner), F32),
        ],
        compiler_params=params(),
        cost_estimate=cost(50_000_000_000, 50_000_000),
        name="mixer_scan",
    )(ends, tok, w_local, w_far, w_near, norm_gain, conv_w, conv_b, step_bias, neg_rate)


def run_gate(ends, cot, normed, u, y, w_local, gate_far, gate_near, out_local, out_far, out_near, skip, gate_gain, heads):
    count, width = cot.shape
    inner = y.shape[1]

    def rows_of(n):
        return pl.BlockSpec((ROWS, n), lambda i: (i, 0))

    shape = jax.ShapeDtypeStruct
    return pl.pallas_call(
        gate_kernel,
        grid=(count // ROWS,),
        in_specs=[SMEM, rows_of(width), rows_of(width), rows_of(inner), rows_of(inner)]
        + [pl.BlockSpec((w_local.shape[0], inner), lambda i: (0, 0))]
        + [
            whole(v.shape)
            for v in (gate_far, gate_near, out_local, out_far, out_near, skip, gate_gain, heads)
        ],
        out_specs=[
            whole((width, inner)),
            whole((inner, width)),
            rows_of(inner),
            rows_of(width),
            rows_of(inner),
            rows_of(inner),
            rows_of(LANES),
            whole((8, inner)),
            whole((8, inner)),
        ],
        out_shape=[
            shape((width, inner), BF16),
            shape((inner, width), BF16),
            shape((count, inner), BF16),
            shape((count, width), BF16),
            shape((count, inner), BF16),
            shape((count, inner), BF16),
            shape((count, LANES), F32),
            shape((8, inner), F32),
            shape((8, inner), F32),
        ],
        scratch_shapes=[pltpu.VMEM((ROWS, inner), F32) for _ in range(4)],
        compiler_params=params(),
        cost_estimate=cost(35_000_000_000, 50_000_000),
        name="gate_both_ways",
    )(ends, cot, normed, u, y, w_local, gate_far, gate_near, out_local, out_far, out_near, skip, gate_gain, heads)


def run_backward(first_pair, pairs, part, carried, ends, u, conv_in, raw, dy, s1, states, conv_w, step_bias, neg_rate, skip, heads):
    count, full_channels = u.shape
    full_inner = dy.shape[1]
    with_bc = part is not None
    inner = pairs * LANES
    channels = inner + (2 * LANES if with_bc else 0)
    per = ROWS // CHUNK
    steps = count // ROWS // 2
    resumed = carried is not None
    last = steps - 1 if resumed else 2 * steps - 1
    at = first_pair // pairs
    bc_at = full_inner // (2 * LANES)
    if part is None:
        part = jnp.zeros((8, LANES), F32)
        part_spec = whole(part.shape)
        part_out_shape = (count, 3 * LANES)
        width_out = channels
        own_taps = conv_w[:, first_pair * LANES : first_pair * LANES + inner]
    else:
        part_spec = pl.BlockSpec((ROWS, 3 * LANES), lambda i: (last - i, 0))
        part_out_shape = (8, LANES)
        width_out = channels + LANES
        own_taps = conv_w[:, first_pair * LANES :]

    def rows_of(n, c=0):
        return pl.BlockSpec((ROWS, n), lambda i: (last - i, c))

    shape = jax.ShapeDtypeStruct
    sums = ((32, channels), (8, channels), (8, LANES), (8, LANES), (LANES, inner), (8, channels))
    in_specs = [
        SMEM,
        rows_of(inner, at),
        rows_of(inner, at),
        rows_of(2 * LANES, bc_at),
        rows_of(2 * LANES, bc_at),
        rows_of(LANES),
        rows_of(inner, at),
        rows_of(LANES),
        pl.BlockSpec((per, LANES, inner), lambda i: (last - i, 0, at)),
        part_spec,
        whole(own_taps.shape),
        whole(step_bias.shape),
        whole(neg_rate.shape),
        pl.BlockSpec((1, inner), lambda i: (0, at)),
        pl.BlockSpec((inner, LANES), lambda i: (at, 0)),
    ]
    args = [ends, u, conv_in, u, conv_in, raw, dy, s1, states, part, own_taps, step_bias, neg_rate, skip, heads]
    aliases = {}
    if resumed:
        aliases = {len(args): 0, len(args) + 1: 1}
        args += list(carried)
        in_specs += [pl.BlockSpec(memory_space=pl.ANY)] * 2 + [whole(s) for s in sums]
    return pl.pallas_call(
        functools.partial(backward_kernel, first_pair, pairs, with_bc, last, resumed),
        grid=(steps,),
        in_specs=in_specs,
        out_specs=[
            rows_of(width_out),
            whole(part_out_shape) if with_bc else rows_of(3 * LANES),
        ]
        + [whole(s) for s in sums],
        out_shape=[shape((count, width_out), BF16), shape(part_out_shape, F32)]
        + [shape(s, F32) for s in sums],
        scratch_shapes=[
            pltpu.VMEM((channels // LANES, ROWS + 8, LANES), F32),
            pltpu.VMEM((ROWS, inner), BF16),
            pltpu.VMEM((ROWS, 2 * LANES), F32),
            pltpu.VMEM((ROWS, channels), F32),
            pltpu.VMEM((CHUNK, inner), F32),
            pltpu.VMEM((CHUNK, inner), F32),
            pltpu.VMEM((CHUNK, inner), BF16),
            pltpu.VMEM((16, inner), F32),
        ],
        input_output_aliases=aliases,
        compiler_params=params(),
        cost_estimate=cost(25_000_000_000, 20_000_000),
        name=("backward_b" if with_bc else "backward_a") + ("_low" if resumed else "_high"),
    )(*args)


def tail_rows(n):
    return pl.BlockSpec((TAIL, n), lambda i: (i, 0))


def run_out(ends, tok, gated, w_out):
    count, width = tok.shape
    return pl.pallas_call(
        out_kernel,
        grid=(count // TAIL,),
        in_specs=[SMEM, tail_rows(width), tail_rows(gated.shape[1]), whole(w_out.shape)],
        out_specs=tail_rows(width),
        out_shape=jax.ShapeDtypeStruct((count, width), BF16),
        compiler_params=params(),
        cost_estimate=cost(8_000_000_000, 15_000_000),
        name="block_out",
    )(ends, tok, gated, w_out)


def run_part(dgate, rest_a, w_gate, w_conv):
    count = dgate.shape[0]
    width = w_conv.shape[0]
    return pl.pallas_call(
        part_kernel,
        grid=(count // TAIL,),
        in_specs=[
            tail_rows(dgate.shape[1]),
            tail_rows(rest_a.shape[1]),
            whole(w_gate.shape),
            pl.BlockSpec((width, rest_a.shape[1]), lambda i: (0, 0)),
        ],
        out_specs=tail_rows(width),
        out_shape=jax.ShapeDtypeStruct((count, width), F32),
        compiler_params=params(),
        cost_estimate=cost(10_000_000_000, 20_000_000),
        name="grad_normed_part",
    )(dgate, rest_a, w_gate, w_conv)


def run_norm(tok, cot, part, rest_b, w_conv, norm_gain):
    count, width = tok.shape
    return pl.pallas_call(
        norm_kernel,
        grid=(count // TAIL,),
        in_specs=[
            tail_rows(width),
            tail_rows(width),
            tail_rows(width),
            tail_rows(rest_b.shape[1]),
            whole(w_conv.shape),
            whole(norm_gain.shape),
        ],
        out_specs=tail_rows(width),
        out_shape=jax.ShapeDtypeStruct((count, width), BF16),
        compiler_params=params(),
        cost_estimate=cost(10_000_000_000, 20_000_000),
        name="norm_backward",
    )(tok, cot, part, rest_b, w_conv, norm_gain)


def pad_lanes(v):
    return jnp.pad(v, ((0, 0), (0, LANES - v.shape[1])))


def swap(v, mask):
    n = lax.axis_size("rep") * lax.axis_size("shard")
    return lax.ppermute(v, ("rep", "shard"), [(i, i ^ mask) for i in range(n)])


def place():
    return lax.axis_index("rep") * lax.axis_size("shard") + lax.axis_index("shard")


SHARD, CORE = 1, 2


def half_rows(v):
    half = v.shape[0] // 2
    core = (place() // CORE) % 2
    return lax.dynamic_slice_in_dim(v, core * half, half, 0)


def take(v, index):
    return lax.dynamic_index_in_dim(v, index, 0, keepdims=False)


def exchanges():
    n = lax.axis_size("rep") * lax.axis_size("shard")
    bits = [SHARD]
    bit = 2 * CORE
    while bit < n:
        bits.append(bit)
        bit *= 2
    return bits


def at_bit(bit):
    return (place() // bit) % 2


def cut(v, bit):
    if v.ndim == 2:
        v = v.reshape(2, v.shape[0] // 2, v.shape[1])
    me = at_bit(bit)
    return take(v, me), take(v, 1 - me).astype(BF16)


def add(kept, got):
    return kept + got.astype(F32)


def join(low, got, bit):
    return jnp.where(at_bit(bit) == 0, jnp.concatenate([low, got], 0), jnp.concatenate([got, low], 0))


def core_sum(g):
    rows, n = g.shape
    v = g.reshape(2, 2, rows // 4, n)
    core = (place() // CORE) % 2
    other = lax.dynamic_index_in_dim(v, 1 - core, 1, keepdims=False).astype(BF16)
    kept = lax.dynamic_index_in_dim(v, core, 1, keepdims=False)
    return kept + swap(other, CORE).astype(F32)


def after(gate, *values):
    return lax.optimization_barrier((gate, *values))


def per_device(
    tokens,
    cotangent,
    seq_lengths,
    seq_device,
    norm_gain,
    in_weight,
    conv_weight,
    conv_bias,
    step_bias,
    decay_log,
    skip_gain,
    gate_gain,
    out_weight,
):
    shards = lax.axis_size("shard")
    shard = lax.axis_index("shard")
    device = lax.axis_index("rep") * shards + shard
    half_count = seq_lengths.shape[0] // 2
    owned = seq_device[:half_count] == device
    first_len = jnp.sum(jnp.where(owned, seq_lengths[:half_count], 0))
    second_len = jnp.sum(jnp.where(owned, seq_lengths[half_count:], 0))
    ends = jnp.stack(
        [first_len, first_len + second_len, lax.axis_index("rep") % 2, shard]
    ).astype(jnp.int32)
    count, width = tokens.shape
    inner = gate_gain.shape[0] * shards
    channels = conv_weight.shape[1] * shards
    head_count = step_bias.shape[0] * shards
    size = inner // head_count
    taps = conv_weight.shape[0]

    small = (norm_gain, conv_weight.reshape(-1), conv_bias, step_bias, decay_log, skip_gain, gate_gain)
    sizes = [v.shape[0] for v in small]
    own = jnp.concatenate(small)
    own = jnp.pad(own, (0, -own.shape[0] % 1024)).reshape(-1, LANES)
    in_half = half_rows(in_weight)
    conv_far = swap(in_half[:, inner:], SHARD)
    other = swap(own, SHARD)
    conv_near = swap(conv_far, CORE)
    conv_near, gate_send, out_send = after(conv_near, in_half[:, :inner], half_rows(out_weight))
    gate_far = swap(gate_send, SHARD)
    out_far = swap(out_send, SHARD)

    packed = jnp.where(shard == 0, jnp.stack([own, other]), jnp.stack([other, own])).reshape(2, -1)
    parts = []
    at = 0
    for n in sizes:
        parts.append(packed[:, at : at + n])
        at += n
    full_norm, _, full_shift, full_step, full_decay, full_skip, full_gate = [
        p.reshape(-1).astype(F32) for p in parts
    ]
    conv_w = parts[1].reshape(shards, taps, -1).transpose(1, 0, 2).reshape(taps, -1).astype(F32)
    conv_b = full_shift[None, :]
    norm_row = full_norm[None, :]
    gate_row = full_gate[None, :]
    lane_head = lax.broadcasted_iota(jnp.int32, (inner, LANES), 0) // size
    heads = (lane_head == lax.broadcasted_iota(jnp.int32, (inner, LANES), 1)).astype(BF16)
    skip = jnp.repeat(full_skip, size)[None, :]
    step_row = pad_lanes(full_step[None, :])
    neg_rate = pad_lanes(-jnp.exp(full_decay)[None, :])

    normed, u, conv_in, raw, y, states, w_conv = run_scan(
        ends, tokens, in_weight, conv_far, conv_near, norm_row, conv_w, conv_b, step_row, neg_rate, inner
    )
    normed, gate_far, out_far = after(normed, gate_far, out_far)
    gate_near = swap(gate_far, CORE)
    out_near = swap(out_far, CORE)
    w_gate, w_out, gated, masked, dy, dgate, s1, gain8, skip8 = run_gate(
        ends, cotangent, normed, u, y, in_weight, gate_far, gate_near, out_weight, out_far, out_near, skip, gate_row, heads
    )
    bits = exchanges()
    far, last_bit = bits[1:-1], bits[-1]
    g_out = dot(gated, masked, ((0,), (0,)))
    h_out = core_sum(g_out)
    g_out, normed = after(g_out, normed)
    g_gate = dot(normed, dgate, ((0,), (0,)))
    quarter = h_out.shape[1] // 2
    kept_o, sent_o = cut(jnp.concatenate([h_out[:, :quarter], h_out[:, quarter:]], axis=2), SHARD)
    g_gate, sent_o = after(g_gate, sent_o)
    got_o = swap(sent_o, SHARD)
    h_gate = core_sum(g_gate)
    half_pairs = inner // LANES // 2
    shared = (s1, states, conv_w, step_row, neg_rate, skip, heads)

    kept, sent = cut(h_gate, SHARD)
    dy, sent = after(dy, sent)
    got = swap(sent, SHARD)
    carry = run_backward(0, half_pairs, None, None, ends, u, conv_in, raw, dy, *shared)
    first_out, kept, got, kept_o, got_o = after(carry[0], kept, got, kept_o, got_o)
    kept, sent = cut(jnp.concatenate([add(kept_o, got_o), add(kept, got)], axis=1), far[0])
    dy, sent = after(dy, sent)
    got = swap(sent, far[0])
    rest_a, part, cw_a, cb_a, _, dl_a, _, _ = run_backward(
        0, half_pairs, None, (first_out, *carry[1:]), ends, u, conv_in, raw, dy, *shared
    )
    rest_a, kept, got = after(rest_a, kept, got)
    g_a = dot(normed, rest_a, ((0,), (0,)))
    held = add(kept, got)
    kept, sent = cut(held, far[1])
    kept_a, sent_a = cut(core_sum(g_a), SHARD)
    part, sent, sent_a = after(part, sent, sent_a)
    got = swap(sent, far[1])
    got_a = swap(sent_a, SHARD)
    carry = run_backward(half_pairs, half_pairs, part, None, ends, u, conv_in, raw, dy, *shared)
    first_out, kept, got, kept_a, got_a = after(carry[0], kept, got, kept_a, got_a)
    held = add(kept, got)
    for bit in far[2:]:
        kept, sent = cut(held, bit)
        held = add(kept, swap(sent, bit))
    low = held.astype(BF16)
    kept_a, sent_a = cut(add(kept_a, got_a), far[0])
    part, low, sent_a = after(part, low, sent_a)
    got = swap(low, last_bit)
    got_a = swap(sent_a, far[0])
    rest_b, _, cw_b, cb_b, sb_b, dl_b, _, _ = run_backward(
        half_pairs, half_pairs, part, (first_out, *carry[1:]), ends, u, conv_in, raw, dy, *shared
    )
    rest_b, low, got, kept_a, got_a = after(rest_b, low, got, kept_a, got_a)
    g_b = dot(normed, rest_b, ((0,), (0,)))

    g_conv = jnp.sum(jnp.concatenate([cw_a, cw_b], 1).reshape(taps, 8, channels), axis=1)
    g_shift = jnp.sum(jnp.concatenate([cb_a, cb_b], 1), axis=0)
    g_step = jnp.sum(sb_b, axis=0)[:head_count]
    g_decay = jnp.sum(dl_a + dl_b, axis=0)[:head_count]
    g_skip = jnp.sum(skip8.reshape(8, head_count, size), axis=(0, 2))
    g_gain = jnp.sum(gain8, axis=0)
    pieces = (
        g_conv.reshape(taps, shards, -1).transpose(1, 0, 2).reshape(shards, -1),
        g_shift.reshape(shards, -1),
        g_step.reshape(shards, -1),
        g_decay.reshape(shards, -1),
        g_skip.reshape(shards, -1),
        g_gain.reshape(shards, -1),
    )
    flat = jnp.concatenate(pieces, axis=1)
    flat = jnp.pad(flat, ((0, 0), (0, -flat.shape[1] % 1024))).reshape(shards, -1, LANES)
    rest_b, flat = after(rest_b, flat)
    flat = flat + swap(flat, CORE)
    low = add(low.astype(F32), got).astype(BF16)
    held_a = add(kept_a, got_a)
    kept_b, sent_b = cut(core_sum(g_b), SHARD)
    backs = far[::-1] + [CORE]
    mine, sent_s = take(flat, at_bit(SHARD)), take(flat, 1 - at_bit(SHARD))
    gated, low, sent_b, sent_s = after(gated, low, sent_b, sent_s)
    got_s = swap(sent_s, SHARD)
    got = swap(low, backs[0])
    got_b = swap(sent_b, SHARD)
    block_out = run_out(ends, tokens, gated, w_out)
    block_out, low, got, kept_b, got_b, got_s = after(block_out, low, got, kept_b, got_b, got_s)
    mine = mine + got_s
    low = join(low, got, backs[0])
    kept_b, sent_b = cut(add(kept_b, got_b), far[0])
    dgate, low, sent_b, mine = after(dgate, low, sent_b, mine)
    got_s = swap(mine, far[0])
    got = swap(low, backs[1])
    got_b = swap(sent_b, far[0])
    grad_part = run_part(dgate, rest_a, w_gate, w_conv)
    grad_part, low, got, kept_b, got_b, got_s = after(grad_part, low, got, kept_b, got_b, got_s)
    mine = mine + got_s
    low = join(low, got, backs[1])
    held_b = jnp.concatenate([held_a, add(kept_b, got_b)], axis=1)
    kept_b, sent_b = cut(held_b, far[1])
    grad_part, low, sent_b, mine = after(grad_part, low, sent_b, mine)
    got = swap(low, backs[2])
    mine = mine + swap(mine, far[1])
    held_b = add(kept_b, swap(sent_b, far[1]))
    for bit in far[2:]:
        mine = mine + swap(mine, bit)
        kept_b, sent_b = cut(held_b, bit)
        held_b = add(kept_b, swap(sent_b, bit))
    low_b = held_b.astype(BF16)
    grad_part, low_b, mine = after(grad_part, low_b, mine)
    got_s = swap(mine, last_bit)
    got_b = swap(low_b, last_bit)
    grad_tokens = run_norm(tokens, cotangent, grad_part, rest_b, w_conv, norm_row)
    grad_tokens, low, got, low_b, got_b, got_s = after(grad_tokens, low, got, low_b, got_b, got_s)
    mine = mine + got_s
    low = join(low, got, backs[2])
    for bit in backs[3:]:
        low = join(low, swap(low, bit), bit)
    low_b = (low_b.astype(F32) + got_b.astype(F32)).astype(BF16)
    for bit in backs:
        low_b = join(low_b, swap(low_b, bit), bit)
    near = out_weight.shape[1]
    by_core = low.reshape(2, low.shape[0] // 2, low.shape[1])
    t_out = jnp.concatenate(
        [by_core[0, :, :near], by_core[0, :, near : 2 * near], by_core[1, :, :near], by_core[1, :, near : 2 * near]], axis=0
    )
    gate_sum = low[:, 2 * near :]
    rest_sum = low_b[:, : channels + head_count]
    t_in = jnp.concatenate([gate_sum, rest_sum], axis=1).astype(F32)
    t_norm = jnp.sum(gate_sum.astype(F32) * in_weight[:, :inner].astype(F32), axis=1)
    t_norm = t_norm + jnp.sum(rest_sum.astype(F32) * in_weight[:, inner:].astype(F32), axis=1)
    t_norm = t_norm / norm_gain.astype(F32)
    mine = mine.reshape(-1)
    outs = []
    at = 0
    for n in sizes[1:]:
        outs.append(mine[at : at + n])
        at += n
    return (
        block_out,
        grad_tokens,
        t_norm,
        t_in,
        outs[0].reshape(taps, -1),
        outs[1],
        outs[2],
        outs[3],
        outs[4],
        outs[5],
        t_out.astype(F32),
    )


def solution(mesh):
    in_specs = (
        P(("rep", "shard"), None),
        P(("rep", "shard"), None),
        P(),
        P(),
        P("shard"),
        P("shard", None),
        P(None, "shard"),
        P("shard"),
        P("shard"),
        P("shard"),
        P("shard"),
        P("shard"),
        P("shard", None),
    )
    out_specs = (
        P(("rep", "shard"), None),
        P(("rep", "shard"), None),
        P("shard"),
        P("shard", None),
        P(None, "shard"),
        P("shard"),
        P("shard"),
        P("shard"),
        P("shard"),
        P("shard"),
        P("shard", None),
    )
    return jax.shard_map(
        per_device, mesh=mesh, in_specs=in_specs, out_specs=out_specs, check_vma=False
    )
```
